32 devices in a mesh: fsdp: 4 (over z), ctx: 4 (over y, core), tp: 2 (over x).
Axes of the slice: x: 2, y: 2, z: 4, core: 2. Of those that a mesh axis runs over, the one named last changes fastest.
Arguments:
- tokens: bfloat16 [8, 1024, 1024], P('fsdp', 'ctx', 'tp'), may hold values from -6 to 6
- prefix: int32 [8], P('fsdp'), may hold values from 102 to 512
- routes: int32 [4, 8, 256, 8], P('ctx', 'fsdp'), may hold values from 0 to 15, all different within a row; in each aligned block of 512 rows (0 to 511, 512 to 1023, ..., all dimensions but the last counted through in order) at most 384 rows name the same one
- w_query: bfloat16 [1024, 1024], P(('fsdp', 'ctx'), 'tp'), may hold values from -0.5 to 0.5
- w_key: bfloat16 [1024, 512], P(('fsdp', 'ctx'), 'tp'), may hold values from -0.5 to 0.5
- w_value: bfloat16 [1024, 512], P(('fsdp', 'ctx'), 'tp'), may hold values from -0.1875 to 0.1875
- w_out: bfloat16 [1024, 1024], P('tp', ('fsdp', 'ctx')), may hold values from -6 to 6
- w_router: bfloat16 [1024, 16], P(('fsdp', 'ctx')), may hold values from -0.09375 to 0.09375
- gain_attn: bfloat16 [1024], P(('fsdp', 'ctx')), may hold values from 0.5 to 1.5
- gain_ffn: bfloat16 [1024], P(('fsdp', 'ctx')), may hold values from 0.5 to 1.5
- w_gate: bfloat16 [16, 1024, 512], P(None, ('fsdp', 'ctx'), 'tp'), may hold values from -0.1875 to 0.1875
- w_up: bfloat16 [16, 1024, 512], P(None, ('fsdp', 'ctx'), 'tp'), may hold values from -0.1875 to 0.1875
- w_down: bfloat16 [16, 512, 1024], P(None, 'tp', ('fsdp', 'ctx')), may hold values from -6 to 6
- cotangent: bfloat16 [8, 1024, 1024], P('fsdp', 'ctx', 'tp'), may hold values from -6 to 6
Outputs:
- output: bfloat16 [8, 1024, 1024], P('fsdp', 'ctx', 'tp')
- grad_tokens: float32 [8, 1024, 1024], P('fsdp', 'ctx', 'tp')
- grad_query: float32 [1024, 1024], P(('fsdp', 'ctx'), 'tp')
- grad_key: float32 [1024, 512], P(('fsdp', 'ctx'), 'tp')
- grad_value: float32 [1024, 512], P(('fsdp', 'ctx'), 'tp')
- grad_out: float32 [1024, 1024], P('tp', ('fsdp', 'ctx'))
- grad_router: float32 [1024, 16], P(('fsdp', 'ctx'))
- grad_gain_attn: float32 [1024], P(('fsdp', 'ctx'))
- grad_gain_ffn: float32 [1024], P(('fsdp', 'ctx'))
- grad_gate: float32 [16, 1024, 512], P(None, ('fsdp', 'ctx'), 'tp')
- grad_up: float32 [16, 1024, 512], P(None, ('fsdp', 'ctx'), 'tp')
- grad_down: float32 [16, 512, 1024], P(None, 'tp', ('fsdp', 'ctx'))
The draws below stay inside these ranges and needn't reach their ends.
Inputs may be any that keep to these rules, and one draw needn't show every extreme that they name: `routes`: each row names 8 different experts. In each aligned block of 512 rows in the array's order (the rows of one device), no expert is named by more than 384 rows, a bound that some block reaches.
All inputs are finite; a program needn't handle non-finite values.
Results may differ from the reference program's by a relative error of at most 0.02.
Values may be sent and summed in bfloat16 or wider, within the bound.
No kernel may reach another device: no remote copies, remote signals or barrier semaphores. Data moves between devices by JAX's collectives and lax.ppermute only.
A program may use at most 512 MiB of HBM per device.

```python
import math
import jax
import jax.numpy as jnp
import numpy as np
from jax import lax

D = 1024
H = 16
KVH = 8
HD = 64
FF = 512
EXPERTS = 16
TOP = 8
SEQ_LEN = 1024
SEQS = 2
BATCH = 8
SPAN = 256
TOK_DEV = 512
CAP = 384
N_FSDP = 4
N_CTX = 4


def touch_ends(values, own_key, smallest, top_value):
    dims = values.shape
    place = [jax.random.randint(jax.random.fold_in(own_key, axis), (), 0, dims[axis]) for axis in range(len(dims))]
    values = values.at[tuple(place)].set(smallest)
    longest = dims.index(max(dims))
    place[longest] = (place[longest] + 1) % dims[longest]
    return values.at[tuple(place)].set(top_value)


def spiked(values, own_key, source, target, parts, factor):
    def block_of(dim):
        return (jnp.arange(values.shape[dim]) // (values.shape[dim] // parts)).reshape((-1,) + (1,) * (values.ndim - 1 - dim))

    near = jax.random.permutation(own_key, parts)[block_of(target)]
    far = (block_of(target) + parts // 2) % parts
    return jnp.where((block_of(source) == near) | (block_of(source) == far), factor * values, values)


def shard_levels(key, dims, cuts, low, top_value):
    level, own = 1.0, jax.random.fold_in(key, 6)
    for position, parts in cuts:
        steps = jnp.exp(jax.random.uniform(jax.random.fold_in(own, position), (parts,), jnp.float32, low / len(cuts), top_value / len(cuts)))
        level = level * jnp.repeat(steps, dims[position] // parts).reshape([-1 if axis == position else 1 for axis in range(len(dims))])
    return level


def shared_out(stream_key, own, number, rows, amount, top, reach, skew):
    sequence = jax.random.permutation(stream_key, amount)
    crowded, ordinary = portions_of(amount, rows * top, reach, skew, True), portions_of(amount, rows * top, reach, skew, False)
    places = jnp.arange(amount)

    def named(sizes, rotation):
        used = int((sizes > 0).sum())
        fixed = max(1, used // 4)
        moved = fixed + (places - fixed + rotation * (used - fixed)) % max(1, amount - fixed)
        return jnp.zeros((amount,), jnp.int32).at[sequence[jnp.where(places < fixed, places, moved)]].set(jnp.asarray(sizes, jnp.int32))

    sizes = jnp.where(number % 4 == 0, named(crowded, number // 4), named(ordinary, number - number // 4 - 1))
    mixed = jax.random.permutation(jax.random.fold_in(own, 3), amount)
    donor, sink = mixed[0:amount // 2 * 2:2], mixed[1:amount // 2 * 2:2]
    margin = jnp.minimum(sizes[donor] - 1, reach - sizes[sink]) // 2
    margin = jnp.where((donor == sequence[0]) | (sink == sequence[0]) | (sizes[sink] == 0), 0, jnp.maximum(margin, 0))
    moved = jax.random.randint(jax.random.fold_in(own, 4), (amount // 2,), 0, 1 << 20) % (margin + 1)
    sizes = sizes.at[donor].add(-moved).at[sink].add(moved)
    items = jnp.searchsorted(jnp.cumsum(sizes), jnp.arange(rows * top), side="right").astype(jnp.int32)
    table = items.reshape(top, rows).T
    table = table[jax.random.permutation(jax.random.fold_in(own, 1), rows)]
    rotation = jax.random.randint(jax.random.fold_in(own, 2), (rows, 1), 0, top)
    return jnp.take_along_axis(table, (jnp.arange(top)[None, :] + rotation) % top, axis=1)


def portions_of(amount, total, limit, skew, full):
    portions = [(1 << 20) // math.isqrt(grade ** skew) + 1 for grade in range(1, amount + 1)]
    largest = limit if full else min(limit, max(-(-total // amount), total * portions[0] // sum(portions)))
    least = 1 if total - largest >= amount - 1 else 0
    given, rest = [largest] + [least] * (amount - 1), total - largest - least * (amount - 1)
    while rest > 0:
        movable = [i for i in range(1, amount) if given[i] < largest] or [i for i in range(1, amount) if given[i] < limit]
        whole, remaining = sum([portions[i] for i in movable]), rest
        for i in movable:
            extra = min(limit - given[i], max(1, remaining * portions[i] // whole), rest)
            given[i] = given[i] + extra
            rest = rest - extra
    return np.array(given)


def centred(rng, dims, spread, limit, shards=(), kind=jnp.bfloat16):
    entries = spread * jax.random.normal(rng, dims, jnp.float32)
    if shards:
        entries = entries * shard_levels(rng, dims, shards, -0.22, 0.18)
    return jnp.clip(entries, -limit, limit).astype(kind)


def noise_with(own_key, extent, width, most, shards, heavy, kind=jnp.bfloat16):
    values = width * jax.random.normal(own_key, extent, jnp.float32)
    if shards:
        values = values * shard_levels(own_key, extent, shards, -0.22, 0.18)
    return jnp.clip(spiked(values, jax.random.fold_in(own_key, 3), *heavy), -most, most).astype(kind)


def setup_inputs(seed: int = 0) -> dict:
    key_of = jax.random.split(jax.random.key(seed), 15)
    tokens = centred(key_of[0], (BATCH, SEQ_LEN, D), 1.0, 6.0, ((0, 4), (1, 4), (2, 2)))
    prefix = touch_ends(jax.random.randint(key_of[1], (BATCH,), SEQ_LEN // 10, SEQ_LEN // 2 + 1), jax.random.fold_in(key_of[1], 1), SEQ_LEN // 10, (SEQ_LEN // 2 + 1) - 1).astype(jnp.int32)
    routes_keys = jax.random.split(jax.random.fold_in(key_of[2], 1), N_CTX * BATCH * SPAN // TOK_DEV)
    routes_turns = jax.random.permutation(jax.random.fold_in(key_of[2], 3), N_CTX * BATCH * SPAN // TOK_DEV)
    routes = jax.vmap(lambda own, number: shared_out(jax.random.fold_in(key_of[2], 2), own, number, TOK_DEV, EXPERTS, TOP, CAP, 1))(routes_keys, routes_turns).reshape((N_CTX, BATCH, SPAN, TOP))
    w_query = centred(key_of[3], (D, H * HD), (D // 8) ** -0.5, 0.5, ((0, 16), (1, 2)))
    w_key = centred(key_of[4], (D, KVH * HD), (D // 8) ** -0.5, 0.5, ((0, 16), (1, 2)))
    w_value = centred(key_of[5], (D, KVH * HD), D ** -0.5, 0.1875, ((0, 16), (1, 2)))
    w_out = centred(key_of[6], (H * HD, D), 1.6, 6.0, ((0, 2), (1, 16)))
    w_router = centred(key_of[7], (D, EXPERTS), (4 * D) ** -0.5, 0.09375, ((0, 16),))
    gain_attn = jnp.clip(1.0 + 0.1 * jax.random.normal(key_of[8], (D,), jnp.float32), 0.5, 1.5).astype(jnp.bfloat16)
    gain_ffn = jnp.clip(1.0 + 0.1 * jax.random.normal(key_of[9], (D,), jnp.float32), 0.5, 1.5).astype(jnp.bfloat16)
    w_gate = centred(key_of[10], (EXPERTS, D, FF), D ** -0.5, 0.1875, ((1, 16), (2, 2)))
    w_up = centred(key_of[11], (EXPERTS, D, FF), D ** -0.5, 0.1875, ((1, 16), (2, 2)))
    w_down = centred(key_of[12], (EXPERTS, FF, D), 1.0, 6.0, ((1, 2), (2, 16)))
    cotangent = noise_with(key_of[13], (BATCH, SEQ_LEN, D), 1.0, 6.0, ((0, 4), (1, 4), (2, 2)), (0, 2, 4, 2.0))
    return dict(tokens=tokens, prefix=prefix, routes=routes, w_query=w_query, w_key=w_key, w_value=w_value, w_out=w_out, w_router=w_router, gain_attn=gain_attn, gain_ffn=gain_ffn, w_gate=w_gate, w_up=w_up, w_down=w_down, cotangent=cotangent)


EPSILON = 1e-06
ATTN_SCALE = 0.015625
RESIDUAL_SCALE = 0.22
MASKED_SCORE = -1e+30
PRECISE = lax.Precision.HIGHEST

@jax.custom_vjp
def low(v):
    return lax.optimization_barrier(v.astype(jnp.bfloat16)).astype(jnp.float32)

@jax.custom_vjp
def low_back(v):
    return v

def low_keep(v):
    return (low(v), None)

def low_pass(kept, grad):
    return (grad,)

def back_keep(v):
    return (v, None)

def back_low(kept, grad):
    return (low(grad),)
low.defvjp(low_keep, low_pass)
low_back.defvjp(back_keep, back_low)

def rms_scale(hidden, gain):
    return hidden * lax.rsqrt(lax.optimization_barrier(jnp.mean(hidden * hidden, axis=-1, keepdims=True)) + EPSILON) * gain

def rotate(vectors, positions):
    half_width = vectors.shape[-1] // 2
    freqs = 10000.0 ** (-jnp.arange(half_width, dtype=jnp.float32) / half_width)
    angles = positions.astype(jnp.float32)[:, None] * freqs[None, :]
    cosine = jnp.cos(angles)[:, None, :]
    sine = jnp.sin(angles)[:, None, :]
    first = vectors[..., :half_width]
    second = vectors[..., half_width:]
    return jnp.concatenate([first * cosine - second * sine, second * cosine + first * sine], axis=-1)

def softmax_rows(values):
    row_max = lax.optimization_barrier(jnp.max(values, axis=-1, keepdims=True))
    expo = jnp.exp(values - row_max)
    return expo / lax.optimization_barrier(jnp.sum(expo, axis=-1, keepdims=True))

def build_slots(route_rows, experts, capacity):
    route_flat = route_rows.reshape(-1)
    one_hot = (route_flat[:, None] == jnp.arange(experts, dtype=jnp.int32)[None, :]).astype(jnp.int32)
    before = jnp.cumsum(one_hot, axis=0, dtype=jnp.int32) - one_hot
    slot_place = (lax.optimization_barrier(jnp.sum(before * one_hot, axis=1)).astype(jnp.int32) + route_flat * capacity).astype(jnp.int32)
    route_order = jnp.arange(route_flat.shape[0], dtype=jnp.int32)
    slot_route = jnp.zeros((experts * capacity,), jnp.int32).at[slot_place].set(route_order)
    filled = jnp.zeros((experts * capacity,), jnp.float32).at[slot_place].set(1.0)
    return (slot_place, slot_route, filled)

def attend(record):
    queries, key_heads, value_heads, prefix_len = record
    grouped = queries.reshape(SEQ_LEN, KVH, H // KVH, HD)
    scores = jnp.einsum('qgrd,kgd->grqk', grouped, key_heads, precision=PRECISE) * ATTN_SCALE
    scores = low_back(scores)
    key_pos = jnp.arange(SEQ_LEN, dtype=jnp.int32)
    visible = (key_pos[None, :] <= key_pos[:, None]) | (key_pos[None, :] < prefix_len)
    scores = jnp.where(visible, scores, MASKED_SCORE)
    probs = low(softmax_rows(scores))
    attended = jnp.einsum('grqk,kgd->qgrd', probs, value_heads, precision=PRECISE)
    return low(low_back(attended.reshape(SEQ_LEN, H * HD)))

def experts_block(record, w_router, w_gate, w_up, w_down):
    normed_two, route_rows = record
    logits = low_back(jnp.dot(normed_two, w_router, precision=PRECISE))
    one_hot = (route_rows[:, :, None] == jnp.arange(EXPERTS, dtype=jnp.int32)[None, None, :]).astype(jnp.float32)
    chosen = lax.optimization_barrier(jnp.sum(one_hot * logits[:, None, :], axis=-1))
    gate_weights = softmax_rows(chosen)
    slot_place, slot_route, filled = build_slots(route_rows, EXPERTS, CAP)
    token_of = slot_route // TOP
    slot_gate = gate_weights.reshape(-1)[slot_route] * filled
    picked = normed_two[token_of].reshape(EXPERTS, CAP, D)
    gate_pre = low_back(jnp.einsum('ecd,edf->ecf', picked, w_gate, precision=PRECISE))
    up_pre = low_back(jnp.einsum('ecd,edf->ecf', picked, w_up, precision=PRECISE))
    hidden = low(gate_pre * jax.nn.sigmoid(gate_pre) * up_pre)
    result = low_back(jnp.einsum('ecf,efd->ecd', hidden, w_down, precision=PRECISE))
    weighted = (slot_gate.reshape(EXPERTS, CAP, 1) * result).reshape(EXPERTS * CAP, D)
    return jax.ops.segment_sum(weighted, token_of, TOK_DEV)

def layer_forward(tokens, w_query, w_key, w_value, w_out, w_router, gain_attn, gain_ffn, w_gate, w_up, w_down, prefix, routes):
    normed = low(rms_scale(tokens, gain_attn)).reshape(BATCH * SEQ_LEN, D)
    positions = jnp.tile(jnp.arange(SEQ_LEN, dtype=jnp.int32), BATCH)
    query_raw = low_back(jnp.dot(normed, w_query, precision=PRECISE))
    key_raw = low_back(jnp.dot(normed, w_key, precision=PRECISE))
    values = low(low_back(jnp.dot(normed, w_value, precision=PRECISE)))
    queries = low(rotate(query_raw.reshape(-1, H, HD), positions))
    key_heads = low(rotate(key_raw.reshape(-1, KVH, HD), positions))
    attended = lax.map(jax.checkpoint(attend), (queries.reshape(BATCH, SEQ_LEN, H, HD), key_heads.reshape(BATCH, SEQ_LEN, KVH, HD), values.reshape(BATCH, SEQ_LEN, KVH, HD), prefix))
    branch = low_back(jnp.dot(attended.reshape(-1, H * HD), w_out, precision=PRECISE))
    middle = tokens + RESIDUAL_SCALE * branch.reshape(BATCH, SEQ_LEN, D)
    normed_two = low(rms_scale(middle, gain_ffn))
    blocks = normed_two.reshape(N_FSDP, SEQS, N_CTX, SPAN, D).transpose(2, 0, 1, 3, 4).reshape(N_CTX * N_FSDP, TOK_DEV, D)
    route_blocks = routes.reshape(N_CTX * N_FSDP, TOK_DEV, TOP)

    def one_block(record):
        return experts_block(record, w_router, w_gate, w_up, w_down)
    moe = lax.map(jax.checkpoint(one_block), (blocks, route_blocks))
    moe = moe.reshape(N_CTX, N_FSDP, SEQS, SPAN, D).transpose(1, 2, 0, 3, 4).reshape(BATCH, SEQ_LEN, D)
    return middle + RESIDUAL_SCALE * moe

def reference(tokens, prefix, routes, w_query, w_key, w_value, w_out, w_router, gain_attn, gain_ffn, w_gate, w_up, w_down, cotangent):
    params = tuple((array.astype(jnp.float32) for array in (tokens, w_query, w_key, w_value, w_out, w_router, gain_attn, gain_ffn, w_gate, w_up, w_down)))

    def forward(*inputs):
        return layer_forward(*inputs, prefix, routes)
    output, pullback = jax.vjp(forward, *params)
    grads = pullback(cotangent.astype(jnp.float32))
    return (output.astype(jnp.bfloat16), grads[0], grads[1], grads[2], grads[3], grads[4], grads[5], grads[6], grads[7], grads[8], grads[9], grads[10])
```

```python
import functools

import jax
import jax.numpy as jnp
from jax import lax
from jax.experimental import pallas as pl
from jax.experimental.pallas import tpu as pltpu
from jax.sharding import PartitionSpec as P

HD = 64
TOP = 8
LANES = 128

EPSILON = 1e-06
ATTN_SCALE = 0.015625
RESIDUAL_SCALE = 0.22
MASKED_SCORE = -1e30
GROUPS = 4
RING = ("fsdp", "ctx")
BF = jnp.bfloat16
F32 = jnp.float32
VMEM_LIMIT = 60 * 1024 * 1024


def nt(a, b):
    return lax.dot_general(a, b, (((1,), (1,)), ((), ())), preferred_element_type=F32)


def nn(a, b):
    return lax.dot_general(a, b, (((1,), (0,)), ((), ())), preferred_element_type=F32)


def tn(a, b):
    return lax.dot_general(a, b, (((0,), (0,)), ((), ())), preferred_element_type=F32)


def params(*semantics):
    return pltpu.CompilerParams(
        dimension_semantics=semantics, vmem_limit_bytes=VMEM_LIMIT
    )


def whole(shape):
    zeros = (0,) * len(shape)
    return pl.BlockSpec(shape, lambda *_: zeros, pipeline_mode=pl.Buffered(1))


def swap_halves(slab):
    lane = lax.broadcasted_iota(jnp.int32, slab.shape, 1) % HD
    return jnp.where(
        lane < HD // 2, pltpu.roll(slab, LANES - HD // 2, 1), pltpu.roll(slab, HD // 2, 1)
    )


def project_kernel(pairs, q_width, x_ref, gain_ref, w_ref, cos_ref, sin_ref, n_ref, q_ref, kv_ref):
    x = x_ref[...].astype(F32)
    scale = lax.rsqrt(jnp.mean(x * x, axis=1, keepdims=True) + EPSILON)
    normed = (x * scale * gain_ref[...]).astype(BF)
    n_ref[...] = normed
    cosine, sine = cos_ref[...], sin_ref[...]
    raw = nn(normed, w_ref[...])
    for slab in range(q_width // LANES):
        cols = slice(slab * LANES, (slab + 1) * LANES)
        part = raw[:, cols]
        turned = (part * cosine + swap_halves(part) * sine).astype(BF)
        q_ref[:, cols] = (turned.astype(F32) * ATTN_SCALE).astype(BF)
    for pair in range(pairs):
        lo = pair * 2 * LANES
        part = raw[:, q_width + lo : q_width + lo + LANES]
        kv_ref[:, lo : lo + LANES] = (part * cosine + swap_halves(part) * sine).astype(BF)
        kv_ref[:, lo + LANES : lo + 2 * LANES] = raw[
            :, q_width + lo + LANES : q_width + lo + 2 * LANES
        ].astype(BF)


def attend_kernel(blocks, span, prefix_ref, base_ref, q_ref, *refs):
    kv_refs = refs[:blocks]
    out_ref, p_ref = refs[blocks:]
    limit_len = prefix_ref[pl.program_id(0)]
    local = base_ref[0] + lax.broadcasted_iota(jnp.int32, (span, 1), 0)
    limit = jnp.maximum(local + 1, limit_len)
    key_pos = jnp.concatenate(
        [
            base_ref[j] + lax.broadcasted_iota(jnp.int32, (1, span), 1)
            for j in range(blocks)
        ],
        axis=1,
    )
    visible = key_pos < limit
    visible = jnp.concatenate([visible, visible], axis=0)
    for g in range(2):
        keys = jnp.concatenate([r[:, g * HD : (g + 1) * HD] for r in kv_refs], axis=0)
        vals = jnp.concatenate(
            [r[:, LANES + g * HD : LANES + (g + 1) * HD] for r in kv_refs], axis=0
        )
        first, second = 2 * g * HD, (2 * g + 1) * HD
        queries = jnp.concatenate(
            [q_ref[:, first : first + HD], q_ref[:, second : second + HD]], axis=0
        )
        scores = jnp.where(visible, nt(queries, keys), MASKED_SCORE)
        expo = jnp.exp(scores - jnp.max(scores, axis=1, keepdims=True))
        probs = (expo * (1.0 / jnp.sum(expo, axis=1, keepdims=True))).astype(BF)
        p_ref[0, g] = probs
        att = nn(probs, vals).astype(BF)
        out_ref[:, first : first + HD] = att[:span]
        out_ref[:, second : second + HD] = att[span:]


def attend_back_kernel(blocks, span, p_ref, q_ref, g_ref, *refs):
    kv_refs = refs[:blocks]
    dq_ref, own_ref, other_ref = refs[blocks:]
    parts = []
    for g in range(2):
        keys = jnp.concatenate([r[:, g * HD : (g + 1) * HD] for r in kv_refs], axis=0)
        vals = jnp.concatenate(
            [r[:, LANES + g * HD : LANES + (g + 1) * HD] for r in kv_refs], axis=0
        )
        first, second = 2 * g * HD, (2 * g + 1) * HD
        queries = jnp.concatenate(
            [q_ref[:, first : first + HD], q_ref[:, second : second + HD]], axis=0
        )
        grads = jnp.concatenate(
            [g_ref[:, first : first + HD], g_ref[:, second : second + HD]], axis=0
        )
        probs = p_ref[0, g]
        wide = probs.astype(F32)
        grad_probs = nt(grads, vals)
        inner = jnp.sum(wide * grad_probs, axis=1, keepdims=True)
        grad_scores = (wide * (grad_probs - inner)).astype(BF)
        dq = nn(grad_scores, keys) * ATTN_SCALE
        dq_ref[:, first : first + HD] = dq[:span]
        dq_ref[:, second : second + HD] = dq[span:]
        parts.append((nn(queries.T, grad_scores), nn(grads.T, probs)))
    stacked = jnp.concatenate([parts[0][0], parts[1][0], parts[0][1], parts[1][1]], axis=0)
    turned = stacked.T.astype(BF)
    half = blocks // 2
    for j in range(half):
        own_ref[j] = turned[j * span : (j + 1) * span]
        other_ref[j] = turned[(half + j) * span : (half + j + 1) * span]


def middle_kernel(
    a_ref, b_ref, wa_ref, wb_ref, x_ref, gain_ref, router_ref, routes_ref, m_ref, n_ref, nt_ref, g_ref
):
    branch = nt(a_ref[...], wa_ref[...]) + nt(b_ref[...], wb_ref[...])
    middle = x_ref[...].astype(F32) + RESIDUAL_SCALE * branch
    m_ref[...] = middle
    scale = lax.rsqrt(jnp.mean(middle * middle, axis=1, keepdims=True) + EPSILON)
    wide = middle * scale * gain_ref[...]
    normed = wide.astype(BF)
    n_ref[...] = normed
    nt_ref[...] = normed.T
    logits = nn(normed, router_ref[...])
    lane = lax.broadcasted_iota(jnp.int32, logits.shape, 1)
    routes = routes_ref[...]
    routed = lane == routes[:, 0:1]
    for k in range(1, TOP):
        routed = routed | (lane == routes[:, k : k + 1])
    logits = jnp.where(routed, logits, MASKED_SCORE)
    expo = jnp.where(routed, jnp.exp(logits - jnp.max(logits, axis=1, keepdims=True)), 0.0)
    g_ref[...] = expo / jnp.sum(expo, axis=1, keepdims=True)


def moe_kernel(
    first_call,
    column_ref,
    w_ref,
    xa_ref,
    xb_ref,
    xta_ref,
    xtb_ref,
    ya_ref,
    yb_ref,
    yta_ref,
    ytb_ref,
    ga_ref,
    gb_ref,
    *refs,
):
    if first_call:
        accs = refs[:6]
        dw_ref = refs[6]
    else:
        inits, accs = refs[:6], refs[6:12]
        dw_ref = refs[12]

    @pl.when(pl.program_id(0) == 0)
    def _():
        for i in range(6):
            if first_call:
                accs[i][...] = jnp.zeros(accs[i].shape, accs[i].dtype)
            else:
                accs[i][...] = inits[i][...]

    expert = column_ref[0] + pl.program_id(0)
    rows, cols = w_ref.shape[0] * w_ref.shape[2], w_ref.shape[3]
    hid = cols // 3
    weights = w_ref[...].reshape(rows, cols)
    w_gu, w_d = weights[:, : 2 * hid], weights[:, 2 * hid :]
    kept = []
    for x_ref, y_ref, gate_ref, moe_ref, dx_ref, gg_ref in (
        (xa_ref, ya_ref, ga_ref, accs[0], accs[2], accs[4]),
        (xb_ref, yb_ref, gb_ref, accs[1], accs[3], accs[5]),
    ):
        pre = nn(x_ref[...], w_gu)
        back = nn(y_ref[...], w_d)
        gates = gate_ref[...]
        lane = lax.broadcasted_iota(jnp.int32, gates.shape, 1)
        here = lane == expert
        weight = RESIDUAL_SCALE * jnp.sum(jnp.where(here, gates, 0.0), axis=1, keepdims=True)
        gate_pre, up_pre = pre[:, :hid], pre[:, hid:]
        sig = jax.nn.sigmoid(gate_pre)
        act = gate_pre * sig
        hidden = act * up_pre
        pull = RESIDUAL_SCALE * jnp.sum(back * hidden, axis=1, keepdims=True)
        gg_ref[...] += jnp.where(here, pull, 0.0)
        scaled = weight * back
        d_up = scaled * act
        d_gate = scaled * up_pre * (sig + act * (1.0 - sig))
        d_gu = jnp.concatenate([d_gate.astype(BF), d_up.astype(BF)], axis=1)
        mixed = (weight * hidden).astype(BF)
        moe_ref[...] += nt(mixed, w_d)
        dx_ref[...] += nt(d_gu, w_gu)
        kept.append((d_gu, mixed))
    dw_gu = nn(xta_ref[...], kept[0][0]) + nn(xtb_ref[...], kept[1][0])
    dw_d = nn(yta_ref[...], kept[0][1]) + nn(ytb_ref[...], kept[1][1])
    shape = dw_ref.shape[:3]
    dw_ref[:, :, :, : 2 * hid] = dw_gu.astype(BF).reshape(shape + (2 * hid,))
    dw_ref[:, :, :, 2 * hid :] = dw_d.astype(BF).reshape(shape + (hid,))


def middle_back_kernel(
    tp_ref,
    sa_ref,
    sb_ref,
    gga_ref,
    ggb_ref,
    gates_ref,
    m_ref,
    y_ref,
    gain_ref,
    router_ref,
    wo_ref,
    gm_ref,
    branch_ref,
    att_ref,
    logit_ref,
    dgain_ref,
):
    @pl.when(pl.program_id(0) == 0)
    def _():
        dgain_ref[...] = jnp.zeros(dgain_ref.shape, F32)

    gates = gates_ref[...]
    pull = gga_ref[...] + ggb_ref[...]
    weighted = gates * pull
    grad_logits = (weighted - gates * jnp.sum(weighted, axis=1, keepdims=True)).astype(BF)
    logit_ref[...] = grad_logits
    grad = (
        sa_ref[...].astype(F32) + sb_ref[...].astype(F32) + nt(grad_logits, router_ref[...])
    )
    middle = m_ref[...]
    width = middle.shape[1]
    scale = lax.rsqrt(jnp.mean(middle * middle, axis=1, keepdims=True) + EPSILON)
    unit = middle * scale
    dgain_ref[...] += jnp.sum(grad * unit, axis=0, keepdims=True)
    scaled = grad * gain_ref[...]
    inner = jnp.sum(scaled * unit, axis=1, keepdims=True) * (1.0 / width)
    grad_middle = y_ref[...].astype(F32) + scale * (scaled - unit * inner)
    half = width // 2
    gm_ref[...] = jnp.where(tp_ref[0] == 0, grad_middle[:, :half], grad_middle[:, half:])
    branch = (RESIDUAL_SCALE * grad_middle).astype(BF)
    branch_ref[...] = branch
    att_ref[...] = nn(branch, wo_ref[...]).astype(BF)


def project_back_kernel(
    pairs,
    tp_ref,
    dq_ref,
    kva_ref,
    kvb_ref,
    kvc_ref,
    cos_ref,
    sin_ref,
    w_ref,
    x_ref,
    gain_ref,
    d_ref,
    own_ref,
    other_ref,
    dot_ref,
    dgain_ref,
):
    @pl.when(pl.program_id(0) == 0)
    def _():
        dgain_ref[...] = jnp.zeros(dgain_ref.shape, F32)

    cosine, sine = cos_ref[...], sin_ref[...]
    q_width = dq_ref.shape[1]
    for slab in range(q_width // LANES):
        cols = slice(slab * LANES, (slab + 1) * LANES)
        part = dq_ref[:, cols]
        d_ref[:, cols] = (part * cosine - swap_halves(part) * sine).astype(BF)
    kv = kva_ref[...].astype(F32) + kvb_ref[...].astype(F32) + kvc_ref[...].astype(F32)
    for pair in range(pairs):
        lo = pair * 2 * LANES
        part = kv[:, lo : lo + LANES]
        d_ref[:, q_width + lo : q_width + lo + LANES] = (
            part * cosine - swap_halves(part) * sine
        ).astype(BF)
        d_ref[:, q_width + lo + LANES : q_width + lo + 2 * LANES] = kv[
            :, lo + LANES : lo + 2 * LANES
        ].astype(BF)
    grad = nt(d_ref[...], w_ref[...])
    x = x_ref[...].astype(F32)
    width = x.shape[1]
    scale = lax.rsqrt(jnp.mean(x * x, axis=1, keepdims=True) + EPSILON)
    unit = x * scale
    dgain_ref[...] += jnp.sum(grad * unit, axis=0, keepdims=True)
    scaled = grad * gain_ref[...]
    inner = jnp.sum(scaled * unit, axis=1, keepdims=True) * (1.0 / width) * scale * scale
    dot_ref[...] = jnp.broadcast_to(inner, dot_ref.shape)
    scaled = scaled * scale
    half = width // 2
    is_first = tp_ref[0] == 0
    own_ref[...] = jnp.where(is_first, scaled[:, :half], scaled[:, half:])
    other_ref[...] = jnp.where(is_first, scaled[:, half:], scaled[:, :half]).astype(BF)


class Ring:
    def __init__(self, wide, ctx):
        self.wide, self.ctx, self.deep = wide, ctx, ctx // 2
        self.size = wide * self.deep
        deep = self.deep
        order = [
            (f, y)
            for y in range(deep)
            for f in (range(wide) if y % 2 == 0 else range(wide - 1, -1, -1))
        ]
        flat = [[f * ctx + y * 2 + c for f, y in order] for c in range(2)]
        n = self.size
        self.forward = [(row[i], row[(i + 1) % n]) for row in flat for i in range(n)]
        self.backward = [(b, a) for a, b in self.forward]
        f, c = lax.axis_index("fsdp"), lax.axis_index("ctx")
        y = c // 2
        self.place = y * wide + jnp.where(y % 2 == 0, f, wide - 1 - f)

    def chip(self, offset):
        place = (self.place + offset) % self.size
        y, q = place // self.wide, place % self.wide
        f = jnp.where(y % 2 == 0, q, self.wide - 1 - q)
        return f * self.deep + y

    def send(self, array, forward=True):
        return lax.ppermute(array, RING, self.forward if forward else self.backward)

    def gather(self, block):
        n, rows = self.size, block.shape[1]
        half = rows // 2
        full = jnp.zeros((n,) + block.shape, block.dtype)

        def put(full, part, offset, row):
            return lax.dynamic_update_slice(full, part[None], (self.chip(offset), 0, row, 0))

        full = put(full, block, 0, 0)
        ahead = back = block
        for step in range(1, n // 2):
            ahead, back = self.send(ahead), self.send(back, False)
            full = put(full, ahead, -step, 0)
            full = put(full, back, step, 0)
        ahead = self.send(ahead[:, :half])
        back = self.send(back[:, half:], False)
        full = put(full, ahead, -(n // 2), 0)
        return put(full, back, n // 2, half)

    def scatter(self, full):
        n, rows = self.size, full.shape[2]
        half = rows // 2

        def part(offset):
            return lax.dynamic_index_in_dim(full, self.chip(offset), 0, keepdims=False)

        far = n // 2
        opposite = part(far)
        ahead = self.send(opposite[:, :half])
        back = self.send(opposite[:, half:], False)
        for step in range(far - 1, 0, -1):
            near, behind = part(step), part(-step)
            if step == far - 1:
                ahead = jnp.concatenate([near[:, :half] + ahead, near[:, half:]], axis=1)
                back = jnp.concatenate([behind[:, :half], behind[:, half:] + back], axis=1)
            else:
                ahead, back = near + ahead, behind + back
            ahead, back = self.send(ahead), self.send(back, False)
        return part(0).astype(F32) + ahead.astype(F32) + back.astype(F32)


def per_device(
    tokens,
    prefix,
    routes,
    w_query,
    w_key,
    w_value,
    w_out,
    w_router,
    gain_attn,
    gain_ffn,
    w_gate,
    w_up,
    w_down,
    cotangent,
):
    wide, ctx = lax.axis_size("fsdp"), lax.axis_size("ctx")
    seqs, span, feature = tokens.shape
    rows = seqs * span
    width = 2 * feature
    shard = w_query.shape[0]
    experts = w_router.shape[1]
    per_core = experts // 2
    group = per_core // GROUPS
    hid = w_gate.shape[2]
    q_width, kv_width = w_query.shape[1], w_key.shape[1]
    pairs = kv_width // LANES
    deep = ctx // 2
    tp, c = lax.axis_index("tp"), lax.axis_index("ctx")
    core, y = c % 2, c // 2
    ring = Ring(wide, ctx)
    n = ring.size
    core_perm = [(i, i ^ 1) for i in range(ctx)]
    swap_core = lambda a: lax.ppermute(a, "ctx", core_perm)
    swap_tp = lambda a: lax.ppermute(a, "tp", [(0, 1), (1, 0)])
    up_y = [(i, (i + 2) % ctx) for i in range(ctx)]
    down_y = [(i, (i - 2) % ctx) for i in range(ctx)]
    tp_scalar = tp.astype(jnp.int32).reshape(1)

    def by_core(mine, other, axis):
        return jnp.where(
            core == 0,
            jnp.concatenate([mine, other], axis),
            jnp.concatenate([other, mine], axis),
        )

    def by_tp(mine, other):
        return jnp.where(
            tp == 0, jnp.concatenate([mine, other], 1), jnp.concatenate([other, mine], 1)
        )

    kv_cols = []
    for pair in range(pairs):
        cols = slice(pair * LANES, (pair + 1) * LANES)
        kv_cols += [w_key[:, cols], w_value[:, cols]]
    small = jnp.concatenate([w_router, gain_attn[:, None], gain_ffn[:, None]], axis=1)
    small = jnp.pad(small, ((0, 0), (0, LANES - experts - 2)))
    bundle = jnp.concatenate([w_query, *kv_cols, w_out.T, small], axis=1)
    own_tokens = tokens.reshape(rows, feature)
    own_cot = cotangent.reshape(rows, feature)
    other_tokens = swap_tp(own_tokens)
    mine = ring.gather(bundle[None])[:, 0]
    theirs = swap_core(mine)
    bundle_full = by_core(mine[:, None], theirs[:, None], 1).reshape(width, -1)
    qkv_width = q_width + 2 * kv_width
    w_qkv = bundle_full[:, :qkv_width]
    wo_mine = bundle_full[:, qkv_width : qkv_width + q_width]
    w_small = bundle_full[:, qkv_width + q_width :]
    router = jnp.where(jnp.arange(LANES)[None, :] < experts, w_small, 0).astype(BF)
    gain_one = w_small[:, experts].astype(F32)[None, :]
    gain_two = w_small[:, experts + 1].astype(F32)[None, :]
    wo_other = swap_tp(wo_mine)

    packed = jnp.concatenate([w_gate, w_up, w_down.transpose(0, 2, 1)], axis=2)
    packed = packed.reshape(2, per_core, shard, 3 * hid)
    mine_w = lax.dynamic_index_in_dim(packed, core, 0, keepdims=False)
    other_w = swap_core(lax.dynamic_index_in_dim(packed, 1 - core, 0, keepdims=False))
    chip_w = by_core(mine_w, other_w, 1)
    group_w = [
        ring.gather(chip_w[i * group : (i + 1) * group]) for i in range(GROUPS)
    ]

    full_tokens = by_tp(own_tokens, other_tokens)
    half_width = HD // 2
    freqs = 10000.0 ** (-jnp.arange(half_width, dtype=F32) / half_width)
    local_pos = c * span + jnp.arange(span, dtype=jnp.int32)
    angles = local_pos.astype(F32)[:, None] * freqs[None, :]
    cosine, sine = jnp.cos(angles), jnp.sin(angles)
    cosine = jnp.tile(jnp.concatenate([cosine] * 4, axis=1), (seqs, 1))
    sine = jnp.tile(jnp.concatenate([-sine, sine, -sine, sine], axis=1), (seqs, 1))
    step_rows = min(rows, 256)
    steps = rows // step_rows
    row_spec = lambda cols: pl.BlockSpec((step_rows, cols), lambda i, *_: (i, 0))
    smem = pl.BlockSpec(memory_space=pltpu.SMEM)
    normed, queries, kv = pl.pallas_call(
        functools.partial(project_kernel, pairs, q_width),
        grid=(steps,),
        in_specs=[
            row_spec(width),
            whole((1, width)),
            whole((width, qkv_width)),
            row_spec(LANES),
            row_spec(LANES),
        ],
        out_specs=[row_spec(width), row_spec(q_width), row_spec(2 * kv_width)],
        out_shape=[
            jax.ShapeDtypeStruct((rows, width), BF),
            jax.ShapeDtypeStruct((rows, q_width), BF),
            jax.ShapeDtypeStruct((rows, 2 * kv_width), BF),
        ],
        compiler_params=params("arbitrary"),
        name="project",
    )(full_tokens, gain_one, w_qkv, cosine, sine)

    own_side = [kv]
    for _ in range(deep - 1):
        own_side.append(lax.ppermute(own_side[-1], "ctx", up_y))
    other_side = [swap_core(block) for block in own_side]
    kv_blocks = own_side + other_side
    base = jnp.stack(
        [(((y - k) % deep) * 2 + core) * span for k in range(deep)]
        + [(((y - k) % deep) * 2 + 1 - core) * span for k in range(deep)]
    ).astype(jnp.int32)
    length = ctx * span
    head_spec = lambda *_: pl.BlockSpec((span, 2 * LANES), lambda s, p, *_: (s, p))
    prob_spec = pl.BlockSpec((1, 2, 2 * span, length), lambda s, p, *_: (s, p, 0, 0))
    attended, probs = pl.pallas_call(
        functools.partial(attend_kernel, ctx, span),
        grid_spec=pltpu.PrefetchScalarGridSpec(
            num_scalar_prefetch=2,
            grid=(seqs, pairs),
            in_specs=[head_spec()] * (1 + ctx),
            out_specs=[head_spec(), prob_spec],
        ),
        out_shape=[
            jax.ShapeDtypeStruct((rows, q_width), BF),
            jax.ShapeDtypeStruct((seqs, 2 * pairs, 2 * span, length), BF),
        ],
        compiler_params=params("arbitrary", "arbitrary"),
        name="attend",
    )(prefix, base, queries, *kv_blocks)
    attended_other = swap_tp(attended)

    full_cot = by_tp(own_cot, swap_tp(own_cot))
    peer_cot = swap_core(full_cot)
    cot_t, peer_cot_t = full_cot.T, peer_cot.T

    route_rows = routes.reshape(rows, TOP)
    middle, normed_two, normed_two_t, gates = pl.pallas_call(
        middle_kernel,
        grid=(steps,),
        in_specs=[
            row_spec(q_width),
            row_spec(q_width),
            whole((width, q_width)),
            whole((width, q_width)),
            row_spec(width),
            whole((1, width)),
            whole((width, LANES)),
            row_spec(TOP),
        ],
        out_specs=[
            row_spec(width),
            row_spec(width),
            pl.BlockSpec((width, step_rows), lambda i: (0, i)),
            row_spec(LANES),
        ],
        out_shape=[
            jax.ShapeDtypeStruct((rows, width), F32),
            jax.ShapeDtypeStruct((rows, width), BF),
            jax.ShapeDtypeStruct((width, rows), BF),
            jax.ShapeDtypeStruct((rows, LANES), F32),
        ],
        compiler_params=params("arbitrary"),
        name="middle",
    )(attended, attended_other, wo_mine, wo_other, full_tokens, gain_two, router, route_rows)

    peer_two, peer_two_t, peer_gates = (
        swap_core(normed_two),
        swap_core(normed_two_t),
        swap_core(gates),
    )
    acc_shapes = [jax.ShapeDtypeStruct((rows, width), F32)] * 4 + [
        jax.ShapeDtypeStruct((rows, LANES), F32)
    ] * 2
    acc_specs = [whole((rows, width))] * 4 + [whole((rows, LANES))] * 2
    chip_rows = 2 * shard
    w_spec = pl.BlockSpec((n, 1, chip_rows, 3 * hid), lambda e, *_: (0, e, 0, 0))
    accs = ()
    shards = []
    for i in range(GROUPS):
        column = (core * per_core + i * group).astype(jnp.int32).reshape(1)
        *accs, grads = pl.pallas_call(
            functools.partial(moe_kernel, i == 0),
            grid=(group,),
            in_specs=[smem, w_spec]
            + [whole((rows, width))] * 2
            + [whole((width, rows))] * 2
            + [whole((rows, width))] * 2
            + [whole((width, rows))] * 2
            + [whole((rows, LANES))] * 2
            + (acc_specs if i else []),
            out_specs=acc_specs + [w_spec],
            out_shape=acc_shapes
            + [jax.ShapeDtypeStruct((n, group, chip_rows, 3 * hid), BF)],
            compiler_params=params("arbitrary"),
            name="experts",
        )(
            column,
            group_w[i],
            normed_two,
            peer_two,
            normed_two_t,
            peer_two_t,
            full_cot,
            peer_cot,
            cot_t,
            peer_cot_t,
            gates,
            peer_gates,
            *accs,
        )
        shards.append(ring.scatter(grads))
    moe, moe_peer, grad_two, grad_two_peer, pull, pull_peer = accs

    part = (grad_two + swap_core(grad_two_peer.astype(BF)).astype(F32)).astype(BF)
    part_other = swap_tp(part)
    pull_mine = pull + swap_core(pull_peer)
    pull_other = swap_tp(pull_mine)
    grad_middle, grad_branch, grad_attended, grad_logits, gain_two_term = pl.pallas_call(
        middle_back_kernel,
        grid=(steps,),
        in_specs=[
            smem,
            row_spec(width),
            row_spec(width),
            row_spec(LANES),
            row_spec(LANES),
            row_spec(LANES),
            row_spec(width),
            row_spec(width),
            whole((1, width)),
            whole((width, LANES)),
            whole((width, q_width)),
        ],
        out_specs=[
            row_spec(feature),
            row_spec(width),
            row_spec(q_width),
            row_spec(LANES),
            whole((1, width)),
        ],
        out_shape=[
            jax.ShapeDtypeStruct((rows, feature), F32),
            jax.ShapeDtypeStruct((rows, width), BF),
            jax.ShapeDtypeStruct((rows, q_width), BF),
            jax.ShapeDtypeStruct((rows, LANES), BF),
            jax.ShapeDtypeStruct((1, width), F32),
        ],
        compiler_params=params("arbitrary"),
        name="middle_back",
    )(
        tp_scalar,
        part,
        part_other,
        pull_mine,
        pull_other,
        gates,
        middle,
        full_cot,
        gain_two,
        router,
        wo_mine,
    )

    moe_sum = moe + swap_core(moe_peer.astype(BF)).astype(F32)
    moe_halves = moe_sum.reshape(rows, 2, feature)
    moe_own = lax.dynamic_index_in_dim(moe_halves, tp, 1, keepdims=False)
    moe_send = lax.dynamic_index_in_dim(moe_halves, 1 - tp, 1, keepdims=False).astype(BF)
    middle_own = lax.dynamic_index_in_dim(
        middle.reshape(rows, 2, feature), tp, 1, keepdims=False
    )
    output = (middle_own + moe_own + swap_tp(moe_send).astype(F32)).astype(BF)

    back_spec = pl.BlockSpec((deep, span, 2 * LANES), lambda s, p: (0, s, p))
    grad_q, grad_kv_own, grad_kv_peer = pl.pallas_call(
        functools.partial(attend_back_kernel, ctx, span),
        grid=(seqs, pairs),
        in_specs=[prob_spec] + [head_spec()] * (2 + ctx),
        out_specs=[head_spec(), back_spec, back_spec],
        out_shape=[
            jax.ShapeDtypeStruct((rows, q_width), F32),
            jax.ShapeDtypeStruct((deep, rows, 2 * kv_width), BF),
            jax.ShapeDtypeStruct((deep, rows, 2 * kv_width), BF),
        ],
        compiler_params=params("arbitrary", "arbitrary"),
        name="attend_back",
    )(probs, queries, grad_attended, *kv_blocks)
    from_peer = swap_core(grad_kv_peer)
    travel = None
    for k in range(deep - 1, 0, -1):
        piece = grad_kv_own[k] + from_peer[k]
        if travel is not None:
            piece = piece + travel
        travel = lax.ppermute(piece, "ctx", down_y)

    grad_qkv, grad_own, grad_send, inner, gain_one_term = pl.pallas_call(
        functools.partial(project_back_kernel, pairs),
        grid=(steps,),
        in_specs=[
            smem,
            row_spec(q_width),
            row_spec(2 * kv_width),
            row_spec(2 * kv_width),
            row_spec(2 * kv_width),
            row_spec(LANES),
            row_spec(LANES),
            whole((width, qkv_width)),
            row_spec(width),
            whole((1, width)),
        ],
        out_specs=[
            row_spec(qkv_width),
            row_spec(feature),
            row_spec(feature),
            row_spec(LANES),
            whole((1, width)),
        ],
        out_shape=[
            jax.ShapeDtypeStruct((rows, qkv_width), BF),
            jax.ShapeDtypeStruct((rows, feature), F32),
            jax.ShapeDtypeStruct((rows, feature), BF),
            jax.ShapeDtypeStruct((rows, LANES), F32),
            jax.ShapeDtypeStruct((1, width), F32),
        ],
        compiler_params=params("arbitrary"),
        name="project_back",
    )(
        tp_scalar,
        grad_q,
        grad_kv_own[0],
        from_peer[0],
        travel if travel is not None else jnp.zeros_like(kv),
        cosine,
        sine,
        w_qkv,
        full_tokens,
        gain_one,
    )
    dots = inner[:, 0]
    dots = dots + swap_tp(dots)
    grad_tokens = (
        grad_middle
        + grad_own
        + swap_tp(grad_send).astype(F32)
        - own_tokens.astype(F32) * dots[:, None]
    )

    def scatter_rows(array):
        parts = array.astype(BF).reshape(n, 2, shard, array.shape[1])
        kept = lax.dynamic_index_in_dim(parts, core, 1)
        sent = swap_core(lax.dynamic_index_in_dim(parts, 1 - core, 1))
        return ring.scatter(kept + sent)[0]

    out_term = tn(grad_branch, attended)
    router_term = tn(normed_two, grad_logits)[:, :experts]
    early = jnp.concatenate([out_term, router_term, gain_two_term.T], axis=1)
    early = jnp.pad(early, ((0, 0), (0, LANES - experts - 1)))
    early = scatter_rows(early)
    late = jnp.concatenate([tn(normed, grad_qkv), gain_one_term.T], axis=1)
    late = jnp.pad(late, ((0, 0), (0, LANES - 1)))
    late = scatter_rows(late)
    grad_out = early[:, :q_width].T
    grad_router = early[:, q_width : q_width + experts]
    grad_gain_ffn = early[:, q_width + experts]
    grad_query = late[:, :q_width]
    key_cols, value_cols = [], []
    for pair in range(pairs):
        lo = q_width + pair * 2 * LANES
        key_cols.append(late[:, lo : lo + LANES])
        value_cols.append(late[:, lo + LANES : lo + 2 * LANES])
    grad_key = jnp.concatenate(key_cols, axis=1)
    grad_value = jnp.concatenate(value_cols, axis=1)
    gain_half = late[:, qkv_width]
    grad_gain_attn = gain_half + swap_tp(gain_half)

    sums = jnp.concatenate(shards, axis=0).reshape(per_core, 2, shard, 3 * hid)
    kept = lax.dynamic_index_in_dim(sums, core, 1, keepdims=False).astype(BF)
    sent = swap_core(lax.dynamic_index_in_dim(sums, 1 - core, 1, keepdims=False).astype(BF))
    all_experts = by_core(kept, sent, 0).astype(F32)
    grad_gate = all_experts[:, :, :hid]
    grad_up = all_experts[:, :, hid : 2 * hid]
    grad_down = all_experts[:, :, 2 * hid :].transpose(0, 2, 1)

    return (
        output.reshape(seqs, span, feature),
        grad_tokens.reshape(seqs, span, feature),
        grad_query,
        grad_key,
        grad_value,
        grad_out,
        grad_router,
        grad_gain_attn,
        grad_gain_ffn,
        grad_gate,
        grad_up,
        grad_down,
    )


def solution(mesh):
    in_specs = (
        P("fsdp", "ctx", "tp"),
        P("fsdp"),
        P("ctx", "fsdp", None, None),
        P(("fsdp", "ctx"), "tp"),
        P(("fsdp", "ctx"), "tp"),
        P(("fsdp", "ctx"), "tp"),
        P("tp", ("fsdp", "ctx")),
        P(("fsdp", "ctx"), None),
        P(("fsdp", "ctx")),
        P(("fsdp", "ctx")),
        P(None, ("fsdp", "ctx"), "tp"),
        P(None, ("fsdp", "ctx"), "tp"),
        P(None, "tp", ("fsdp", "ctx")),
        P("fsdp", "ctx", "tp"),
    )
    out_specs = (
        P("fsdp", "ctx", "tp"),
        P("fsdp", "ctx", "tp"),
        P(("fsdp", "ctx"), "tp"),
        P(("fsdp", "ctx"), "tp"),
        P(("fsdp", "ctx"), "tp"),
        P("tp", ("fsdp", "ctx")),
        P(("fsdp", "ctx"), None),
        P(("fsdp", "ctx")),
        P(("fsdp", "ctx")),
        P(None, ("fsdp", "ctx"), "tp"),
        P(None, ("fsdp", "ctx"), "tp"),
        P(None, "tp", ("fsdp", "ctx")),
    )
    return jax.shard_map(
        per_device, mesh=mesh, in_specs=in_specs, out_specs=out_specs, check_vma=False
    )
```

```python
import functools

import jax
import jax.numpy as jnp
from jax import lax
from jax.experimental import pallas as pl
from jax.experimental.pallas import tpu as pltpu
from jax.sharding import PartitionSpec as P

HD = 64
TOP = 8
LANES = 128

EPSILON = 1e-06
ATTN_SCALE = 0.015625
RESIDUAL_SCALE = 0.22
MASKED_SCORE = -1e30
GATHERS = 2
CALLS = 2
RING = ("fsdp", "ctx")
BF = jnp.bfloat16
F32 = jnp.float32
VMEM_LIMIT = 24 * 1024 * 1024
MOE_VMEM = 56 * 1024 * 1024


def nt(a, b):
    return lax.dot_general(a, b, (((1,), (1,)), ((), ())), preferred_element_type=F32)


def nn(a, b):
    return lax.dot_general(a, b, (((1,), (0,)), ((), ())), preferred_element_type=F32)


def tn(a, b):
    return lax.dot_general(a, b, (((0,), (0,)), ((), ())), preferred_element_type=F32)


def params(*semantics):
    return pltpu.CompilerParams(
        dimension_semantics=semantics, vmem_limit_bytes=VMEM_LIMIT
    )


def whole(shape):
    zeros = (0,) * len(shape)
    return pl.BlockSpec(shape, lambda *_: zeros, pipeline_mode=pl.Buffered(1))


def swap_halves(slab):
    lane = lax.broadcasted_iota(jnp.int32, slab.shape, 1) % HD
    return jnp.where(
        lane < HD // 2, pltpu.roll(slab, LANES - HD // 2, 1), pltpu.roll(slab, HD // 2, 1)
    )


def column_as_row(ref, column):
    lane = lax.broadcasted_iota(jnp.int32, (16, ref.shape[1]), 1)
    return nt(jnp.where(lane == column, 1.0, 0.0).astype(BF), ref[...])[:1]


def pack_kernel(q_ref, k_ref, v_ref, out_ref, router_ref, one_ref, two_ref, packed_ref):
    rows, q_width = q_ref.shape
    packed_ref[0, :, :q_width] = q_ref[...]
    at = q_width
    for pair in range(k_ref.shape[1] // LANES):
        cols = slice(pair * LANES, (pair + 1) * LANES)
        packed_ref[0, :, at : at + LANES] = k_ref[:, cols]
        packed_ref[0, :, at + LANES : at + 2 * LANES] = v_ref[:, cols]
        at += 2 * LANES
    packed_ref[0, :, at : at + q_width] = out_ref[...].T
    at += q_width
    experts = router_ref.shape[1]
    square = (rows, rows)
    diagonal = lax.broadcasted_iota(jnp.int32, square, 0) == lax.broadcasted_iota(
        jnp.int32, square, 1
    )
    gains = [
        jnp.sum(jnp.where(diagonal, r[...].astype(F32), 0.0), axis=1, keepdims=True)
        for r in (one_ref, two_ref)
    ]
    lane = lax.broadcasted_iota(jnp.int32, (rows, LANES), 1)
    wide = jnp.where(lane == experts, gains[0], 0.0)
    wide = jnp.where(lane == experts + 1, gains[1], wide)
    packed_ref[0, :, at:] = wide.astype(BF)
    packed_ref[0, :, at : at + experts] = router_ref[...]


def pack_experts_kernel(core_ref, gate_ref, up_ref, down_ref, mine_ref, other_ref):
    count, _, cols = mine_ref.shape
    hid = cols // 3
    for out_ref, core in ((mine_ref, core_ref[0]), (other_ref, 1 - core_ref[0])):
        for i in range(count):
            e = core * count + i
            out_ref[i, :, :hid] = gate_ref[e]
            out_ref[i, :, hid : 2 * hid] = up_ref[e]
            out_ref[i, :, 2 * hid :] = down_ref[e].T


def join_kernel(core_ref, mine_ref, other_ref, *groups):
    rows = mine_ref.shape[1]
    for mine_first in (True, False):

        @pl.when((core_ref[0] == 0) == mine_first)
        def _():
            at = 0
            for out_ref in groups:
                size = out_ref.shape[0]
                first, second = (mine_ref, other_ref) if mine_first else (other_ref, mine_ref)
                out_ref[:, :rows] = first[at : at + size]
                out_ref[:, rows:] = second[at : at + size]
                at += size


def assemble_kernel(places, where_ref, *refs):
    count = len(places)
    parts, outs, sem = refs[:count], refs[count:-1], refs[-1]

    def copies():
        for j, (_, _, rows) in enumerate(places):
            first = 0
            for out in outs:
                cols = out.shape[1]
                yield pltpu.make_async_copy(
                    parts[j].at[0, :, pl.ds(first, cols)],
                    out.at[pl.ds(pl.multiple_of(where_ref[j], 16), rows)],
                    sem,
                )
                first += cols

    for copy in copies():
        copy.start()
    for copy in copies():
        copy.wait()


def side_by_side(tp_ref, mine, other):
    first = tp_ref[0] == 0
    return jnp.concatenate([jnp.where(first, mine, other), jnp.where(first, other, mine)], axis=1)


def features_kernel(tp_ref, mine_ref, other_ref, full_ref):
    full_ref[...] = side_by_side(tp_ref, mine_ref[...], other_ref[...])


def project_kernel(
    pairs,
    q_width,
    gain_col,
    tp_ref,
    mine_ref,
    other_ref,
    small_ref,
    w_ref,
    cos_ref,
    sin_ref,
    x_ref,
    n_ref,
    q_ref,
    kv_ref,
):
    x_ref[...] = side_by_side(tp_ref, mine_ref[...], other_ref[...])
    x = x_ref[...].astype(F32)
    gain = column_as_row(small_ref, gain_col)
    scale = lax.rsqrt(jnp.mean(x * x, axis=1, keepdims=True) + EPSILON)
    normed = (x * scale * gain).astype(BF)
    n_ref[...] = normed
    cosine, sine = cos_ref[...], sin_ref[...]
    raw = nn(normed, w_ref[...])
    for slab in range(q_width // LANES):
        cols = slice(slab * LANES, (slab + 1) * LANES)
        part = raw[:, cols]
        turned = (part * cosine + swap_halves(part) * sine).astype(BF)
        q_ref[:, cols] = (turned.astype(F32) * ATTN_SCALE).astype(BF)
    for pair in range(pairs):
        lo = pair * 2 * LANES
        part = raw[:, q_width + lo : q_width + lo + LANES]
        kv_ref[:, lo : lo + LANES] = (part * cosine + swap_halves(part) * sine).astype(BF)
        kv_ref[:, lo + LANES : lo + 2 * LANES] = raw[
            :, q_width + lo + LANES : q_width + lo + 2 * LANES
        ].astype(BF)


def attend_kernel(blocks, span, prefix_ref, base_ref, q_ref, *refs):
    kv_refs = refs[:blocks]
    out_ref, p_ref = refs[blocks:]
    limit_len = prefix_ref[pl.program_id(0)]
    local = base_ref[0] + lax.broadcasted_iota(jnp.int32, (span, 1), 0)
    limit = jnp.maximum(local + 1, limit_len)
    key_pos = jnp.concatenate(
        [
            base_ref[j] + lax.broadcasted_iota(jnp.int32, (1, span), 1)
            for j in range(blocks)
        ],
        axis=1,
    )
    visible = key_pos < limit
    visible = jnp.concatenate([visible, visible], axis=0)
    for g in range(2):
        keys = jnp.concatenate([r[:, g * HD : (g + 1) * HD] for r in kv_refs], axis=0)
        vals = jnp.concatenate(
            [r[:, LANES + g * HD : LANES + (g + 1) * HD] for r in kv_refs], axis=0
        )
        first, second = 2 * g * HD, (2 * g + 1) * HD
        queries = jnp.concatenate(
            [q_ref[:, first : first + HD], q_ref[:, second : second + HD]], axis=0
        )
        scores = jnp.where(visible, nt(queries, keys), MASKED_SCORE)
        expo = jnp.exp(scores - jnp.max(scores, axis=1, keepdims=True))
        probs = (expo * (1.0 / jnp.sum(expo, axis=1, keepdims=True))).astype(BF)
        p_ref[0, g] = probs
        att = nn(probs, vals).astype(BF)
        out_ref[:, first : first + HD] = att[:span]
        out_ref[:, second : second + HD] = att[span:]


def attend_back_kernel(blocks, span, p_ref, q_ref, g_ref, cos_ref, sin_ref, *refs):
    kv_refs = refs[:blocks]
    dq_ref, own_ref, other_ref = refs[blocks:]
    cosine, sine = cos_ref[...], sin_ref[...]
    parts = []
    for g in range(2):
        keys = jnp.concatenate([r[:, g * HD : (g + 1) * HD] for r in kv_refs], axis=0)
        vals = jnp.concatenate(
            [r[:, LANES + g * HD : LANES + (g + 1) * HD] for r in kv_refs], axis=0
        )
        first, second = 2 * g * HD, (2 * g + 1) * HD
        queries = jnp.concatenate(
            [q_ref[:, first : first + HD], q_ref[:, second : second + HD]], axis=0
        )
        grads = jnp.concatenate(
            [g_ref[:, first : first + HD], g_ref[:, second : second + HD]], axis=0
        )
        probs = p_ref[0, g]
        wide = probs.astype(F32)
        grad_probs = nt(grads, vals)
        inner = jnp.sum(wide * grad_probs, axis=1, keepdims=True)
        grad_scores = (wide * (grad_probs - inner)).astype(BF)
        dq = nn(grad_scores, keys) * ATTN_SCALE
        slab = jnp.concatenate([dq[:span], dq[span:]], axis=1)
        turned = slab * cosine - swap_halves(slab) * sine
        dq_ref[:, first : first + LANES] = turned.astype(BF)
        parts.append((nn(queries.T, grad_scores), nn(grads.T, probs)))
    stacked = jnp.concatenate([parts[0][0], parts[1][0], parts[0][1], parts[1][1]], axis=0)
    turned = stacked.T.astype(BF)
    half = blocks // 2
    for j in range(half):
        own_ref[j] = turned[j * span : (j + 1) * span]
        other_ref[j] = turned[(half + j) * span : (half + j + 1) * span]


def middle_kernel(
    gain_col, a_ref, b_ref, wa_ref, wb_ref, x_ref, small_ref, routes_ref, m_ref, n_ref, g_ref
):
    branch = nt(a_ref[...], wa_ref[...]) + nt(b_ref[...], wb_ref[...])
    middle = x_ref[...].astype(F32) + RESIDUAL_SCALE * branch
    m_ref[...] = middle
    scale = lax.rsqrt(jnp.mean(middle * middle, axis=1, keepdims=True) + EPSILON)
    wide = middle * scale * column_as_row(small_ref, gain_col)
    normed = wide.astype(BF)
    width = normed.shape[1]
    n_ref[:, :width] = normed
    logits = nn(normed, small_ref[...])
    lane = lax.broadcasted_iota(jnp.int32, logits.shape, 1)
    routes = routes_ref[...]
    routed = lane == routes[:, 0:1]
    for k in range(1, TOP):
        routed = routed | (lane == routes[:, k : k + 1])
    logits = jnp.where(routed, logits, MASKED_SCORE)
    expo = jnp.where(routed, jnp.exp(logits - jnp.max(logits, axis=1, keepdims=True)), 0.0)
    gates = expo / jnp.sum(expo, axis=1, keepdims=True)
    g_ref[...] = gates
    n_ref[:, width:] = in_two(gates, gain_col - 1)


def in_two(pull, experts):
    high = pull.astype(BF).astype(F32)
    return (high + pltpu.roll(pull - high, experts, 1)).astype(BF)


def in_one(terms, experts):
    wide = terms.astype(F32)
    lane = lax.broadcasted_iota(jnp.int32, wide.shape, 1)
    both = wide + pltpu.roll(wide, LANES - experts, 1)
    return jnp.where(lane < experts, both, 0.0)


def moe_kernel(first_call, last_call, experts, start, group, places, where_ref, *refs):
    count = len(places)
    w_parts, refs = refs[:count], refs[count:]
    sources, refs = refs[:4], refs[4:]
    inits, refs = ((), refs) if first_call else (refs[:2], refs[2:])
    outs, mixed_out, dw_parts, refs = refs[:2], refs[2], refs[3 : 3 + count], refs[3 + count :]
    here, accs, refs = refs[:4], refs[4:6], refs[6:]
    mixed_all, narrow, w_all, dw_all, w_sem, dw_sem, near_sem, acc_sem, out_sem, mixed_sem = refs
    xa_ref, ya_ref, xb_ref, yb_ref = here
    rows, width = ya_ref.shape
    hid = w_all.shape[2] // 3

    def window(j):
        return pl.ds(pl.multiple_of(where_ref[1 + j], 16), places[j][2])

    def load(e, j):
        return pltpu.make_async_copy(
            w_parts[j].at[start + e], w_all.at[e, window(j)], w_sem.at[e]
        )

    def store(e, j):
        return pltpu.make_async_copy(
            dw_all.at[e % 2, window(j)], dw_parts[j].at[e], dw_sem.at[e % 2]
        )

    nears = [
        pltpu.make_async_copy(a, b, near_sem.at[i]) for i, (a, b) in enumerate(zip(sources, here))
    ]
    fetches = [
        pltpu.make_async_copy(a, b, acc_sem.at[i]) for i, (a, b) in enumerate(zip(inits, accs))
    ]
    mixed_store = pltpu.make_async_copy(mixed_all, mixed_out, mixed_sem)
    for j in range(count):
        load(0, j).start()
    for copy in nears[:2]:
        copy.start()
    results = []
    for e in range(group):
        for j in range(count):
            load(e, j).wait()
        if e == 0:
            for copy in nears[:2]:
                copy.wait()
            for copy in [*fetches[:1], *nears[2:], *fetches[1:]]:
                copy.start()
        expert = where_ref[0] + e
        w_gu, w_d = w_all[e, :, : 2 * hid], w_all[e, :, 2 * hid :]
        kept = []
        for side, (x_ref, y_ref) in enumerate(((xa_ref, ya_ref), (xb_ref, yb_ref))):
            acc = accs[side]
            if e == 0 and side == 1:
                for copy in nears[2:]:
                    copy.wait()
                for other in range(1, group):
                    for j in range(count):
                        load(other, j).start()
            pre = nn(x_ref[:, :width], w_gu)
            back = nn(y_ref[...], w_d)
            gates = in_one(x_ref[:, width:], experts)
            lane = lax.broadcasted_iota(jnp.int32, gates.shape, 1)
            mask = lane == expert
            weight = RESIDUAL_SCALE * jnp.sum(
                jnp.where(mask, gates, 0.0), axis=1, keepdims=True
            )
            gate_pre, up_pre = pre[:, :hid], pre[:, hid:]
            sig = jax.nn.sigmoid(gate_pre)
            act = gate_pre * sig
            hidden = act * up_pre
            pull = RESIDUAL_SCALE * jnp.sum(back * hidden, axis=1, keepdims=True)
            scaled = weight * back
            d_up = scaled * act
            d_gate = scaled * up_pre * (sig + act * (1.0 - sig))
            d_gu = jnp.concatenate([d_gate.astype(BF), d_up.astype(BF)], axis=1)
            mixed = (weight * hidden).astype(BF)
            mixed_all[e, side * rows : (side + 1) * rows] = mixed
            if first_call and e == 0:
                acc[:, :width] = nt(d_gu, w_gu)
                acc[:, width:] = jnp.where(mask, pull, 0.0)
            else:
                if e == 0:
                    fetches[side].wait()
                acc[:, :width] += nt(d_gu, w_gu)
                acc[:, width:] += jnp.where(mask, pull, 0.0)
            kept.append((d_gu, mixed))
            if e == group - 1:
                if last_call and side:
                    narrow[:, :width] = acc[:, :width].astype(BF)
                    narrow[:, width:] = in_two(acc[:, width:], experts)
                    acc = narrow
                results.append(pltpu.make_async_copy(acc, outs[side], out_sem.at[side]))
                results[-1].start()
        if e == group - 1:
            mixed_store.start()
        dw_gu = tn(xa_ref[:, :width], kept[0][0]) + tn(xb_ref[:, :width], kept[1][0])
        dw_d = tn(ya_ref[...], kept[0][1]) + tn(yb_ref[...], kept[1][1])
        if e >= 2:
            for j in range(count):
                store(e - 2, j).wait()
        dw_all[e % 2, :, : 2 * hid] = dw_gu.astype(BF)
        dw_all[e % 2, :, 2 * hid :] = dw_d.astype(BF)
        for j in range(count):
            store(e, j).start()
    for e in range(max(0, group - 2), group):
        for j in range(count):
            store(e, j).wait()
    for copy in results:
        copy.wait()
    mixed_store.wait()


def moe_sum_kernel(places, sets, calls, group, where_ref, *refs):
    count = len(places)
    w_sets = [refs[k * count : (k + 1) * count] for k in range(sets)]
    refs = refs[sets * count :]
    mixed_parts, refs = refs[:calls], refs[calls:]
    own_ref, peer_ref, w_all, mixed_all, total, w_sem, mixed_sem = refs
    hid = w_all.shape[2]
    rows = own_ref.shape[0]
    experts = calls * group
    set_size = experts // sets

    def loads(e):
        for j in range(count):
            yield pltpu.make_async_copy(
                w_sets[e // set_size][j].at[e % set_size, :, pl.ds(2 * hid, hid)],
                w_all.at[e % 2, pl.ds(pl.multiple_of(where_ref[1 + j], 16), places[j][2])],
                w_sem.at[e % 2],
            )
        yield pltpu.make_async_copy(
            mixed_parts[e // group].at[e % group], mixed_all.at[e % 2], mixed_sem.at[e % 2]
        )

    for copy in loads(0):
        copy.start()
    for e in range(experts):
        for copy in loads(e):
            copy.wait()
        if e + 1 < experts:
            for copy in loads(e + 1):
                copy.start()
        term = nt(mixed_all[e % 2], w_all[e % 2])
        if e == 0:
            total[...] = term
        else:
            total[...] += term
    own_ref[...] = total[:rows]
    peer_ref[...] = total[rows:].astype(BF)


def weight_grad_kernel(count, gain_at, core_ref, *refs):
    pairs, refs = refs[: 2 * count], refs[2 * count :]
    gain_ref, kept_ref, sent_ref = refs
    n, shard, _ = kept_ref.shape
    width = gain_ref.shape[1]
    terms = [tn(pairs[2 * i][:, :width], pairs[2 * i + 1][...]) for i in range(count)]
    if gain_at is not None:
        row = lax.broadcasted_iota(jnp.int32, (8, LANES), 0)
        lane = lax.broadcasted_iota(jnp.int32, (8, LANES), 1)
        place = jnp.where((row == 0) & (lane == gain_at), 1.0, 0.0)
        gains = tn(jnp.broadcast_to(gain_ref[...], (8, gain_ref.shape[1])), place)
        if terms[-1].shape[1] == LANES:
            terms[-1] = terms[-1] + gains
        else:
            terms.append(gains)
    first = 0
    for term in terms:
        cols = term.shape[1]
        parts = term.astype(BF).reshape(n, 2, shard, cols)
        for mine in range(2):

            @pl.when(core_ref[0] == mine)
            def _():
                kept_ref[:, :, first : first + cols] = parts[:, mine]
                sent_ref[:, :, first : first + cols] = parts[:, 1 - mine]

        first += cols


def order_kernel(places, chips_ref, *refs):
    count = len(places)
    pairs, parts = refs[:-count], refs[-count:]
    for j, (_, row, rows) in enumerate(places):
        chip = chips_ref[j]
        window = pl.ds(row, rows)
        first = 0
        for kept_ref, other_ref in zip(pairs[::2], pairs[1::2]):
            cols = kept_ref.shape[2]
            parts[j][0, :, first : first + cols] = kept_ref[chip, window] + other_ref[chip, window]
            first += cols


def add_terms_kernel(experts, own_ref, peer_ref, sum_ref):
    width = own_ref.shape[1] - LANES
    sum_ref[:, :width] = (own_ref[:, :width] + peer_ref[:, :width].astype(F32)).astype(BF)
    pull = own_ref[:, width:] + in_one(peer_ref[:, width:], experts)
    sum_ref[:, width:] = in_two(pull, experts)


def middle_back_kernel(
    gain_col,
    tp_ref,
    sa_ref,
    sb_ref,
    gates_ref,
    m_ref,
    y_ref,
    small_ref,
    wo_ref,
    gm_ref,
    branch_ref,
    att_ref,
    logit_ref,
    dgain_ref,
):
    @pl.when(pl.program_id(0) == 0)
    def _():
        dgain_ref[...] = jnp.zeros(dgain_ref.shape, F32)

    gates = gates_ref[...]
    width = m_ref.shape[1]
    pull = in_one(sa_ref[:, width:], gain_col - 1) + in_one(sb_ref[:, width:], gain_col - 1)
    weighted = gates * pull
    grad_logits = (weighted - gates * jnp.sum(weighted, axis=1, keepdims=True)).astype(BF)
    logit_ref[...] = grad_logits
    grad = sa_ref[:, :width].astype(F32) + sb_ref[:, :width].astype(F32)
    grad = grad + nt(grad_logits, small_ref[...])
    middle = m_ref[...]
    scale = lax.rsqrt(jnp.mean(middle * middle, axis=1, keepdims=True) + EPSILON)
    unit = middle * scale
    dgain_ref[...] += jnp.sum(grad * unit, axis=0, keepdims=True)
    scaled = grad * column_as_row(small_ref, gain_col)
    inner = jnp.sum(scaled * unit, axis=1, keepdims=True) * (1.0 / width)
    grad_middle = y_ref[...].astype(F32) + scale * (scaled - unit * inner)
    half = width // 2
    gm_ref[...] = jnp.where(tp_ref[0] == 0, grad_middle[:, :half], grad_middle[:, half:])
    branch = (RESIDUAL_SCALE * grad_middle).astype(BF)
    branch_ref[...] = branch
    att_ref[...] = nn(branch, wo_ref[...]).astype(BF)


def project_back_kernel(
    pairs,
    gain_col,
    tp_ref,
    dq_ref,
    kva_ref,
    kvb_ref,
    kvc_ref,
    cos_ref,
    sin_ref,
    w_ref,
    x_ref,
    small_ref,
    d_ref,
    own_ref,
    other_ref,
    dot_ref,
    dgain_ref,
):
    @pl.when(pl.program_id(0) == 0)
    def _():
        dgain_ref[...] = jnp.zeros(dgain_ref.shape, F32)

    cosine, sine = cos_ref[...], sin_ref[...]
    q_width = dq_ref.shape[1]
    kv = kva_ref[...].astype(F32) + kvb_ref[...].astype(F32) + kvc_ref[...].astype(F32)
    for pair in range(pairs):
        lo = pair * 2 * LANES
        part = kv[:, lo : lo + LANES]
        d_ref[:, lo : lo + LANES] = (part * cosine - swap_halves(part) * sine).astype(BF)
        d_ref[:, lo + LANES : lo + 2 * LANES] = kv[:, lo + LANES : lo + 2 * LANES].astype(BF)
    grad = nt(dq_ref[...], w_ref[:, :q_width]) + nt(d_ref[...], w_ref[:, q_width:])
    x = x_ref[...].astype(F32)
    width = x.shape[1]
    scale = lax.rsqrt(jnp.mean(x * x, axis=1, keepdims=True) + EPSILON)
    unit = x * scale
    dgain_ref[...] += jnp.sum(grad * unit, axis=0, keepdims=True)
    scaled = grad * column_as_row(small_ref, gain_col)
    inner = jnp.sum(scaled * unit, axis=1, keepdims=True) * (1.0 / width) * scale * scale
    dot_ref[...] = jnp.broadcast_to(inner, dot_ref.shape)
    scaled = scaled * scale
    half = width // 2
    is_first = tp_ref[0] == 0
    own_ref[...] = jnp.where(is_first, scaled[:, :half], scaled[:, half:])
    other_ref[...] = jnp.where(is_first, scaled[:, half:], scaled[:, :half]).astype(BF)


class Ring:
    def __init__(self, wide, ctx):
        self.wide, self.ctx, self.deep = wide, ctx, ctx // 2
        self.size = wide * self.deep
        deep = self.deep
        order = [
            (f, y)
            for y in range(deep)
            for f in (range(wide) if y % 2 == 0 else range(wide - 1, -1, -1))
        ]
        flat = [[f * ctx + y * 2 + c for f, y in order] for c in range(2)]
        n = self.size
        self.forward = [(row[i], row[(i + 1) % n]) for row in flat for i in range(n)]
        self.backward = [(b, a) for a, b in self.forward]
        f, c = lax.axis_index("fsdp"), lax.axis_index("ctx")
        y = c // 2
        self.place = y * wide + jnp.where(y % 2 == 0, f, wide - 1 - f)

    def chip(self, offset):
        place = (self.place + offset) % self.size
        y, q = place // self.wide, place % self.wide
        f = jnp.where(y % 2 == 0, q, self.wide - 1 - q)
        return f * self.deep + y

    def send(self, array, forward=True):
        return lax.ppermute(array, RING, self.forward if forward else self.backward)

    def places(self, rows):
        far, half = self.size // 2, rows // 2
        found = [(0, 0, rows)]
        for step in range(1, far):
            found += [(-step, 0, rows), (step, 0, rows)]
        if half % 16:
            return found + [(-far, 0, rows)]
        return found + [(-far, 0, half), (far, half, half)]


class Gather:
    def __init__(self, ring, block, name):
        self.ring, self.step, self.rows, self.name = ring, 0, block.shape[1], name
        self.moving = (block, block)
        self.parts = [block]

    def tick(self):
        self.step += 1
        ahead, back = self.moving
        if self.done():
            half = self.rows // 2
            if half % 16:
                self.parts.append(self.ring.send(ahead))
                return
            ahead, back = ahead[:, :half], back[:, half:]
        with jax.named_scope(f"{self.name}_step_{self.step}"):
            self.moving = (self.ring.send(ahead), self.ring.send(back, False))
        self.parts += self.moving

    def done(self):
        return self.step == self.ring.size // 2


class Scatter:
    def __init__(self, ring, parts, name):
        self.ring, self.parts, self.step, self.name = ring, parts, 0, name
        self.far = ring.size // 2
        self.halved = len(parts) == ring.size + 1
        self.moving = (parts[-2], parts[-1]) if self.halved else (parts[-1],)

    def tick(self):
        self.step += 1
        if self.step > 1:
            s = self.far - self.step + 1
            behind, near = self.parts[2 * s - 1], self.parts[2 * s]
            if self.step > 2:
                ahead, back = near + self.moving[0], behind + self.moving[1]
            elif self.halved:
                half = near.shape[1] // 2
                ahead = jnp.concatenate([near[:, :half] + self.moving[0], near[:, half:]], axis=1)
                back = jnp.concatenate(
                    [behind[:, :half], behind[:, half:] + self.moving[1]], axis=1
                )
            else:
                ahead, back = near + self.moving[0], behind
            self.moving = (ahead, back)
        with jax.named_scope(f"{self.name}_step_{self.step}"):
            self.moving = tuple(
                self.ring.send(array, i == 0) for i, array in enumerate(self.moving)
            )

    def done(self):
        return self.step == self.far

    def result(self):
        ahead, back = self.moving
        return self.parts[0].astype(F32) + ahead.astype(F32) + back.astype(F32)


def lock(*values):
    return lax.optimization_barrier(values)


def per_device(
    tokens,
    prefix,
    routes,
    w_query,
    w_key,
    w_value,
    w_out,
    w_router,
    gain_attn,
    gain_ffn,
    w_gate,
    w_up,
    w_down,
    cotangent,
):
    wide, ctx = lax.axis_size("fsdp"), lax.axis_size("ctx")
    seqs, span, feature = tokens.shape
    rows = seqs * span
    width = 2 * feature
    shard = w_query.shape[0]
    experts = w_router.shape[1]
    per_core = experts // 2
    hid = w_gate.shape[2]
    q_width, kv_width = w_query.shape[1], w_key.shape[1]
    pairs = kv_width // LANES
    deep = ctx // 2
    tp, c = lax.axis_index("tp"), lax.axis_index("ctx")
    core, y = c % 2, c // 2
    ring = Ring(wide, ctx)
    n = ring.size
    core_perm = [(i, i ^ 1) for i in range(ctx)]

    def swap_core(array, name="rows"):
        with jax.named_scope(f"{name}_over_core"):
            return lax.ppermute(array, "ctx", core_perm)

    def swap_tp(array, name="rows"):
        with jax.named_scope(f"{name}_over_tp"):
            return lax.ppermute(array, "tp", [(0, 1), (1, 0)])

    up_y = [(i, (i + 2) % ctx) for i in range(ctx)]
    down_y = [(i, (i - 2) % ctx) for i in range(ctx)]

    def shift_y(array, perm, name):
        with jax.named_scope(f"{name}_over_y"):
            return lax.ppermute(array, "ctx", perm)

    tp_scalar = tp.astype(jnp.int32).reshape(1)

    def by_core(mine, other, axis):
        return jnp.where(
            core == 0,
            jnp.concatenate([mine, other], axis),
            jnp.concatenate([other, mine], axis),
        )

    vmem = pl.BlockSpec(memory_space=pltpu.VMEM)
    smem = pl.BlockSpec(memory_space=pltpu.SMEM)
    any_spec = pl.BlockSpec(memory_space=pl.ANY)
    qkv_width = q_width + 2 * kv_width
    bundle = pl.pallas_call(
        pack_kernel,
        in_specs=[vmem] * 7,
        out_specs=vmem,
        out_shape=jax.ShapeDtypeStruct((1, shard, qkv_width + q_width + LANES), BF),
        compiler_params=params(),
        name="pack",
    )(w_query, w_key, w_value, w_out, w_router, gain_attn[None], gain_ffn[None])
    own_tokens = tokens.reshape(rows, feature)
    own_cot = cotangent.reshape(rows, feature)
    other_tokens = swap_tp(own_tokens, "own_tokens")
    first = Gather(ring, bundle, "bundle")
    from_core = [swap_core(bundle, "bundle")]
    core_scalar = core.astype(jnp.int32).reshape(1)
    half_shape = jax.ShapeDtypeStruct((per_core, shard, 3 * hid), BF)
    first.tick()
    mine_w, other_w = pl.pallas_call(
        pack_experts_kernel,
        in_specs=[smem] + [vmem] * 3,
        out_specs=[vmem] * 2,
        out_shape=[half_shape] * 2,
        compiler_params=params(),
        name="pack_experts",
    )(core_scalar, *lock(w_gate, w_up, w_down, bundle)[:3])
    blocks_w = list(
        pl.pallas_call(
            join_kernel,
            in_specs=[smem] + [vmem] * 2,
            out_specs=[vmem] * GATHERS,
            out_shape=[
                jax.ShapeDtypeStruct((per_core // GATHERS, 2 * shard, 3 * hid), BF)
            ]
            * GATHERS,
            compiler_params=params(),
            name="join",
        )(core_scalar, mine_w, swap_core(other_w, "other_w"))
    )
    first.tick()
    *first.moving, mine_w = lock(*first.moving, mine_w)
    first.tick()
    *first.moving, blocks_w[0] = lock(*first.moving, blocks_w[0])
    while not first.done():
        first.tick()
    from_core += [swap_core(part, "part") for part in first.parts[1:]]
    chips = [ring.chip(d) for d, _, _ in ring.places(shard)]
    chip_list = jnp.stack(chips).astype(jnp.int32)
    bundle_places = ring.places(shard)
    bundle_rows = [
        (chips[j] * 2 + side) * shard + row
        for side in (core, 1 - core)
        for j, (_, row, _) in enumerate(bundle_places)
    ]
    in_hbm = lambda array: pltpu.with_memory_space_constraint(array, pltpu.HBM)
    w_qkv, wo_mine, w_small = pl.pallas_call(
        functools.partial(assemble_kernel, bundle_places * 2),
        in_specs=[smem] + [any_spec] * len(bundle_rows),
        out_specs=[vmem] * 3,
        out_shape=[
            jax.ShapeDtypeStruct((width, w), BF) for w in (qkv_width, q_width, LANES)
        ],
        scratch_shapes=[pltpu.SemaphoreType.DMA(())],
        compiler_params=params(),
        name="assemble",
    )(
        jnp.stack(bundle_rows).astype(jnp.int32),
        *[in_hbm(part) for part in first.parts + from_core],
    )
    weights = [Gather(ring, block, f"weights_{i}") for i, block in enumerate(blocks_w)]
    under_way = []

    def segment(ticks, *values):
        held = [array for chain in under_way for array in chain.moving]
        out = lock(*held, *values)
        at = 0
        for chain in under_way:
            size = len(chain.moving)
            chain.moving = tuple(out[at : at + size])
            at += size
        under_way[:] = [chain for chain in ticks if not chain.done()]
        for chain in under_way:
            chain.tick()
        return out[at:]

    start_block = lock(blocks_w[0], *first.parts[-2:])[0]
    weights[0].moving = (start_block, start_block)
    segment(weights[:1], start_block)
    half_width = HD // 2
    freqs = 10000.0 ** (-jnp.arange(half_width, dtype=F32) / half_width)
    local_pos = c * span + jnp.arange(span, dtype=jnp.int32)
    angles = local_pos.astype(F32)[:, None] * freqs[None, :]
    cosine, sine = jnp.cos(angles), jnp.sin(angles)
    cosine = jnp.tile(jnp.concatenate([cosine] * 4, axis=1), (seqs, 1))
    sine = jnp.tile(jnp.concatenate([-sine, sine, -sine, sine], axis=1), (seqs, 1))
    step_rows = min(rows, 256)
    steps = rows // step_rows
    row_spec = lambda cols: pl.BlockSpec((step_rows, cols), lambda i, *_: (i, 0))
    full_tokens, normed, queries, kv = pl.pallas_call(
        functools.partial(project_kernel, pairs, q_width, experts),
        grid=(steps,),
        in_specs=[
            smem,
            row_spec(feature),
            row_spec(feature),
            whole((width, LANES)),
            whole((width, qkv_width)),
            row_spec(LANES),
            row_spec(LANES),
        ],
        out_specs=[row_spec(width), row_spec(width), row_spec(q_width), row_spec(2 * kv_width)],
        out_shape=[
            jax.ShapeDtypeStruct((rows, width), BF),
            jax.ShapeDtypeStruct((rows, width), BF),
            jax.ShapeDtypeStruct((rows, q_width), BF),
            jax.ShapeDtypeStruct((rows, 2 * kv_width), BF),
        ],
        compiler_params=params("arbitrary"),
        name="project",
    )(tp_scalar, own_tokens, other_tokens, w_small, w_qkv, cosine, sine)

    own_side = [kv]
    for _ in range(deep - 1):
        own_side.append(shift_y(own_side[-1], up_y, "kv"))
    other_side = [swap_core(block, "block") for block in own_side]
    kv_blocks = own_side + other_side
    base = jnp.stack(
        [(((y - k) % deep) * 2 + core) * span for k in range(deep)]
        + [(((y - k) % deep) * 2 + 1 - core) * span for k in range(deep)]
    ).astype(jnp.int32)
    length = ctx * span

    other_cot = swap_tp(own_cot, "own_cot")
    queries, other_cot, wo_mine, *kv_blocks = segment(
        weights[:1], queries, other_cot, wo_mine, *kv_blocks
    )
    wo_other = swap_tp(wo_mine, "wo_mine")
    head_spec = lambda: pl.BlockSpec((span, 2 * LANES), lambda s, p, *_: (s, p))
    prob_spec = pl.BlockSpec((1, 2, 2 * span, length), lambda s, p, *_: (s, p, 0, 0))
    attended, probs = pl.pallas_call(
        functools.partial(attend_kernel, ctx, span),
        grid_spec=pltpu.PrefetchScalarGridSpec(
            num_scalar_prefetch=2,
            grid=(seqs, pairs),
            in_specs=[head_spec()] * (1 + ctx),
            out_specs=[head_spec(), prob_spec],
        ),
        out_shape=[
            jax.ShapeDtypeStruct((rows, q_width), BF),
            pltpu.HBM((seqs, 2 * pairs, 2 * span, length), BF),
        ],
        compiler_params=params("arbitrary", "arbitrary"),
        name="attend",
    )(prefix, base, queries, *kv_blocks)

    full_cot = pl.pallas_call(
        features_kernel,
        in_specs=[smem] + [vmem] * 2,
        out_specs=vmem,
        out_shape=pltpu.HBM((rows, width), BF),
        compiler_params=params(),
        name="features",
    )(tp_scalar, own_cot, other_cot)
    attended, wo_other, full_cot = segment(weights[:1], attended, wo_other, full_cot)
    for _ in range(ring.size // 2 - 4):
        (attended,) = segment(weights[:1], attended)

    attended_other = swap_tp(attended, "attended")
    peer_cot = swap_core(full_cot, "full_cot")
    attended_other, peer_cot = segment(weights, attended_other, peer_cot)
    route_rows = routes.reshape(rows, TOP)
    middle, normed_two, gates = pl.pallas_call(
        functools.partial(middle_kernel, experts + 1),
        grid=(steps,),
        in_specs=[
            row_spec(q_width),
            row_spec(q_width),
            whole((width, q_width)),
            whole((width, q_width)),
            row_spec(width),
            whole((width, LANES)),
            row_spec(TOP),
        ],
        out_specs=[
            row_spec(width),
            row_spec(width + LANES),
            row_spec(LANES),
        ],
        out_shape=[
            pltpu.HBM((rows, width), F32),
            pltpu.HBM((rows, width + LANES), BF),
            jax.ShapeDtypeStruct((rows, LANES), F32),
        ],
        compiler_params=params("arbitrary"),
        name="middle",
    )(attended, attended_other, wo_mine, wo_other, full_tokens, w_small, route_rows)
    peer_two = swap_core(normed_two, "normed_two")
    (peer_two,) = segment(weights[1:], peer_two)

    near = [(normed_two, BF), (full_cot, BF), (peer_two, BF), (peer_cot, BF)]
    sources = [in_hbm(array) for array, _ in near]
    wide_acc, acc_shape = (rows, width), (rows, width + LANES)
    places = ring.places(2 * shard)
    count = len(places)
    part_rows = [ring.chip(d) * 2 * shard + row for d, row, _ in places]
    calls = GATHERS * CALLS
    call_size = per_core // calls

    def run_experts(call, accs):
        where = jnp.stack([core * per_core + call * call_size] + part_rows)
        first_call, last_call = call == 0, call == calls - 1
        outs = pl.pallas_call(
            functools.partial(
                moe_kernel,
                first_call,
                last_call,
                experts,
                call % CALLS * call_size,
                call_size,
                places,
            ),
            in_specs=[smem] + [any_spec] * (count + 4 + len(accs)),
            out_specs=[any_spec] * (3 + count),
            out_shape=[
                pltpu.HBM(acc_shape, F32),
                pltpu.HBM(acc_shape, BF if last_call else F32),
                pltpu.HBM((call_size, 2 * rows, hid), BF),
            ]
            + [pltpu.HBM((call_size, r, 3 * hid), BF) for _, _, r in places],
            scratch_shapes=[pltpu.VMEM(array.shape, kind) for array, kind in near]
            + [pltpu.VMEM(acc_shape, F32)] * 2
            + [
                pltpu.VMEM((call_size, 2 * rows, hid), BF),
                pltpu.VMEM(acc_shape, BF),
                pltpu.VMEM((call_size, width, 3 * hid), BF),
                pltpu.VMEM((2, width, 3 * hid), BF),
                pltpu.SemaphoreType.DMA((call_size,)),
                pltpu.SemaphoreType.DMA((2,)),
                pltpu.SemaphoreType.DMA((4,)),
                pltpu.SemaphoreType.DMA((2,)),
                pltpu.SemaphoreType.DMA((2,)),
                pltpu.SemaphoreType.DMA(()),
            ],
            compiler_params=pltpu.CompilerParams(vmem_limit_bytes=MOE_VMEM),
            name="experts",
        )(
            where.astype(jnp.int32),
            *[in_hbm(block) for block in weights[call // CALLS].parts],
            *sources,
            *accs,
        )
        return outs[:2], outs[2], outs[3:]

    accs, mixed_parts, sums = (), [], []

    for call in range(calls):
        for chain in weights[call // CALLS : call // CALLS + 1]:
            while not chain.done():
                accs = segment([chain, *sums[:1]], *accs)
        if call:
            accs = segment([*weights[1:], *sums][:2] if not weights[-1].done() else sums[:2], *accs)
        accs, mixed, dw_parts = run_experts(call, accs)
        mixed_parts.append(mixed)
        sums.append(Scatter(ring, dw_parts, f"sums_{call}"))

    grad_two, grad_two_peer = segment(sums[2:], *accs)
    grad_two, from_peer = segment([], grad_two, swap_core(grad_two_peer, "grad_two"))
    part = pl.pallas_call(
        functools.partial(add_terms_kernel, experts),
        grid=(steps,),
        in_specs=[row_spec(width + LANES)] * 2,
        out_specs=row_spec(width + LANES),
        out_shape=jax.ShapeDtypeStruct(acc_shape, BF),
        compiler_params=params("arbitrary"),
        name="add_terms",
    )(grad_two, from_peer)
    (part,) = segment(sums[:2], part)
    part_other = swap_tp(part, "part")

    moe, moe_peer = pl.pallas_call(
        functools.partial(moe_sum_kernel, places, GATHERS, calls, call_size),
        in_specs=[smem] + [any_spec] * (count * GATHERS + calls),
        out_specs=[vmem] * 2,
        out_shape=[
            jax.ShapeDtypeStruct(wide_acc, F32),
            jax.ShapeDtypeStruct(wide_acc, BF),
        ],
        scratch_shapes=[
            pltpu.VMEM((2, width, hid), BF),
            pltpu.VMEM((2, 2 * rows, hid), BF),
            pltpu.VMEM((2 * rows, width), F32),
            pltpu.SemaphoreType.DMA((2,)),
            pltpu.SemaphoreType.DMA((2,)),
        ],
        compiler_params=params(),
        name="experts_output",
    )(
        jnp.stack([core * 0] + part_rows).astype(jnp.int32),
        *[in_hbm(block) for chain in weights for block in chain.parts],
        *lock(*[in_hbm(mixed) for mixed in mixed_parts], part)[:-1],
    )
    part_other, moe, moe_peer = segment(sums[1:3], part_other, moe, moe_peer)
    grad_middle, grad_branch, grad_attended, grad_logits, gain_two_term = pl.pallas_call(
        functools.partial(middle_back_kernel, experts + 1),
        grid=(steps,),
        in_specs=[
            smem,
            row_spec(width + LANES),
            row_spec(width + LANES),
            row_spec(LANES),
            row_spec(width),
            row_spec(width),
            whole((width, LANES)),
            whole((width, q_width)),
        ],
        out_specs=[
            row_spec(feature),
            row_spec(width),
            row_spec(q_width),
            row_spec(LANES),
            whole((1, width)),
        ],
        out_shape=[
            jax.ShapeDtypeStruct((rows, feature), F32),
            jax.ShapeDtypeStruct((rows, width), BF),
            jax.ShapeDtypeStruct((rows, q_width), BF),
            jax.ShapeDtypeStruct((rows, LANES), BF),
            jax.ShapeDtypeStruct((1, width), F32),
        ],
        compiler_params=params("arbitrary"),
        name="middle_back",
    )(
        tp_scalar,
        part,
        part_other,
        gates,
        middle,
        full_cot,
        w_small,
        wo_mine,
    )

    back_spec = pl.BlockSpec((deep, span, 2 * LANES), lambda s, p: (0, s, p))
    turn_spec = pl.BlockSpec((span, LANES), lambda s, p: (s, 0))
    grad_q, grad_kv_own, grad_kv_peer = pl.pallas_call(
        functools.partial(attend_back_kernel, ctx, span),
        grid=(seqs, pairs),
        in_specs=[prob_spec] + [head_spec()] * 2 + [turn_spec] * 2 + [head_spec()] * ctx,
        out_specs=[head_spec(), back_spec, back_spec],
        out_shape=[
            jax.ShapeDtypeStruct((rows, q_width), BF),
            jax.ShapeDtypeStruct((deep, rows, 2 * kv_width), BF),
            jax.ShapeDtypeStruct((deep, rows, 2 * kv_width), BF),
        ],
        compiler_params=params("arbitrary", "arbitrary"),
        name="attend_back",
    )(in_hbm(probs), queries, grad_attended, cosine, sine, *kv_blocks)
    def weight_grads(name, pair_list, gain_term, gain_at, cols):
        shape = jax.ShapeDtypeStruct((n, shard, cols), BF)
        flat = [array for pair in pair_list for array in pair]
        kept, sent = pl.pallas_call(
            functools.partial(weight_grad_kernel, len(pair_list), gain_at),
            in_specs=[smem] + [vmem] * (len(flat) + 1),
            out_specs=[vmem] * 2,
            out_shape=[shape] * 2,
            compiler_params=params(),
            name="weight_grads",
        )(core_scalar, *flat, gain_term)
        return kept, sent

    early = weight_grads(
        "early",
        [(grad_branch, attended), (normed_two, grad_logits)],
        gain_two_term,
        experts,
        q_width + LANES,
    )
    grad_q, grad_kv_own, grad_kv_peer, moe_peer, *early = segment(
        [], grad_q, grad_kv_own, grad_kv_peer, moe_peer, *early
    )
    from_peer = swap_core(grad_kv_peer, "grad_kv")
    early_other = swap_core(early[1], "early")
    from_core_moe = swap_core(moe_peer, "moe")
    from_peer, early_other, from_core_moe = segment([], from_peer, early_other, from_core_moe)
    half_at = lambda array, side: lax.dynamic_slice_in_dim(array, side * feature, feature, 1)
    moe_sum = moe + from_core_moe.astype(F32)
    moe_send = half_at(moe_sum, 1 - tp).astype(BF)
    travel = jnp.zeros_like(kv)
    for k in range(deep - 1, 0, -1):
        piece = grad_kv_own[k] + from_peer[k]
        if k < deep - 1:
            piece = piece + travel
        piece, moe_send = segment([sums[2]] if k == 1 else [], piece, moe_send)
        travel = shift_y(piece, down_y, "grad_kv")
    moe_other = swap_tp(moe_send, "moe_send")
    travel, moe_other = segment(sums[2:], travel, moe_other)

    grad_kv, grad_own, grad_send, inner, gain_one_term = pl.pallas_call(
        functools.partial(project_back_kernel, pairs, experts),
        grid=(steps,),
        in_specs=[
            smem,
            row_spec(q_width),
            row_spec(2 * kv_width),
            row_spec(2 * kv_width),
            row_spec(2 * kv_width),
            row_spec(LANES),
            row_spec(LANES),
            whole((width, qkv_width)),
            row_spec(width),
            whole((width, LANES)),
        ],
        out_specs=[
            row_spec(2 * kv_width),
            row_spec(feature),
            row_spec(feature),
            row_spec(LANES),
            whole((1, width)),
        ],
        out_shape=[
            jax.ShapeDtypeStruct((rows, 2 * kv_width), BF),
            jax.ShapeDtypeStruct((rows, feature), F32),
            jax.ShapeDtypeStruct((rows, feature), BF),
            jax.ShapeDtypeStruct((rows, LANES), F32),
            jax.ShapeDtypeStruct((1, width), F32),
        ],
        compiler_params=params("arbitrary"),
        name="project_back",
    )(
        tp_scalar,
        grad_q,
        grad_kv_own[0],
        from_peer[0],
        travel,
        cosine,
        sine,
        w_qkv,
        full_tokens,
        w_small,
    )
    dots = inner[:, 0]
    late = weight_grads(
        "late",
        [(normed, grad_q), (normed, grad_kv)],
        gain_one_term,
        0,
        q_width + 2 * kv_width + LANES,
    )
    grad_send, dots, *late = segment(sums[3:], grad_send, dots, *late)
    late_other = swap_core(late[1], "late")
    dots_other = swap_tp(dots, "dots")
    grad_other = swap_tp(grad_send, "grad_send")
    late_other, dots_other, grad_other = segment([], late_other, dots_other, grad_other)
    cols = early_other.shape[2] + late_other.shape[2]
    last = Scatter(
        ring,
        pl.pallas_call(
            functools.partial(order_kernel, bundle_places),
            in_specs=[smem] + [vmem] * 4,
            out_specs=[vmem] * len(bundle_places),
            out_shape=[jax.ShapeDtypeStruct((1, r, cols), BF) for _, _, r in bundle_places],
            compiler_params=params(),
            name="order",
        )(chip_list, early[0], early_other, late[0], late_other),
        "last",
    )
    last.moving = lock(*last.moving, late_other)[:-1]
    segment([last, sums[3]])
    grad_tokens = (
        grad_middle
        + grad_own
        + grad_other.astype(F32)
        - own_tokens.astype(F32) * (dots + dots_other)[:, None]
    )
    output = (half_at(middle, tp) + half_at(moe_sum, tp) + moe_other.astype(F32)).astype(BF)
    while not all(chain.done() for chain in [last, *sums]):
        segment([last, *[chain for chain in sums if not chain.done()][:1]])
    last = last.result()[0]
    early, late = last[:, : q_width + LANES], last[:, q_width + LANES :]
    grad_out = early[:, :q_width].T
    grad_router = early[:, q_width : q_width + experts]
    grad_gain_ffn = early[:, q_width + experts]
    grad_query = late[:, :q_width]
    key_cols, value_cols = [], []
    for pair in range(pairs):
        lo = q_width + pair * 2 * LANES
        key_cols.append(late[:, lo : lo + LANES])
        value_cols.append(late[:, lo + LANES : lo + 2 * LANES])
    grad_key = jnp.concatenate(key_cols, axis=1)
    grad_value = jnp.concatenate(value_cols, axis=1)
    gain_half = late[:, q_width + 2 * kv_width]
    grad_gain_attn = gain_half + swap_tp(gain_half, "gain_half")

    totals = jnp.concatenate([chain.result() for chain in sums], axis=0)
    totals = totals.reshape(per_core, 2, shard, 3 * hid)
    kept = lax.dynamic_index_in_dim(totals, core, 1, keepdims=False).astype(BF)
    sent = swap_core(lax.dynamic_index_in_dim(totals, 1 - core, 1, keepdims=False).astype(BF))
    all_experts = by_core(kept, sent, 0).astype(F32)
    grad_gate = all_experts[:, :, :hid]
    grad_up = all_experts[:, :, hid : 2 * hid]
    grad_down = all_experts[:, :, 2 * hid :].transpose(0, 2, 1)

    return (
        output.reshape(seqs, span, feature),
        grad_tokens.reshape(seqs, span, feature),
        grad_query,
        grad_key,
        grad_value,
        grad_out,
        grad_router,
        grad_gain_attn,
        grad_gain_ffn,
        grad_gate,
        grad_up,
        grad_down,
    )


def solution(mesh):
    in_specs = (
        P("fsdp", "ctx", "tp"),
        P("fsdp"),
        P("ctx", "fsdp", None, None),
        P(("fsdp", "ctx"), "tp"),
        P(("fsdp", "ctx"), "tp"),
        P(("fsdp", "ctx"), "tp"),
        P("tp", ("fsdp", "ctx")),
        P(("fsdp", "ctx"), None),
        P(("fsdp", "ctx")),
        P(("fsdp", "ctx")),
        P(None, ("fsdp", "ctx"), "tp"),
        P(None, ("fsdp", "ctx"), "tp"),
        P(None, "tp", ("fsdp", "ctx")),
        P("fsdp", "ctx", "tp"),
    )
    out_specs = (
        P("fsdp", "ctx", "tp"),
        P("fsdp", "ctx", "tp"),
        P(("fsdp", "ctx"), "tp"),
        P(("fsdp", "ctx"), "tp"),
        P(("fsdp", "ctx"), "tp"),
        P("tp", ("fsdp", "ctx")),
        P(("fsdp", "ctx"), None),
        P(("fsdp", "ctx")),
        P(("fsdp", "ctx")),
        P(None, ("fsdp", "ctx"), "tp"),
        P(None, ("fsdp", "ctx"), "tp"),
        P(None, "tp", ("fsdp", "ctx")),
    )
    return jax.shard_map(
        per_device, mesh=mesh, in_specs=in_specs, out_specs=out_specs, check_vma=False
    )
```

```python
import functools

import jax
import jax.numpy as jnp
from jax import lax
from jax.experimental import pallas as pl
from jax.experimental.pallas import tpu as pltpu
from jax.sharding import PartitionSpec as P

HD = 64
TOP = 8
LANES = 128

EPSILON = 1e-06
ATTN_SCALE = 0.015625
RESIDUAL_SCALE = 0.22
MASKED_SCORE = -1e30
GATHERS = 2
CALLS = 2
RING = ("fsdp", "ctx")
BF = jnp.bfloat16
F32 = jnp.float32
VMEM_LIMIT = 24 * 1024 * 1024
MOE_VMEM = 56 * 1024 * 1024


def nt(a, b):
    return lax.dot_general(a, b, (((1,), (1,)), ((), ())), preferred_element_type=F32)


def nn(a, b):
    return lax.dot_general(a, b, (((1,), (0,)), ((), ())), preferred_element_type=F32)


def tn(a, b):
    return lax.dot_general(a, b, (((0,), (0,)), ((), ())), preferred_element_type=F32)


def params(*semantics):
    return pltpu.CompilerParams(
        dimension_semantics=semantics, vmem_limit_bytes=VMEM_LIMIT
    )


def whole(shape):
    zeros = (0,) * len(shape)
    return pl.BlockSpec(shape, lambda *_: zeros, pipeline_mode=pl.Buffered(1))


def swap_halves(slab):
    lane = lax.broadcasted_iota(jnp.int32, slab.shape, 1) % HD
    return jnp.where(
        lane < HD // 2, pltpu.roll(slab, LANES - HD // 2, 1), pltpu.roll(slab, HD // 2, 1)
    )


def column_as_row(ref, column):
    lane = lax.broadcasted_iota(jnp.int32, (16, ref.shape[1]), 1)
    return nt(jnp.where(lane == column, 1.0, 0.0).astype(BF), ref[...])[:1]


def pack_kernel(q_ref, k_ref, v_ref, out_ref, router_ref, one_ref, two_ref, packed_ref, *scratch):
    stage, sem = scratch
    rows, q_width = q_ref.shape
    copies, at = [], 0

    def copy(source, width):
        nonlocal at
        copies.append(pltpu.make_async_copy(source, packed_ref.at[0, :, pl.ds(at, width)], sem))
        copies[-1].start()
        at += width

    copy(q_ref, q_width)
    for pair in range(k_ref.shape[1] // LANES):
        cols = pl.ds(pair * LANES, LANES)
        copy(k_ref.at[:, cols], LANES)
        copy(v_ref.at[:, cols], LANES)
    copy(out_ref, q_width)
    experts = router_ref.shape[0]
    stage[...] = jnp.zeros(stage.shape, F32)
    stage[:experts, :rows] = router_ref[...].astype(F32)
    stage[experts : experts + 1, :rows] = one_ref[...].astype(F32)
    stage[experts + 1 : experts + 2, :rows] = two_ref[...].astype(F32)
    packed_ref[0, :, at:] = stage[...].T[:rows].astype(BF)
    for each in copies:
        each.wait()


def pack_experts_kernel(core_ref, gate_ref, up_ref, down_ref, mine_ref, other_ref, sem):
    count, _, cols = mine_ref.shape
    hid = cols // 3
    copies = []
    for out_ref, core in ((mine_ref, core_ref[0]), (other_ref, 1 - core_ref[0])):
        for i, source in enumerate((gate_ref, up_ref, down_ref)):
            copies.append(
                pltpu.make_async_copy(
                    source.at[pl.ds(core * count, count)],
                    out_ref.at[:, :, pl.ds(i * hid, hid)],
                    sem,
                )
            )
            copies[-1].start()
    for copy in copies:
        copy.wait()


def join_kernel(core_ref, mine_ref, other_ref, *groups):
    rows = mine_ref.shape[1]
    for mine_first in (True, False):

        @pl.when((core_ref[0] == 0) == mine_first)
        def _():
            at = 0
            for out_ref in groups:
                size = out_ref.shape[0]
                first, second = (mine_ref, other_ref) if mine_first else (other_ref, mine_ref)
                out_ref[:, :rows] = first[at : at + size]
                out_ref[:, rows:] = second[at : at + size]
                at += size


def assemble_kernel(places, where_ref, *refs):
    count = len(places)
    parts, outs, sem = refs[:count], refs[count:-1], refs[-1]

    def copies():
        for j, (_, _, rows) in enumerate(places):
            first = 0
            for out in outs:
                cols = out.shape[1]
                yield pltpu.make_async_copy(
                    parts[j].at[0, :, pl.ds(first, cols)],
                    out.at[pl.ds(pl.multiple_of(where_ref[j], 16), rows)],
                    sem,
                )
                first += cols

    for copy in copies():
        copy.start()
    for copy in copies():
        copy.wait()


def side_by_side(tp_ref, mine, other):
    first = tp_ref[0] == 0
    return jnp.concatenate([jnp.where(first, mine, other), jnp.where(first, other, mine)], axis=1)


def features_kernel(tp_ref, mine_ref, other_ref, full_ref):
    full_ref[...] = side_by_side(tp_ref, mine_ref[...], other_ref[...])


def project_kernel(
    pairs,
    q_width,
    gain_col,
    tp_ref,
    mine_ref,
    other_ref,
    small_ref,
    w_ref,
    cos_ref,
    sin_ref,
    x_ref,
    n_ref,
    q_ref,
    kv_ref,
):
    x_ref[...] = side_by_side(tp_ref, mine_ref[...], other_ref[...])
    x = x_ref[...].astype(F32)
    gain = column_as_row(small_ref, gain_col)
    scale = lax.rsqrt(jnp.mean(x * x, axis=1, keepdims=True) + EPSILON)
    normed = (x * scale * gain).astype(BF)
    n_ref[...] = normed
    cosine, sine = cos_ref[...], sin_ref[...]
    raw = nn(normed, w_ref[...])
    for slab in range(q_width // LANES):
        cols = slice(slab * LANES, (slab + 1) * LANES)
        part = raw[:, cols]
        turned = (part * cosine + swap_halves(part) * sine).astype(BF)
        q_ref[:, cols] = (turned.astype(F32) * ATTN_SCALE).astype(BF)
    for pair in range(pairs):
        lo = pair * 2 * LANES
        part = raw[:, q_width + lo : q_width + lo + LANES]
        kv_ref[:, lo : lo + LANES] = (part * cosine + swap_halves(part) * sine).astype(BF)
        kv_ref[:, lo + LANES : lo + 2 * LANES] = raw[
            :, q_width + lo + LANES : q_width + lo + 2 * LANES
        ].astype(BF)


def attend_kernel(blocks, span, prefix_ref, base_ref, q_ref, *refs):
    kv_refs = refs[:blocks]
    out_ref, p_ref = refs[blocks:]
    limit_len = prefix_ref[pl.program_id(0)]
    local = base_ref[0] + lax.broadcasted_iota(jnp.int32, (span, 1), 0)
    limit = jnp.maximum(local + 1, limit_len)
    key_pos = jnp.concatenate(
        [
            base_ref[j] + lax.broadcasted_iota(jnp.int32, (1, span), 1)
            for j in range(blocks)
        ],
        axis=1,
    )
    visible = key_pos < limit
    visible = jnp.concatenate([visible, visible], axis=0)
    for g in range(2):
        keys = jnp.concatenate([r[:, g * HD : (g + 1) * HD] for r in kv_refs], axis=0)
        vals = jnp.concatenate(
            [r[:, LANES + g * HD : LANES + (g + 1) * HD] for r in kv_refs], axis=0
        )
        first, second = 2 * g * HD, (2 * g + 1) * HD
        queries = jnp.concatenate(
            [q_ref[:, first : first + HD], q_ref[:, second : second + HD]], axis=0
        )
        scores = jnp.where(visible, nt(queries, keys), MASKED_SCORE)
        expo = jnp.exp(scores - jnp.max(scores, axis=1, keepdims=True))
        probs = (expo * (1.0 / jnp.sum(expo, axis=1, keepdims=True))).astype(BF)
        p_ref[0, g] = probs
        att = nn(probs, vals).astype(BF)
        out_ref[:, first : first + HD] = att[:span]
        out_ref[:, second : second + HD] = att[span:]


def attend_back_kernel(blocks, span, p_ref, q_ref, g_ref, cos_ref, sin_ref, *refs):
    kv_refs = refs[:blocks]
    dq_ref, own_ref, other_ref = refs[blocks:]
    cosine, sine = cos_ref[...], sin_ref[...]
    parts = []
    for g in range(2):
        keys = jnp.concatenate([r[:, g * HD : (g + 1) * HD] for r in kv_refs], axis=0)
        vals = jnp.concatenate(
            [r[:, LANES + g * HD : LANES + (g + 1) * HD] for r in kv_refs], axis=0
        )
        first, second = 2 * g * HD, (2 * g + 1) * HD
        queries = jnp.concatenate(
            [q_ref[:, first : first + HD], q_ref[:, second : second + HD]], axis=0
        )
        grads = jnp.concatenate(
            [g_ref[:, first : first + HD], g_ref[:, second : second + HD]], axis=0
        )
        probs = p_ref[0, g]
        wide = probs.astype(F32)
        grad_probs = nt(grads, vals)
        inner = jnp.sum(wide * grad_probs, axis=1, keepdims=True)
        grad_scores = (wide * (grad_probs - inner)).astype(BF)
        dq = nn(grad_scores, keys) * ATTN_SCALE
        slab = jnp.concatenate([dq[:span], dq[span:]], axis=1)
        turned = slab * cosine - swap_halves(slab) * sine
        dq_ref[:, first : first + LANES] = turned.astype(BF)
        parts.append((nn(queries.T, grad_scores), nn(grads.T, probs)))
    stacked = jnp.concatenate([parts[0][0], parts[1][0], parts[0][1], parts[1][1]], axis=0)
    turned = stacked.T.astype(BF)
    half = blocks // 2
    for j in range(half):
        own_ref[j] = turned[j * span : (j + 1) * span]
        other_ref[j] = turned[(half + j) * span : (half + j + 1) * span]


def middle_kernel(
    gain_col, a_ref, b_ref, wa_ref, wb_ref, x_ref, small_ref, routes_ref, m_ref, n_ref, g_ref
):
    branch = nt(a_ref[...], wa_ref[...]) + nt(b_ref[...], wb_ref[...])
    middle = x_ref[...].astype(F32) + RESIDUAL_SCALE * branch
    m_ref[...] = middle
    scale = lax.rsqrt(jnp.mean(middle * middle, axis=1, keepdims=True) + EPSILON)
    wide = middle * scale * column_as_row(small_ref, gain_col)
    normed = wide.astype(BF)
    width = normed.shape[1]
    n_ref[:, :width] = normed
    logits = nn(normed, small_ref[...])
    lane = lax.broadcasted_iota(jnp.int32, logits.shape, 1)
    routes = routes_ref[...]
    routed = lane == routes[:, 0:1]
    for k in range(1, TOP):
        routed = routed | (lane == routes[:, k : k + 1])
    logits = jnp.where(routed, logits, MASKED_SCORE)
    expo = jnp.where(routed, jnp.exp(logits - jnp.max(logits, axis=1, keepdims=True)), 0.0)
    gates = expo / jnp.sum(expo, axis=1, keepdims=True)
    g_ref[...] = gates
    n_ref[:, width:] = in_two(gates, gain_col - 1)


def in_two(pull, experts):
    high = pull.astype(BF).astype(F32)
    return (high + pltpu.roll(pull - high, experts, 1)).astype(BF)


def in_one(terms, experts):
    wide = terms.astype(F32)
    lane = lax.broadcasted_iota(jnp.int32, wide.shape, 1)
    both = wide + pltpu.roll(wide, LANES - experts, 1)
    return jnp.where(lane < experts, both, 0.0)


def moe_kernel(first_call, last_call, joins, experts, column, start, group, places, where_ref, *refs):
    count = len(places)
    w_parts, refs = refs[:count], refs[count:]
    sources, refs = refs[:4], refs[4:]
    inits, refs = ((), refs) if first_call else (refs[:2], refs[2:])
    refs = refs[count:] if joins else refs
    outs, mixed_out, dw_parts, refs = refs[:2], refs[2], refs[3 : 3 + count], refs[3 + count :]
    here, accs, refs = refs[:4], refs[4:6], refs[6:]
    mixed_all, narrow, w_all, dw_all, w_sem, dw_sem, near_sem, acc_sem, out_sem, mixed_sem = refs
    xa_ref, ya_ref, xb_ref, yb_ref = here
    rows, width = ya_ref.shape
    hid = w_all.shape[2] // 3

    def window(j):
        return pl.ds(pl.multiple_of(where_ref[1 + j], 16), places[j][2])

    def load(e, j):
        return pltpu.make_async_copy(
            w_parts[j].at[start + e], w_all.at[e, window(j)], w_sem.at[e]
        )

    def store(e, j):
        return pltpu.make_async_copy(
            dw_all.at[e % 2, window(j)], dw_parts[j].at[start + e], dw_sem.at[e % 2]
        )

    nears = [
        pltpu.make_async_copy(a, b, near_sem.at[i]) for i, (a, b) in enumerate(zip(sources, here))
    ]
    fetches = [
        pltpu.make_async_copy(a, b, acc_sem.at[i]) for i, (a, b) in enumerate(zip(inits, accs))
    ]
    mixed_store = pltpu.make_async_copy(mixed_all, mixed_out, mixed_sem)
    for j in range(count):
        load(0, j).start()
    for copy in nears[:2]:
        copy.start()
    results = []
    for e in range(group):
        for j in range(count):
            load(e, j).wait()
        if e == 0:
            for copy in nears[:2]:
                copy.wait()
            for copy in [*fetches[:1], *nears[2:], *fetches[1:]]:
                copy.start()
        expert = where_ref[0] + column + e
        w_gu, w_d = w_all[e, :, : 2 * hid], w_all[e, :, 2 * hid :]
        kept = []
        for side, (x_ref, y_ref) in enumerate(((xa_ref, ya_ref), (xb_ref, yb_ref))):
            acc = accs[side]
            if e == 0 and side == 1:
                for copy in nears[2:]:
                    copy.wait()
                for other in range(1, group):
                    for j in range(count):
                        load(other, j).start()
            pre = nn(x_ref[:, :width], w_gu)
            back = nn(y_ref[...], w_d)
            gates = in_one(x_ref[:, width:], experts)
            lane = lax.broadcasted_iota(jnp.int32, gates.shape, 1)
            mask = lane == expert
            weight = RESIDUAL_SCALE * jnp.sum(
                jnp.where(mask, gates, 0.0), axis=1, keepdims=True
            )
            gate_pre, up_pre = pre[:, :hid], pre[:, hid:]
            sig = jax.nn.sigmoid(gate_pre)
            act = gate_pre * sig
            hidden = act * up_pre
            pull = RESIDUAL_SCALE * jnp.sum(back * hidden, axis=1, keepdims=True)
            scaled = weight * back
            d_up = scaled * act
            d_gate = scaled * up_pre * (sig + act * (1.0 - sig))
            d_gu = jnp.concatenate([d_gate.astype(BF), d_up.astype(BF)], axis=1)
            mixed = (weight * hidden).astype(BF)
            mixed_all[e, side * rows : (side + 1) * rows] = mixed
            if first_call and e == 0:
                acc[:, :width] = nt(d_gu, w_gu)
                acc[:, width:] = jnp.where(mask, pull, 0.0)
            else:
                if e == 0:
                    fetches[side].wait()
                acc[:, :width] += nt(d_gu, w_gu)
                acc[:, width:] += jnp.where(mask, pull, 0.0)
            kept.append((d_gu, mixed))
            if e == group - 1:
                if last_call and side:
                    narrow[:, :width] = acc[:, :width].astype(BF)
                    narrow[:, width:] = in_two(acc[:, width:], experts)
                    acc = narrow
                results.append(pltpu.make_async_copy(acc, outs[side], out_sem.at[side]))
                results[-1].start()
        if e == group - 1:
            mixed_store.start()
        dw_gu = tn(xa_ref[:, :width], kept[0][0]) + tn(xb_ref[:, :width], kept[1][0])
        dw_d = tn(ya_ref[...], kept[0][1]) + tn(yb_ref[...], kept[1][1])
        if e >= 2:
            for j in range(count):
                store(e - 2, j).wait()
        dw_all[e % 2, :, : 2 * hid] = dw_gu.astype(BF)
        dw_all[e % 2, :, 2 * hid :] = dw_d.astype(BF)
        for j in range(count):
            store(e, j).start()
    for e in range(max(0, group - 2), group):
        for j in range(count):
            store(e, j).wait()
    for copy in results:
        copy.wait()
    mixed_store.wait()


def moe_sum_kernel(places, sets, calls, group, where_ref, *refs):
    count = len(places)
    w_sets = [refs[k * count : (k + 1) * count] for k in range(sets)]
    refs = refs[sets * count :]
    mixed_parts, refs = refs[:calls], refs[calls:]
    own_ref, peer_ref, w_all, mixed_all, w_sem, mixed_sem = refs
    rows = own_ref.shape[0]
    size = calls * group // sets
    hid = w_all.shape[2] // size

    def loads(k):
        for i in range(size):
            cols = pl.ds(i * hid, hid)
            for j in range(count):
                yield pltpu.make_async_copy(
                    w_sets[k][j].at[i, :, pl.ds(2 * hid, hid)],
                    w_all.at[k, pl.ds(pl.multiple_of(where_ref[1 + j], 16), places[j][2]), cols],
                    w_sem.at[k],
                )
            e = k * size + i
            yield pltpu.make_async_copy(
                mixed_parts[e // group].at[e % group], mixed_all.at[k, :, cols], mixed_sem.at[k]
            )

    for k in range(sets):
        for copy in loads(k):
            copy.start()
    total = None
    for k in range(sets):
        for copy in loads(k):
            copy.wait()
        term = nt(mixed_all[k], w_all[k])
        total = term if total is None else total + term
    own_ref[...] = total[:rows]
    peer_ref[...] = total[rows:].astype(BF)


def weight_grad_kernel(counts, gain_at, core_ref, *refs):
    sides = []
    for size in counts:
        sides.append(jnp.concatenate([ref[...] for ref in refs[:size]], axis=0))
        refs = refs[size:]
    gain_refs, (kept_ref, sent_ref) = refs[:-2], refs[-2:]
    n, shard, _ = kept_ref.shape
    width = 2 * n * shard
    terms = [tn(left[:, :width], right) for left, right in zip(sides[::2], sides[1::2])]
    if gain_refs:
        if terms[-1].shape[1] != LANES:
            terms.append(jnp.zeros((width, LANES), F32))
        row = lax.broadcasted_iota(jnp.int32, (8, LANES), 0)
        lane = lax.broadcasted_iota(jnp.int32, (8, LANES), 1)
        place = jnp.where((row == 0) & (lane == gain_at), 1.0, 0.0)
        gain = sum(ref[...] for ref in gain_refs)
        terms[-1] = terms[-1] + tn(jnp.broadcast_to(gain, (8, width)), place)
    first = 0
    for term in terms:
        cols = term.shape[1]
        parts = term.astype(BF).reshape(n, 2, shard, cols)
        for mine in range(2):

            @pl.when(core_ref[0] == mine)
            def _():
                kept_ref[:, :, first : first + cols] = parts[:, mine]
                sent_ref[:, :, first : first + cols] = parts[:, 1 - mine]

        first += cols


def order_kernel(places, chips_ref, *refs):
    count = len(places)
    pairs, parts = refs[:-count], refs[-count:]
    for j, (_, row, rows) in enumerate(places):
        chip = chips_ref[j]
        window = pl.ds(row, rows)
        first = 0
        for kept_ref, other_ref in zip(pairs[::2], pairs[1::2]):
            cols = kept_ref.shape[2]
            parts[j][0, :, first : first + cols] = kept_ref[chip, window] + other_ref[chip, window]
            first += cols


def add_terms_kernel(experts, own_ref, peer_ref, sum_ref):
    width = own_ref.shape[1] - LANES
    total = own_ref[:, :width] + peer_ref[:, :width].astype(F32)
    sum_ref[:, :width] = total.astype(BF)
    pull = own_ref[:, width:] + in_one(peer_ref[:, width:], experts)
    sum_ref[:, width:] = in_two(pull, experts)


def close_experts_kernel(core_ref, own_ref, ahead_ref, back_ref, kept_ref, sent_ref):
    rows = kept_ref.shape[1]
    total = own_ref[...].astype(F32) + ahead_ref[...].astype(F32) + back_ref[...].astype(F32)
    is_first = core_ref[0] == 0
    kept_ref[...] = jnp.where(is_first, total[:, :rows], total[:, rows:])
    sent_ref[...] = jnp.where(is_first, total[:, rows:], total[:, :rows]).astype(BF)


def expert_grads_kernel(chains, core_ref, *refs):
    kept_refs, sent_refs, outs = refs[:chains], refs[chains : 2 * chains], refs[2 * chains :]
    count, _, cols = kept_refs[0].shape
    hid = cols // 3
    for k in range(chains):
        for ref, core in ((kept_refs[k], core_ref[0]), (sent_refs[k], 1 - core_ref[0])):
            for i in range(count):
                at = core * chains * count + k * count + i
                for part, out in enumerate(outs):
                    out[at] = ref[i, :, part * hid : (part + 1) * hid].astype(F32)


def close_weights_kernel(widths, own_ref, ahead_ref, back_ref, *outs):
    def total(cols):
        return (
            own_ref[0, :, cols].astype(F32)
            + ahead_ref[0, :, cols].astype(F32)
            + back_ref[0, :, cols].astype(F32)
        )

    first = 0
    for kind, width in widths:
        if kind == "pairs":
            for pair in range(width // (2 * LANES)):
                for side in range(2):
                    lo = first + (2 * pair + side) * LANES
                    outs[side][:, pair * LANES : (pair + 1) * LANES] = total(slice(lo, lo + LANES))
            outs = outs[2:]
        else:
            outs[0][...] = total(slice(first, first + width))
            outs = outs[1:]
        first += width


def token_grads_kernel(x_ref, own_ref, dot_ref, other_ref, middle_ref, out_ref):
    feature = x_ref.shape[1]
    other = other_ref[...]
    dot = dot_ref[:, :1] + in_one(other[:, feature:], 1)[:, :1]
    total = middle_ref[...] + own_ref[...] + other[:, :feature].astype(F32)
    out_ref[...] = total - x_ref[...].astype(F32) * dot


def middle_back_kernel(
    gain_col,
    tp_ref,
    sa_ref,
    sb_ref,
    gates_ref,
    m_ref,
    y_ref,
    small_ref,
    wo_ref,
    gm_ref,
    branch_ref,
    att_ref,
    logit_ref,
    dgain_ref,
):
    @pl.when(pl.program_id(0) == 0)
    def _():
        dgain_ref[...] = jnp.zeros(dgain_ref.shape, F32)

    gates = gates_ref[...]
    width = m_ref.shape[1]
    pull = in_one(sa_ref[:, width:], gain_col - 1) + in_one(sb_ref[:, width:], gain_col - 1)
    weighted = gates * pull
    grad_logits = (weighted - gates * jnp.sum(weighted, axis=1, keepdims=True)).astype(BF)
    logit_ref[...] = grad_logits
    grad = sa_ref[:, :width].astype(F32) + sb_ref[:, :width].astype(F32)
    grad = grad + nt(grad_logits, small_ref[...])
    middle = m_ref[...]
    scale = lax.rsqrt(jnp.mean(middle * middle, axis=1, keepdims=True) + EPSILON)
    unit = middle * scale
    dgain_ref[...] += jnp.sum(grad * unit, axis=0, keepdims=True)
    scaled = grad * column_as_row(small_ref, gain_col)
    inner = jnp.sum(scaled * unit, axis=1, keepdims=True) * (1.0 / width)
    grad_middle = y_ref[...].astype(F32) + scale * (scaled - unit * inner)
    half = width // 2
    gm_ref[...] = jnp.where(tp_ref[0] == 0, grad_middle[:, :half], grad_middle[:, half:])
    branch = (RESIDUAL_SCALE * grad_middle).astype(BF)
    branch_ref[...] = branch
    att_ref[...] = nn(branch, wo_ref[...]).astype(BF)


def project_back_kernel(pairs, gain_col, seqs, tp_ref, *refs):
    dq_ref, kva_ref, kvb_ref, kvc_ref, cos_ref, sin_ref, w_ref, x_ref, small_ref = refs[:9]
    d_ref, own_ref, other_ref, dot_ref, dgain_ref = refs[9:]
    gain = column_as_row(small_ref, gain_col)
    is_first = tp_ref[0] == 0
    rows, q_width = dq_ref.shape
    span = rows // seqs
    for s in range(seqs):
        at = slice(s * span, (s + 1) * span)
        cosine, sine = cos_ref[at], sin_ref[at]
        kv = kva_ref[0, at].astype(F32) + kvb_ref[0, at].astype(F32) + kvc_ref[at].astype(F32)
        for pair in range(pairs):
            lo = pair * 2 * LANES
            part = kv[:, lo : lo + LANES]
            d_ref[at, lo : lo + LANES] = (part * cosine - swap_halves(part) * sine).astype(BF)
            d_ref[at, lo + LANES : lo + 2 * LANES] = kv[:, lo + LANES : lo + 2 * LANES].astype(BF)
        grad = nt(dq_ref[at], w_ref[:, :q_width]) + nt(d_ref[at], w_ref[:, q_width:])
        x = x_ref[at].astype(F32)
        width = x.shape[1]
        scale = lax.rsqrt(jnp.mean(x * x, axis=1, keepdims=True) + EPSILON)
        unit = x * scale
        term = jnp.sum(grad * unit, axis=0, keepdims=True)
        if s == 0:
            dgain_ref[...] = term
        else:
            dgain_ref[...] += term
        scaled = grad * gain
        inner = jnp.sum(scaled * unit, axis=1, keepdims=True) * (1.0 / width) * scale * scale
        lane = lax.broadcasted_iota(jnp.int32, (span, LANES), 1)
        dot = jnp.where(lane == 0, inner, 0.0)
        dot_ref[at] = dot
        scaled = scaled * scale
        half = width // 2
        own_ref[at] = jnp.where(is_first, scaled[:, :half], scaled[:, half:])
        other_ref[at, :half] = jnp.where(is_first, scaled[:, half:], scaled[:, :half]).astype(BF)
        other_ref[at, half:] = in_two(dot, 1)


class Ring:
    def __init__(self, wide, ctx):
        self.wide, self.ctx, self.deep = wide, ctx, ctx // 2
        self.size = wide * self.deep
        deep = self.deep
        order = [
            (f, y)
            for y in range(deep)
            for f in (range(wide) if y % 2 == 0 else range(wide - 1, -1, -1))
        ]
        flat = [[f * ctx + y * 2 + c for f, y in order] for c in range(2)]
        n = self.size
        self.forward = [(row[i], row[(i + 1) % n]) for row in flat for i in range(n)]
        self.backward = [(b, a) for a, b in self.forward]
        f, c = lax.axis_index("fsdp"), lax.axis_index("ctx")
        y = c // 2
        self.place = y * wide + jnp.where(y % 2 == 0, f, wide - 1 - f)

    def chip(self, offset):
        place = (self.place + offset) % self.size
        y, q = place // self.wide, place % self.wide
        f = jnp.where(y % 2 == 0, q, self.wide - 1 - q)
        return f * self.deep + y

    def send(self, array, forward=True):
        return lax.ppermute(array, RING, self.forward if forward else self.backward)

    def places(self, rows):
        far, half = self.size // 2, rows // 2
        found = [(0, 0, rows)]
        for step in range(1, far):
            found += [(-step, 0, rows), (step, 0, rows)]
        if half % 16:
            return found + [(-far, 0, rows)]
        return found + [(-far, 0, half), (far, half, half)]


class Gather:
    def __init__(self, ring, block, name):
        self.ring, self.step, self.rows, self.name = ring, 0, block.shape[1], name
        self.moving = (block, block)
        self.parts = [block]

    def prepare(self):
        if self.step == self.ring.size // 2 - 1:
            half = self.rows // 2
            ahead, back = self.moving
            self.moving = (ahead[:, :half], back[:, half:]) if half % 16 == 0 else (ahead,)

    def send(self):
        self.step += 1
        with jax.named_scope(f"{self.name}_step_{self.step}"):
            self.moving = tuple(
                self.ring.send(array, i == 0) for i, array in enumerate(self.moving)
            )
        self.parts += self.moving

    def done(self):
        return self.step == self.ring.size // 2


class Scatter:
    def __init__(self, ring, parts, name):
        self.ring, self.parts, self.step, self.name = ring, parts, 0, name
        self.far = ring.size // 2
        self.halved = len(parts) == ring.size + 1
        self.moving = (parts[-2], parts[-1]) if self.halved else (parts[-1],)

    def prepare(self):
        if self.step:
            s = self.far - self.step
            self.moving = add_pair(self.parts[2 * s], self.parts[2 * s - 1], *self.moving)

    def send(self):
        self.step += 1
        with jax.named_scope(f"{self.name}_step_{self.step}"):
            self.moving = tuple(
                self.ring.send(array, i == 0) for i, array in enumerate(self.moving)
            )

    def done(self):
        return self.step == self.far


def add_pair_kernel(near_ref, behind_ref, *refs):
    moved, outs = refs[:-2], refs[-2:]
    rows = near_ref.shape[1]
    for i, (mine, out) in enumerate(zip((near_ref, behind_ref), outs)):
        if i >= len(moved):
            out[...] = mine[...]
            continue
        came = moved[i]
        size = came.shape[1]
        at = slice(0, size) if i == 0 else slice(rows - size, rows)
        total = (mine[:, at].astype(F32) + came[...].astype(F32)).astype(BF)
        if size == rows:
            out[...] = total
        else:
            rest = slice(size, rows) if i == 0 else slice(0, rows - size)
            out[:, at] = total
            out[:, rest] = mine[:, rest]


def add_pair(near, behind, *moved):
    def spec(array):
        return pl.BlockSpec((1,) + array.shape[1:], lambda i: (i, 0, 0))

    arrays = (near, behind, *moved)
    out = jax.ShapeDtypeStruct(near.shape, BF)
    return pl.pallas_call(
        add_pair_kernel,
        grid=(near.shape[0],),
        in_specs=[spec(array) for array in arrays],
        out_specs=[spec(near)] * 2,
        out_shape=[out] * 2,
        compiler_params=params("arbitrary"),
        name="add_pair",
    )(*arrays)


def pinned(call):
    def run(*args):
        return call(
            *[
                pltpu.with_memory_space_constraint(a, pltpu.HBM)
                if a.ndim > 1 and a.dtype != jnp.int32
                else a
                for a in args
            ]
        )

    return run


def lock(*values):
    return lax.optimization_barrier(values)


def per_device(
    tokens,
    prefix,
    routes,
    w_query,
    w_key,
    w_value,
    w_out,
    w_router,
    gain_attn,
    gain_ffn,
    w_gate,
    w_up,
    w_down,
    cotangent,
):
    wide, ctx = lax.axis_size("fsdp"), lax.axis_size("ctx")
    seqs, span, feature = tokens.shape
    rows = seqs * span
    width = 2 * feature
    shard = w_query.shape[0]
    experts = w_router.shape[1]
    per_core = experts // 2
    hid = w_gate.shape[2]
    q_width, kv_width = w_query.shape[1], w_key.shape[1]
    pairs = kv_width // LANES
    deep = ctx // 2
    tp, c = lax.axis_index("tp"), lax.axis_index("ctx")
    core, y = c % 2, c // 2
    ring = Ring(wide, ctx)
    n = ring.size
    core_perm = [(i, i ^ 1) for i in range(ctx)]

    def swap_core(array, name="rows"):
        with jax.named_scope(f"{name}_over_core"):
            return lax.ppermute(array, "ctx", core_perm)

    def swap_tp(array, name="rows"):
        with jax.named_scope(f"{name}_over_tp"):
            return lax.ppermute(array, "tp", [(0, 1), (1, 0)])

    up_y = [(i, (i + 2) % ctx) for i in range(ctx)]
    down_y = [(i, (i - 2) % ctx) for i in range(ctx)]

    def shift_y(array, perm, name):
        with jax.named_scope(f"{name}_over_y"):
            return lax.ppermute(array, "ctx", perm)

    tp_scalar = tp.astype(jnp.int32).reshape(1)

    def by_core(mine, other, axis):
        return jnp.where(
            core == 0,
            jnp.concatenate([mine, other], axis),
            jnp.concatenate([other, mine], axis),
        )

    vmem = pl.BlockSpec(memory_space=pltpu.VMEM)
    smem = pl.BlockSpec(memory_space=pltpu.SMEM)
    any_spec = pl.BlockSpec(memory_space=pl.ANY)
    qkv_width = q_width + 2 * kv_width
    in_hbm = lambda array: pltpu.with_memory_space_constraint(array, pltpu.HBM)
    small_rows = max(shard, LANES)
    bundle = pl.pallas_call(
        pack_kernel,
        in_specs=[any_spec] * 4 + [vmem] * 3,
        out_specs=vmem,
        out_shape=jax.ShapeDtypeStruct((1, shard, qkv_width + q_width + LANES), BF),
        scratch_shapes=[pltpu.VMEM((LANES, small_rows), F32), pltpu.SemaphoreType.DMA(())],
        compiler_params=params(),
        name="pack",
    )(
        *[in_hbm(w) for w in (w_query, w_key, w_value, w_out.T)],
        w_router.T,
        gain_attn[None],
        gain_ffn[None],
    )
    own_tokens = tokens.reshape(rows, feature)
    own_cot = cotangent.reshape(rows, feature)
    core_scalar = core.astype(jnp.int32).reshape(1)
    def segment(ticks, *values):
        chains = [chain for chain in ticks if not chain.done()]

        values = together(chains, *values)
        if any(chain.step for chain in chains):
            for chain in chains:
                chain.prepare()
            values = together(chains, *values)
        for chain in chains:
            chain.send()
        return values

    def together(chains, *values):
        held = [array for chain in chains for array in chain.moving]
        out = lock(*held, *values)
        at = 0
        for chain in chains:
            size = len(chain.moving)
            chain.moving = tuple(out[at : at + size])
            at += size
        return out[at:]

    def arrive(chain, *values):
        return together([chain], *values)

    first = Gather(ring, bundle, "bundle")
    half_shape = jax.ShapeDtypeStruct((per_core, shard, 3 * hid), BF)
    *raw_w, own_tokens, bundle = segment(
        [first], w_gate, w_up, w_down.transpose(0, 2, 1), own_tokens, bundle
    )
    mine_w, other_w = pl.pallas_call(
        pack_experts_kernel,
        in_specs=[smem] + [any_spec] * 3,
        out_specs=[vmem] * 2,
        out_shape=[half_shape] * 2,
        scratch_shapes=[pltpu.SemaphoreType.DMA(())],
        compiler_params=params(),
        name="pack_experts",
    )(core_scalar, *[in_hbm(w) for w in raw_w])
    from_core = [swap_core(bundle, "bundle")]
    other_w = swap_core(other_w, "experts")
    from_core[0], other_w, mine_w = segment([first], from_core[0], other_w, mine_w)
    blocks_w = list(
        pl.pallas_call(
            join_kernel,
            in_specs=[smem] + [vmem] * 2,
            out_specs=[vmem] * GATHERS,
            out_shape=[
                jax.ShapeDtypeStruct((per_core // GATHERS, 2 * shard, 3 * hid), BF)
            ]
            * GATHERS,
            compiler_params=params(),
            name="join",
        )(core_scalar, mine_w, other_w)
    )
    half_width = HD // 2
    freqs = 10000.0 ** (-jnp.arange(half_width, dtype=F32) / half_width)
    local_pos = c * span + jnp.arange(span, dtype=jnp.int32)
    angles = local_pos.astype(F32)[:, None] * freqs[None, :]
    cosine, sine = jnp.cos(angles), jnp.sin(angles)
    cosine = jnp.tile(jnp.concatenate([cosine] * 4, axis=1), (seqs, 1))
    sine = jnp.tile(jnp.concatenate([-sine, sine, -sine, sine], axis=1), (seqs, 1))
    chips = [ring.chip(d) for d, _, _ in ring.places(shard)]
    chip_list = jnp.stack(chips).astype(jnp.int32)
    bundle_places = ring.places(shard)
    bundle_rows = [
        (chips[j] * 2 + side) * shard + row
        for side in (core, 1 - core)
        for j, (_, row, _) in enumerate(bundle_places)
    ]
    bundle_where = jnp.stack(bundle_rows).astype(jnp.int32)
    places = ring.places(2 * shard)
    part_rows = [ring.chip(d) * 2 * shard + row for d, row, _ in places]
    part_where = jnp.stack([core * per_core] + part_rows).astype(jnp.int32)
    base = jnp.stack(
        [(((y - k) % deep) * 2 + core) * span for k in range(deep)]
        + [(((y - k) % deep) * 2 + 1 - core) * span for k in range(deep)]
    ).astype(jnp.int32)
    other_tokens = swap_tp(own_tokens, "tokens")
    shared = 1
    while not first.done():
        fresh = [swap_core(part, "part") for part in first.parts[shared : first.step * 2 - 1]]
        shared += len(fresh)
        last_step = first.step == ring.size // 2 - 1
        *fresh, blocks_w[0], cosine, sine, chip_list, bundle_where, part_where, base, tokens_here = segment(
            [first],
            *fresh,
            blocks_w[0],
            cosine,
            sine,
            chip_list,
            bundle_where,
            part_where,
            base,
            other_tokens if last_step else own_tokens,
        )
        if last_step:
            other_tokens = tokens_here
        from_core += fresh
    weights = [Gather(ring, block, f"weights_{i}") for i, block in enumerate(blocks_w)]
    rest = [swap_core(part, "part") for part in first.parts[shared:-2]]
    other_cot = swap_tp(own_cot, "cotangent")
    *rest, other_cot, weights[0].moving = arrive(
        first, *rest, other_cot, weights[0].moving[0]
    )
    weights[0].moving = (weights[0].moving,) * 2
    weights[0].send()
    from_core += rest
    rest = [swap_core(part, "part") for part in first.parts[shared + len(rest) :]]
    from_core += rest
    w_qkv, wo_mine, w_small = pl.pallas_call(
        functools.partial(assemble_kernel, bundle_places * 2),
        in_specs=[smem] + [any_spec] * len(bundle_rows),
        out_specs=[vmem] * 3,
        out_shape=[
            jax.ShapeDtypeStruct((width, w), BF) for w in (qkv_width, q_width, LANES)
        ],
        scratch_shapes=[pltpu.SemaphoreType.DMA(())],
        compiler_params=params(),
        name="assemble",
    )(
        bundle_where,
        *[in_hbm(part) for part in first.parts + from_core],
    )
    step_rows = min(rows, 256)
    steps = rows // step_rows
    row_spec = lambda cols: pl.BlockSpec((step_rows, cols), lambda i, *_: (i, 0))
    full_tokens, normed, queries, kv = (pl.pallas_call(
        functools.partial(project_kernel, pairs, q_width, experts),
        grid=(steps,),
        in_specs=[
            smem,
            row_spec(feature),
            row_spec(feature),
            whole((width, LANES)),
            whole((width, qkv_width)),
            row_spec(LANES),
            row_spec(LANES),
        ],
        out_specs=[row_spec(width), row_spec(width), row_spec(q_width), row_spec(2 * kv_width)],
        out_shape=[
            pltpu.HBM((rows, width), BF),
            pltpu.HBM((rows, width), BF),
            jax.ShapeDtypeStruct((rows, q_width), BF),
            jax.ShapeDtypeStruct((rows, 2 * kv_width), BF),
        ],
        compiler_params=params("arbitrary"),
        name="project",
    ))(tp_scalar, own_tokens, other_tokens, w_small, w_qkv, cosine, sine)

    own_side = [kv]
    for _ in range(deep - 1):
        own_side.append(shift_y(own_side[-1], up_y, "kv"))
    other_side = [swap_core(kv, "kv")]
    wo_other = swap_tp(wo_mine, "w_out")
    length = ctx * span

    queries, *own_side = segment(weights[:1], queries, *own_side)
    other_side += [swap_core(block, "kv") for block in own_side[1:]]
    kv_blocks = own_side + other_side
    head_spec = lambda: pl.BlockSpec((span, 2 * LANES), lambda s, p, *_: (s, p))
    prob_spec = pl.BlockSpec((1, 2, 2 * span, length), lambda s, p, *_: (s, p, 0, 0))
    attended, probs = (pl.pallas_call(
        functools.partial(attend_kernel, ctx, span),
        grid_spec=pltpu.PrefetchScalarGridSpec(
            num_scalar_prefetch=2,
            grid=(seqs, pairs),
            in_specs=[head_spec()] * (1 + ctx),
            out_specs=[head_spec(), prob_spec],
        ),
        out_shape=[
            jax.ShapeDtypeStruct((rows, q_width), BF),
            pltpu.HBM((seqs, 2 * pairs, 2 * span, length), BF),
        ],
        compiler_params=params("arbitrary", "arbitrary"),
        name="attend",
    ))(prefix, base, queries, *kv_blocks)

    attended, wo_other = segment(weights[:1], attended, wo_other)
    for _ in range(ring.size // 2 - 4):
        (attended,) = segment(weights[:1], attended)

    attended_other = swap_tp(attended, "attended")
    full_cot = (pl.pallas_call(
            features_kernel,
            in_specs=[smem] + [vmem] * 2,
            out_specs=vmem,
            out_shape=pltpu.HBM((rows, width), BF),
            compiler_params=params(),
            name="features",
        )
    )(tp_scalar, own_cot, other_cot)
    peer_cot = swap_core(full_cot, "full_cot")
    (attended_other,) = segment(weights[:1], attended_other)
    route_rows = routes.reshape(rows, TOP)
    middle, normed_two, gates = (pinned(pl.pallas_call(
        functools.partial(middle_kernel, experts + 1),
        grid=(steps,),
        in_specs=[
            row_spec(q_width),
            row_spec(q_width),
            whole((width, q_width)),
            whole((width, q_width)),
            row_spec(width),
            whole((width, LANES)),
            row_spec(TOP),
        ],
        out_specs=[
            row_spec(width),
            row_spec(width + LANES),
            row_spec(LANES),
        ],
        out_shape=[
            pltpu.HBM((rows, width), F32),
            pltpu.HBM((rows, width + LANES), BF),
            pltpu.HBM((rows, LANES), F32),
        ],
        compiler_params=params("arbitrary"),
        name="middle",
    )))(attended, attended_other, wo_mine, wo_other, full_tokens, w_small, route_rows)
    normed_two, peer_cot = arrive(weights[0], normed_two, peer_cot)
    (normed_two,) = segment(weights[1:], normed_two)
    peer_two = swap_core(normed_two, "normed_two")

    near = [(normed_two, BF), (full_cot, BF), (peer_two, BF), (peer_cot, BF)]
    sources = [in_hbm(array) for array, _ in near]
    wide_acc, acc_shape = (rows, width), (rows, width + LANES)
    count = len(places)
    calls = GATHERS * CALLS
    call_size = per_core // calls

    def run_experts(call, accs, dw_parts):
        lead = 1 + count + 4 + len(accs)
        first_call, last_call = call == 0, call == calls - 1
        outs = pl.pallas_call(
            functools.partial(
                moe_kernel,
                first_call,
                last_call,
                bool(dw_parts),
                experts,
                call * call_size,
                call % CALLS * call_size,
                call_size,
                places,
            ),
            in_specs=[smem] + [any_spec] * (lead - 1 + len(dw_parts)),
            out_specs=[any_spec] * (3 + count),
            out_shape=[
                pltpu.HBM(acc_shape, F32),
                pltpu.HBM(acc_shape, BF if last_call else F32),
                pltpu.HBM((call_size, 2 * rows, hid), BF),
            ]
            + [pltpu.HBM((call_size * CALLS, r, 3 * hid), BF) for _, _, r in places],
            input_output_aliases={lead + j: 3 + j for j in range(len(dw_parts))},
            scratch_shapes=[pltpu.VMEM(array.shape, kind) for array, kind in near]
            + [pltpu.VMEM(acc_shape, F32)] * 2
            + [
                pltpu.VMEM((call_size, 2 * rows, hid), BF),
                pltpu.VMEM(acc_shape, BF),
                pltpu.VMEM((call_size, width, 3 * hid), BF),
                pltpu.VMEM((2, width, 3 * hid), BF),
                pltpu.SemaphoreType.DMA((call_size,)),
                pltpu.SemaphoreType.DMA((2,)),
                pltpu.SemaphoreType.DMA((4,)),
                pltpu.SemaphoreType.DMA((2,)),
                pltpu.SemaphoreType.DMA((2,)),
                pltpu.SemaphoreType.DMA(()),
            ],
            compiler_params=pltpu.CompilerParams(vmem_limit_bytes=MOE_VMEM),
            name="experts",
        )(
            part_where,
            *[in_hbm(block) for block in weights[call // CALLS].parts],
            *sources,
            *accs,
            *dw_parts,
        )
        return outs[:2], outs[2], outs[3:]

    accs, mixed_parts, sums = (), [], []

    for g in range(GATHERS):
        dw_parts = ()
        if g:
            while not weights[g].done():
                accs = segment(weights[g : g + 1], *accs)
            accs = arrive(weights[g], *accs)
        for call in range(g * CALLS, (g + 1) * CALLS):
            if call:
                accs = segment([*weights[g + 1 : g + 2], *sums][:1], *accs)
            accs, mixed, dw_parts = run_experts(call, accs, dw_parts)
            mixed_parts.append(mixed)
        sums.append(Scatter(ring, dw_parts, f"sums_{g}"))

    grad_two, grad_two_peer = arrive(sums[0], *accs)
    sums[0].prepare()
    part = pl.pallas_call(
        functools.partial(add_terms_kernel, experts),
        in_specs=[vmem] * 2,
        out_specs=vmem,
        out_shape=jax.ShapeDtypeStruct(acc_shape, BF),
        compiler_params=params(),
        name="add_terms",
    )(grad_two, swap_core(grad_two_peer, "grad_two"))
    (part,) = together(sums[:1], part)
    part_other = swap_tp(part, "part")
    sums[0].send()

    moe, moe_peer = pl.pallas_call(
        functools.partial(moe_sum_kernel, places, GATHERS, calls, call_size),
        in_specs=[smem] + [any_spec] * (count * GATHERS + calls),
        out_specs=[vmem] * 2,
        out_shape=[pltpu.HBM(wide_acc, F32), pltpu.HBM(wide_acc, BF)],
        scratch_shapes=[
            pltpu.VMEM((GATHERS, width, per_core // GATHERS * hid), BF),
            pltpu.VMEM((GATHERS, 2 * rows, per_core // GATHERS * hid), BF),
            pltpu.SemaphoreType.DMA((GATHERS,)),
            pltpu.SemaphoreType.DMA((GATHERS,)),
        ],
        compiler_params=pltpu.CompilerParams(vmem_limit_bytes=MOE_VMEM),
        name="experts_output",
    )(
        part_where,
        *[in_hbm(block) for chain in weights for block in chain.parts],
        *lock(*[in_hbm(mixed) for mixed in mixed_parts], part)[:calls],
    )

    moe, moe_peer = segment(sums[:1], moe, moe_peer)
    from_core_moe = swap_core(moe_peer, "moe")

    grad_middle, grad_branch, grad_attended, grad_logits, gain_two_term = pl.pallas_call(
        functools.partial(middle_back_kernel, experts + 1),
        grid=(steps,),
        in_specs=[
            smem,
            row_spec(width + LANES),
            row_spec(width + LANES),
            row_spec(LANES),
            row_spec(width),
            row_spec(width),
            whole((width, LANES)),
            whole((width, q_width)),
        ],
        out_specs=[
            row_spec(feature),
            row_spec(width),
            row_spec(q_width),
            row_spec(LANES),
            whole((1, width)),
        ],
        out_shape=[
            pltpu.HBM((rows, feature), F32),
            jax.ShapeDtypeStruct((rows, width), BF),
            jax.ShapeDtypeStruct((rows, q_width), BF),
            jax.ShapeDtypeStruct((rows, LANES), BF),
            jax.ShapeDtypeStruct((1, width), F32),
        ],
        compiler_params=params("arbitrary"),
        name="middle_back",
    )(tp_scalar, part, part_other, gates, middle, full_cot, w_small, wo_mine)
    back_spec = pl.BlockSpec((deep, span, 2 * LANES), lambda s, p: (0, s, p))
    turn_spec = pl.BlockSpec((span, LANES), lambda s, p: (s, 0))
    grad_q, grad_kv_own, grad_kv_peer = pl.pallas_call(
        functools.partial(attend_back_kernel, ctx, span),
        grid=(seqs, pairs),
        in_specs=[prob_spec] + [head_spec()] * 2 + [turn_spec] * 2 + [head_spec()] * ctx,
        out_specs=[head_spec(), back_spec, back_spec],
        out_shape=[
            jax.ShapeDtypeStruct((rows, q_width), BF),
            jax.ShapeDtypeStruct((deep, rows, 2 * kv_width), BF),
            jax.ShapeDtypeStruct((deep, rows, 2 * kv_width), BF),
        ],
        compiler_params=params("arbitrary", "arbitrary"),
        name="attend_back",
    )(in_hbm(probs), queries, grad_attended, cosine, sine, *kv_blocks)
    grad_q, grad_kv_own, grad_kv_peer, from_core_moe = arrive(
        sums[0], grad_q, grad_kv_own, grad_kv_peer, from_core_moe
    )

    def to_owner(grad_kv_own, from_peer):
        travel = jnp.zeros(from_peer.shape[1:], BF)
        for k in range(deep - 1, 0, -1):
            piece = grad_kv_own[k] + from_peer[k]
            if k < deep - 1:
                piece = piece + travel
            travel = shift_y(piece, down_y, "grad_kv")
        return travel

    def weight_grads(name, sides, gain_terms, gain_at, cols):
        flat = [array for side in sides for array in side]
        return (pl.pallas_call(
                functools.partial(weight_grad_kernel, [len(side) for side in sides], gain_at),
                in_specs=[smem] + [vmem] * (len(flat) + len(gain_terms)),
                out_specs=[vmem] * 2,
                out_shape=[jax.ShapeDtypeStruct((n, shard, cols), BF)] * 2,
                compiler_params=params(),
                name=f"{name}_weight_grads",
            )
        )(core_scalar, *flat, *gain_terms)

    def close_experts(chain):
        own = chain.parts[0]
        shape = (own.shape[0], shard, 3 * hid)
        kept, sent = pl.pallas_call(
            close_experts_kernel,
            in_specs=[smem] + [vmem] * 3,
            out_specs=[vmem] * 2,
            out_shape=[jax.ShapeDtypeStruct(shape, F32), jax.ShapeDtypeStruct(shape, BF)],
            compiler_params=params(),
            name="close_experts",
        )(core_scalar, own, *chain.moving)
        return kept, sent

    (grad_kv_peer,) = segment(sums[1:], grad_kv_peer)
    from_peer = swap_core(grad_kv_peer, "grad_kv")
    early = weight_grads(
        "early",
        [[grad_branch], [attended], [normed], [grad_q], [normed_two], [grad_logits]],
        [gain_two_term],
        experts,
        2 * q_width + LANES,
    )
    travel = to_owner(grad_kv_own, from_peer)
    early = segment(sums[1:], *early)
    half_at = lambda array, side: lax.dynamic_slice_in_dim(array, side * feature, feature, 1)
    early_other = swap_core(early[1], "early")
    closed = [close_experts(sums[0])]
    moe_sum = moe + from_core_moe.astype(F32)
    moe_send = half_at(moe_sum, 1 - tp).astype(BF)
    travel, early_other, moe_send, *closed[0] = lock(travel, early_other, moe_send, *closed[0])
    shapes = [
        ((rows, 2 * kv_width), BF),
        ((rows, feature), F32),
        ((rows, feature + LANES), BF),
        ((rows, LANES), F32),
        ((1, width), F32),
    ]
    grad_kv, grad_own, grad_send, inner, gain_one_term = pl.pallas_call(
        functools.partial(project_back_kernel, pairs, experts, seqs),
        in_specs=[smem] + [vmem] * 9,
        out_specs=[vmem] * 5,
        out_shape=[jax.ShapeDtypeStruct(shape, kind) for shape, kind in shapes],
        compiler_params=params(),
        name="project_back",
    )(
        tp_scalar,
        grad_q,
        grad_kv_own,
        from_peer,
        travel,
        cosine,
        sine,
        w_qkv,
        full_tokens,
        w_small,
    )
    late = weight_grads(
        "late", [[normed], [grad_kv]], [gain_one_term], 0, 2 * kv_width + LANES
    )
    late_other = swap_core(late[1], "late")
    late_other, early_other = lock(late_other, early_other)
    cols = early_other.shape[2] + late_other.shape[2]
    last = Scatter(
        ring,
        pinned(pl.pallas_call(
            functools.partial(order_kernel, bundle_places),
            in_specs=[smem] + [vmem] * 4,
            out_specs=[vmem] * len(bundle_places),
            out_shape=[jax.ShapeDtypeStruct((1, r, cols), BF) for _, _, r in bundle_places],
            compiler_params=params(),
            name="order",
        ))(chip_list, early[0], early_other, late[0], late_other),
        "last",
    )
    (grad_send,) = together([last, sums[1]], grad_send)
    last.send()
    sums[1].prepare()
    sums[1].send()
    grad_other, moe_other = swap_tp(grad_send, "grad_normed"), swap_tp(moe_send, "moe_send")
    segment([sums[1], last])
    grad_other, moe_other = segment([last], grad_other, moe_other)
    grad_tokens = pinned(
        pl.pallas_call(
            token_grads_kernel,
            in_specs=[vmem] * 5,
            out_specs=vmem,
            out_shape=jax.ShapeDtypeStruct((rows, feature), F32),
            compiler_params=params(),
            name="token_grads",
        )
    )(own_tokens, grad_own, inner, grad_other, grad_middle)
    output = (half_at(middle, tp) + half_at(moe_sum, tp) + moe_other.astype(F32)).astype(BF)
    while not sums[1].done():
        segment(sums[1:])
    grad_tokens, output = together([sums[1], last], grad_tokens, output)
    closed.append(close_experts(sums[1]))
    closed = [[kept, swap_core(sent, "expert_grads")] for kept, sent in closed]
    while not last.done():
        segment([last])
    arrive(last)
    widths = (("one", q_width), ("one", q_width), ("one", LANES), ("pairs", 2 * kv_width), ("one", LANES))
    out_term, grad_query, small_term, grad_key, grad_value, gain_term = (pinned(pl.pallas_call(
            functools.partial(close_weights_kernel, widths),
            in_specs=[vmem] * 3,
            out_specs=[vmem] * 6,
            out_shape=[
                jax.ShapeDtypeStruct((shard, w), F32)
                for w in (q_width, q_width, LANES, kv_width, kv_width, LANES)
            ],
            compiler_params=params(),
            name="close_weights",
        ))
    )(last.parts[0], *last.moving)
    grad_out = out_term.T
    grad_router = small_term[:, :experts]
    grad_gain_ffn = small_term[:, experts]
    gain_half = gain_term[:, 0]
    grad_gain_attn = gain_half + swap_tp(gain_half, "gain")
    gain_half, *closed[1] = lock(gain_half, *closed[1])

    grad_gate, grad_up, down_term = (pl.pallas_call(
            functools.partial(expert_grads_kernel, len(sums)),
            in_specs=[smem] + [vmem] * (2 * len(sums)),
            out_specs=[vmem] * 3,
            out_shape=[pltpu.HBM((experts, shard, hid), F32)] * 3,
            compiler_params=params(),
            name="expert_grads",
        )
    )(
        core_scalar,
        *[closed[k][0] for k in range(len(sums))],
        *[closed[k][1] for k in range(len(sums))],
    )
    grad_down = down_term.transpose(0, 2, 1)

    return (
        output.reshape(seqs, span, feature),
        grad_tokens.reshape(seqs, span, feature),
        grad_query,
        grad_key,
        grad_value,
        grad_out,
        grad_router,
        grad_gain_attn,
        grad_gain_ffn,
        grad_gate,
        grad_up,
        grad_down,
    )


def solution(mesh):
    in_specs = (
        P("fsdp", "ctx", "tp"),
        P("fsdp"),
        P("ctx", "fsdp", None, None),
        P(("fsdp", "ctx"), "tp"),
        P(("fsdp", "ctx"), "tp"),
        P(("fsdp", "ctx"), "tp"),
        P("tp", ("fsdp", "ctx")),
        P(("fsdp", "ctx"), None),
        P(("fsdp", "ctx")),
        P(("fsdp", "ctx")),
        P(None, ("fsdp", "ctx"), "tp"),
        P(None, ("fsdp", "ctx"), "tp"),
        P(None, "tp", ("fsdp", "ctx")),
        P("fsdp", "ctx", "tp"),
    )
    out_specs = (
        P("fsdp", "ctx", "tp"),
        P("fsdp", "ctx", "tp"),
        P(("fsdp", "ctx"), "tp"),
        P(("fsdp", "ctx"), "tp"),
        P(("fsdp", "ctx"), "tp"),
        P("tp", ("fsdp", "ctx")),
        P(("fsdp", "ctx"), None),
        P(("fsdp", "ctx")),
        P(("fsdp", "ctx")),
        P(None, ("fsdp", "ctx"), "tp"),
        P(None, ("fsdp", "ctx"), "tp"),
        P(None, "tp", ("fsdp", "ctx")),
    )
    return jax.shard_map(
        per_device, mesh=mesh, in_specs=in_specs, out_specs=out_specs, check_vma=False
    )
```

```python
import functools

import jax
import jax.numpy as jnp
from jax import lax
from jax.experimental import pallas as pl
from jax.experimental.pallas import tpu as pltpu
from jax.sharding import PartitionSpec as P

HD = 64
TOP = 8
LANES = 128

EPSILON = 1e-06
ATTN_SCALE = 0.015625
RESIDUAL_SCALE = 0.22
MASKED_SCORE = -1e30
RING = ("fsdp", "ctx")
BF = jnp.bfloat16
F32 = jnp.float32
VMEM_LIMIT = 24 * 1024 * 1024
MOE_VMEM = 56 * 1024 * 1024


def nt(a, b):
    return lax.dot_general(a, b, (((1,), (1,)), ((), ())), preferred_element_type=F32)


def nn(a, b):
    return lax.dot_general(a, b, (((1,), (0,)), ((), ())), preferred_element_type=F32)


def tn(a, b):
    return lax.dot_general(a, b, (((0,), (0,)), ((), ())), preferred_element_type=F32)


def params(*semantics):
    return pltpu.CompilerParams(
        dimension_semantics=semantics, vmem_limit_bytes=VMEM_LIMIT
    )


def whole(shape):
    zeros = (0,) * len(shape)
    return pl.BlockSpec(shape, lambda *_: zeros, pipeline_mode=pl.Buffered(1))


def swap_halves(slab):
    lane = lax.broadcasted_iota(jnp.int32, slab.shape, 1) % HD
    return jnp.where(
        lane < HD // 2, pltpu.roll(slab, LANES - HD // 2, 1), pltpu.roll(slab, HD // 2, 1)
    )


def column_as_row(ref, column):
    lane = lax.broadcasted_iota(jnp.int32, (16, ref.shape[1]), 1)
    return nt(jnp.where(lane == column, 1.0, 0.0).astype(BF), ref[...])[:1]


def pack_kernel(q_ref, k_ref, v_ref, out_ref, router_ref, one_ref, two_ref, packed_ref, *scratch):
    stage, sem = scratch
    rows, q_width = q_ref.shape
    copies, at = [], 0

    def copy(source, width):
        nonlocal at
        copies.append(pltpu.make_async_copy(source, packed_ref.at[0, :, pl.ds(at, width)], sem))
        copies[-1].start()
        at += width

    copy(q_ref, q_width)
    for pair in range(k_ref.shape[1] // LANES):
        cols = pl.ds(pair * LANES, LANES)
        copy(k_ref.at[:, cols], LANES)
        copy(v_ref.at[:, cols], LANES)
    copy(out_ref, q_width)
    experts = router_ref.shape[0]
    stage[...] = jnp.zeros(stage.shape, F32)
    stage[:experts, :rows] = router_ref[...].astype(F32)
    stage[experts : experts + 1, :rows] = one_ref[...].astype(F32)
    stage[experts + 1 : experts + 2, :rows] = two_ref[...].astype(F32)
    packed_ref[0, :, at:] = stage[...].T[:rows].astype(BF)
    for each in copies:
        each.wait()


def pack_experts_kernel(core_ref, gate_ref, up_ref, down_ref, mine_ref, other_ref, sem):
    count, _, cols = mine_ref.shape
    hid = cols // 3
    copies = []
    for out_ref, core in ((mine_ref, core_ref[0]), (other_ref, 1 - core_ref[0])):
        for i, source in enumerate((gate_ref, up_ref, down_ref)):
            copies.append(
                pltpu.make_async_copy(
                    source.at[pl.ds(core * count, count)],
                    out_ref.at[:, :, pl.ds(i * hid, hid)],
                    sem,
                )
            )
            copies[-1].start()
    for copy in copies:
        copy.wait()


def join_kernel(core_ref, mine_ref, other_ref, *groups):
    rows = mine_ref.shape[1]
    for mine_first in (True, False):

        @pl.when((core_ref[0] == 0) == mine_first)
        def _():
            at = 0
            for out_ref in groups:
                size = out_ref.shape[0]
                first, second = (mine_ref, other_ref) if mine_first else (other_ref, mine_ref)
                out_ref[:, :rows] = first[at : at + size]
                out_ref[:, rows:] = second[at : at + size]
                at += size


def assemble_kernel(places, where_ref, *refs):
    count = len(places)
    parts, outs, sem = refs[:count], refs[count:-1], refs[-1]

    def copies():
        for j, (_, _, rows) in enumerate(places):
            first = 0
            for out in outs:
                cols = out.shape[1]
                yield pltpu.make_async_copy(
                    parts[j].at[0, :, pl.ds(first, cols)],
                    out.at[pl.ds(pl.multiple_of(where_ref[j], 16), rows)],
                    sem,
                )
                first += cols

    for copy in copies():
        copy.start()
    for copy in copies():
        copy.wait()


def side_by_side(tp_ref, mine, other):
    first = tp_ref[0] == 0
    return jnp.concatenate([jnp.where(first, mine, other), jnp.where(first, other, mine)], axis=1)


def features_kernel(tp_ref, mine_ref, other_ref, full_ref):
    full_ref[...] = side_by_side(tp_ref, mine_ref[...], other_ref[...])


def project_kernel(
    pairs,
    q_width,
    gain_col,
    tp_ref,
    mine_ref,
    other_ref,
    small_ref,
    w_ref,
    cos_ref,
    sin_ref,
    x_ref,
    n_ref,
    q_ref,
    kv_ref,
):
    x_ref[...] = side_by_side(tp_ref, mine_ref[...], other_ref[...])
    x = x_ref[...].astype(F32)
    gain = column_as_row(small_ref, gain_col)
    scale = lax.rsqrt(jnp.mean(x * x, axis=1, keepdims=True) + EPSILON)
    normed = (x * scale * gain).astype(BF)
    n_ref[...] = normed
    cosine, sine = cos_ref[...], sin_ref[...]
    raw = nn(normed, w_ref[...])
    for slab in range(q_width // LANES):
        cols = slice(slab * LANES, (slab + 1) * LANES)
        part = raw[:, cols]
        turned = (part * cosine + swap_halves(part) * sine).astype(BF)
        q_ref[:, cols] = (turned.astype(F32) * ATTN_SCALE).astype(BF)
    for pair in range(pairs):
        lo = pair * 2 * LANES
        part = raw[:, q_width + lo : q_width + lo + LANES]
        kv_ref[:, lo : lo + LANES] = (part * cosine + swap_halves(part) * sine).astype(BF)
        kv_ref[:, lo + LANES : lo + 2 * LANES] = raw[
            :, q_width + lo + LANES : q_width + lo + 2 * LANES
        ].astype(BF)


def attend_kernel(blocks, span, prefix_ref, base_ref, q_ref, *refs):
    kv_refs = refs[:blocks]
    out_ref, p_ref = refs[blocks:]
    limit_len = prefix_ref[pl.program_id(0)]
    local = base_ref[0] + lax.broadcasted_iota(jnp.int32, (span, 1), 0)
    limit = jnp.maximum(local + 1, limit_len)
    key_pos = jnp.concatenate(
        [
            base_ref[j] + lax.broadcasted_iota(jnp.int32, (1, span), 1)
            for j in range(blocks)
        ],
        axis=1,
    )
    visible = key_pos < limit
    visible = jnp.concatenate([visible, visible], axis=0)
    for g in range(2):
        keys = jnp.concatenate([r[:, g * HD : (g + 1) * HD] for r in kv_refs], axis=0)
        vals = jnp.concatenate(
            [r[:, LANES + g * HD : LANES + (g + 1) * HD] for r in kv_refs], axis=0
        )
        first, second = 2 * g * HD, (2 * g + 1) * HD
        queries = jnp.concatenate(
            [q_ref[:, first : first + HD], q_ref[:, second : second + HD]], axis=0
        )
        scores = jnp.where(visible, nt(queries, keys), MASKED_SCORE)
        expo = jnp.exp(scores - jnp.max(scores, axis=1, keepdims=True))
        probs = (expo * (1.0 / jnp.sum(expo, axis=1, keepdims=True))).astype(BF)
        p_ref[0, g] = probs
        att = nn(probs, vals).astype(BF)
        out_ref[:, first : first + HD] = att[:span]
        out_ref[:, second : second + HD] = att[span:]


def attend_back_kernel(blocks, span, p_ref, q_ref, g_ref, cos_ref, sin_ref, *refs):
    kv_refs = refs[:blocks]
    dq_ref, own_ref, other_ref = refs[blocks:]
    cosine, sine = cos_ref[...], sin_ref[...]
    parts = []
    for g in range(2):
        keys = jnp.concatenate([r[:, g * HD : (g + 1) * HD] for r in kv_refs], axis=0)
        vals = jnp.concatenate(
            [r[:, LANES + g * HD : LANES + (g + 1) * HD] for r in kv_refs], axis=0
        )
        first, second = 2 * g * HD, (2 * g + 1) * HD
        queries = jnp.concatenate(
            [q_ref[:, first : first + HD], q_ref[:, second : second + HD]], axis=0
        )
        grads = jnp.concatenate(
            [g_ref[:, first : first + HD], g_ref[:, second : second + HD]], axis=0
        )
        probs = p_ref[0, g]
        wide = probs.astype(F32)
        grad_probs = nt(grads, vals)
        inner = jnp.sum(wide * grad_probs, axis=1, keepdims=True)
        grad_scores = (wide * (grad_probs - inner)).astype(BF)
        dq = nn(grad_scores, keys) * ATTN_SCALE
        slab = jnp.concatenate([dq[:span], dq[span:]], axis=1)
        turned = slab * cosine - swap_halves(slab) * sine
        dq_ref[:, first : first + LANES] = turned.astype(BF)
        parts.append((nn(queries.T, grad_scores), nn(grads.T, probs)))
    stacked = jnp.concatenate([parts[0][0], parts[1][0], parts[0][1], parts[1][1]], axis=0)
    turned = stacked.T.astype(BF)
    half = blocks // 2
    for j in range(half):
        own_ref[j] = turned[j * span : (j + 1) * span]
        other_ref[j] = turned[(half + j) * span : (half + j + 1) * span]


def middle_kernel(
    gain_col, a_ref, b_ref, wa_ref, wb_ref, x_ref, small_ref, routes_ref, m_ref, n_ref, g_ref
):
    branch = nt(a_ref[...], wa_ref[...]) + nt(b_ref[...], wb_ref[...])
    middle = x_ref[...].astype(F32) + RESIDUAL_SCALE * branch
    m_ref[...] = middle
    scale = lax.rsqrt(jnp.mean(middle * middle, axis=1, keepdims=True) + EPSILON)
    wide = middle * scale * column_as_row(small_ref, gain_col)
    normed = wide.astype(BF)
    width = normed.shape[1]
    n_ref[:, :width] = normed
    logits = nn(normed, small_ref[...])
    lane = lax.broadcasted_iota(jnp.int32, logits.shape, 1)
    routes = routes_ref[...]
    routed = lane == routes[:, 0:1]
    for k in range(1, TOP):
        routed = routed | (lane == routes[:, k : k + 1])
    logits = jnp.where(routed, logits, MASKED_SCORE)
    expo = jnp.where(routed, jnp.exp(logits - jnp.max(logits, axis=1, keepdims=True)), 0.0)
    gates = expo / jnp.sum(expo, axis=1, keepdims=True)
    g_ref[...] = gates
    n_ref[:, width:] = in_two(gates, gain_col - 1)


def in_two(pull, experts):
    high = pull.astype(BF).astype(F32)
    return (high + pltpu.roll(pull - high, experts, 1)).astype(BF)


def in_one(terms, experts):
    wide = terms.astype(F32)
    lane = lax.broadcasted_iota(jnp.int32, wide.shape, 1)
    both = wide + pltpu.roll(wide, LANES - experts, 1)
    return jnp.where(lane < experts, both, 0.0)


def moe_kernel(
    first_call, last_call, joins, experts, column, start, sums_start, group, places, where_ref, *refs
):
    count = len(places)
    w_parts, refs = refs[:count], refs[count:]
    sources, refs = refs[:4], refs[4:]
    inits, refs = ((), refs) if first_call else (refs[:2], refs[2:])
    refs = refs[count:] if joins else refs
    outs, mixed_out, dw_parts, refs = refs[:2], refs[2], refs[3 : 3 + count], refs[3 + count :]
    here, accs, refs = refs[:4], refs[4:6], refs[6:]
    mixed_all, narrow, w_all, dw_all, w_sem, dw_sem, near_sem, acc_sem, out_sem, mixed_sem = refs
    xa_ref, ya_ref, xb_ref, yb_ref = here
    rows, width = ya_ref.shape
    hid = w_all.shape[2] // 3

    def window(j):
        return pl.ds(pl.multiple_of(where_ref[1 + j], 16), places[j][2])

    def load(e, j):
        return pltpu.make_async_copy(
            w_parts[j].at[start + e], w_all.at[e, window(j)], w_sem.at[e]
        )

    def store(e, j):
        return pltpu.make_async_copy(
            dw_all.at[e % 2, window(j)], dw_parts[j].at[sums_start + e], dw_sem.at[e % 2]
        )

    nears = [
        pltpu.make_async_copy(a, b, near_sem.at[i]) for i, (a, b) in enumerate(zip(sources, here))
    ]
    fetches = [
        pltpu.make_async_copy(a, b, acc_sem.at[i]) for i, (a, b) in enumerate(zip(inits, accs))
    ]
    mixed_store = pltpu.make_async_copy(mixed_all, mixed_out, mixed_sem)
    for j in range(count):
        load(0, j).start()
    for copy in nears[:2]:
        copy.start()
    results = []
    for e in range(group):
        for j in range(count):
            load(e, j).wait()
        if e == 0:
            for copy in nears[:2]:
                copy.wait()
            for copy in [*fetches[:1], *nears[2:], *fetches[1:]]:
                copy.start()
        expert = where_ref[0] + column + e
        w_gu, w_d = w_all[e, :, : 2 * hid], w_all[e, :, 2 * hid :]
        kept = []
        for side, (x_ref, y_ref) in enumerate(((xa_ref, ya_ref), (xb_ref, yb_ref))):
            acc = accs[side]
            if e == 0 and side == 1:
                for copy in nears[2:]:
                    copy.wait()
                for other in range(1, group):
                    for j in range(count):
                        load(other, j).start()
            pre = nn(x_ref[:, :width], w_gu)
            back = nn(y_ref[...], w_d)
            gates = in_one(x_ref[:, width:], experts)
            lane = lax.broadcasted_iota(jnp.int32, gates.shape, 1)
            mask = lane == expert
            weight = RESIDUAL_SCALE * jnp.sum(
                jnp.where(mask, gates, 0.0), axis=1, keepdims=True
            )
            gate_pre, up_pre = pre[:, :hid], pre[:, hid:]
            sig = jax.nn.sigmoid(gate_pre)
            act = gate_pre * sig
            hidden = act * up_pre
            pull = RESIDUAL_SCALE * jnp.sum(back * hidden, axis=1, keepdims=True)
            scaled = weight * back
            d_up = scaled * act
            d_gate = scaled * up_pre * (sig + act * (1.0 - sig))
            d_gu = jnp.concatenate([d_gate.astype(BF), d_up.astype(BF)], axis=1)
            mixed = (weight * hidden).astype(BF)
            mixed_all[e, side * rows : (side + 1) * rows] = mixed
            if first_call and e == 0:
                acc[:, :width] = nt(d_gu, w_gu)
                acc[:, width:] = jnp.where(mask, pull, 0.0)
            else:
                if e == 0:
                    fetches[side].wait()
                acc[:, :width] += nt(d_gu, w_gu)
                acc[:, width:] += jnp.where(mask, pull, 0.0)
            kept.append((d_gu, mixed))
            if e == group - 1:
                if last_call and side:
                    narrow[:, :width] = acc[:, :width].astype(BF)
                    narrow[:, width:] = in_two(acc[:, width:], experts)
                    acc = narrow
                results.append(pltpu.make_async_copy(acc, outs[side], out_sem.at[side]))
                results[-1].start()
        if e == group - 1:
            mixed_store.start()
        dw_gu = tn(xa_ref[:, :width], kept[0][0]) + tn(xb_ref[:, :width], kept[1][0])
        dw_d = tn(ya_ref[...], kept[0][1]) + tn(yb_ref[...], kept[1][1])
        if e >= 2:
            for j in range(count):
                store(e - 2, j).wait()
        dw_all[e % 2, :, : 2 * hid] = dw_gu.astype(BF)
        dw_all[e % 2, :, 2 * hid :] = dw_d.astype(BF)
        for j in range(count):
            store(e, j).start()
    for e in range(max(0, group - 2), group):
        for j in range(count):
            store(e, j).wait()
    for copy in results:
        copy.wait()
    mixed_store.wait()


def moe_sum_kernel(places, plan, where_ref, *refs):
    count, sets = len(places), len(plan)
    w_sets = [refs[k * count : (k + 1) * count] for k in range(sets)]
    refs = refs[sets * count :]
    calls = sum(len(sizes) for sizes in plan)
    mixed_parts, refs = refs[:calls], refs[calls:]
    own_ref, peer_ref, refs = refs[0], refs[1], refs[2:]
    w_all, mixed_all, (w_sem, mixed_sem) = refs[:sets], refs[sets : 2 * sets], refs[2 * sets :]
    rows = own_ref.shape[0]

    def loads(k):
        hid = w_all[k].shape[1] // sum(plan[k])
        at = 0
        for call, size in enumerate(plan[k]):
            source = mixed_parts[sum(len(sizes) for sizes in plan[:k]) + call]
            for i in range(size):
                cols = pl.ds(at * hid, hid)
                for j in range(count):
                    window = pl.ds(pl.multiple_of(where_ref[1 + j], 16), places[j][2])
                    yield pltpu.make_async_copy(
                        w_sets[k][j].at[at, :, pl.ds(2 * hid, hid)],
                        w_all[k].at[window, cols],
                        w_sem.at[k],
                    )
                yield pltpu.make_async_copy(
                    source.at[i], mixed_all[k].at[:, cols], mixed_sem.at[k]
                )
                at += 1

    for k in range(sets):
        for copy in loads(k):
            copy.start()
    total = None
    for k in range(sets):
        for copy in loads(k):
            copy.wait()
        term = nt(mixed_all[k][...], w_all[k][...])
        total = term if total is None else total + term
    own_ref[...] = total[:rows]
    peer_ref[...] = total[rows:].astype(BF)


def weight_grad_kernel(counts, gain_at, core_ref, *refs):
    sides = []
    for size in counts:
        sides.append(jnp.concatenate([ref[...] for ref in refs[:size]], axis=0))
        refs = refs[size:]
    gain_refs, (kept_ref, sent_ref) = refs[:-2], refs[-2:]
    n, shard, _ = kept_ref.shape
    width = 2 * n * shard
    terms = [tn(left[:, :width], right) for left, right in zip(sides[::2], sides[1::2])]
    if gain_refs:
        if terms[-1].shape[1] != LANES:
            terms.append(jnp.zeros((width, LANES), F32))
        row = lax.broadcasted_iota(jnp.int32, (8, LANES), 0)
        lane = lax.broadcasted_iota(jnp.int32, (8, LANES), 1)
        place = jnp.where((row == 0) & (lane == gain_at), 1.0, 0.0)
        gain = sum(ref[...] for ref in gain_refs)
        terms[-1] = terms[-1] + tn(jnp.broadcast_to(gain, (8, width)), place)
    first = 0
    for term in terms:
        cols = term.shape[1]
        parts = term.astype(BF).reshape(n, 2, shard, cols)
        for mine in range(2):

            @pl.when(core_ref[0] == mine)
            def _():
                kept_ref[:, :, first : first + cols] = parts[:, mine]
                sent_ref[:, :, first : first + cols] = parts[:, 1 - mine]

        first += cols


def order_kernel(places, chips_ref, *refs):
    count = len(places)
    pairs, parts = refs[:-count], refs[-count:]
    for j, (_, row, rows) in enumerate(places):
        chip = chips_ref[j]
        window = pl.ds(row, rows)
        first = 0
        for kept_ref, other_ref in zip(pairs[::2], pairs[1::2]):
            cols = kept_ref.shape[2]
            parts[j][0, :, first : first + cols] = kept_ref[chip, window] + other_ref[chip, window]
            first += cols


def add_terms_kernel(experts, own_ref, peer_ref, sum_ref):
    width = own_ref.shape[1] - LANES
    total = own_ref[:, :width] + peer_ref[:, :width].astype(F32)
    sum_ref[:, :width] = total.astype(BF)
    pull = own_ref[:, width:] + in_one(peer_ref[:, width:], experts)
    sum_ref[:, width:] = in_two(pull, experts)


def close_experts_kernel(core_ref, own_ref, ahead_ref, back_ref, kept_ref, sent_ref):
    rows = kept_ref.shape[1]
    total = own_ref[...].astype(F32) + ahead_ref[...].astype(F32) + back_ref[...].astype(F32)
    is_first = core_ref[0] == 0
    kept_ref[...] = jnp.where(is_first, total[:, :rows], total[:, rows:])
    sent_ref[...] = jnp.where(is_first, total[:, rows:], total[:, :rows]).astype(BF)


def expert_grads_kernel(chains, core_ref, *refs):
    kept_refs, sent_refs, outs = refs[:chains], refs[chains : 2 * chains], refs[2 * chains :]
    count, _, cols = kept_refs[0].shape
    hid = cols // 3
    for k in range(chains):
        for ref, core in ((kept_refs[k], core_ref[0]), (sent_refs[k], 1 - core_ref[0])):
            for i in range(count):
                at = core * chains * count + k * count + i
                for part, out in enumerate(outs):
                    out[at] = ref[i, :, part * hid : (part + 1) * hid].astype(F32)


def close_weights_kernel(widths, own_ref, ahead_ref, back_ref, *outs):
    def total(cols):
        return (
            own_ref[0, :, cols].astype(F32)
            + ahead_ref[0, :, cols].astype(F32)
            + back_ref[0, :, cols].astype(F32)
        )

    first = 0
    for kind, width in widths:
        if kind == "pairs":
            for pair in range(width // (2 * LANES)):
                for side in range(2):
                    lo = first + (2 * pair + side) * LANES
                    outs[side][:, pair * LANES : (pair + 1) * LANES] = total(slice(lo, lo + LANES))
            outs = outs[2:]
        else:
            outs[0][...] = total(slice(first, first + width))
            outs = outs[1:]
        first += width


def token_grads_kernel(x_ref, own_ref, dot_ref, other_ref, middle_ref, out_ref):
    feature = x_ref.shape[1]
    other = other_ref[...]
    dot = dot_ref[:, :1] + in_one(other[:, feature:], 1)[:, :1]
    total = middle_ref[...] + own_ref[...] + other[:, :feature].astype(F32)
    out_ref[...] = total - x_ref[...].astype(F32) * dot


def middle_back_kernel(
    gain_col,
    tp_ref,
    sa_ref,
    sb_ref,
    gates_ref,
    m_ref,
    y_ref,
    small_ref,
    wo_ref,
    gm_ref,
    branch_ref,
    att_ref,
    logit_ref,
    dgain_ref,
):
    @pl.when(pl.program_id(0) == 0)
    def _():
        dgain_ref[...] = jnp.zeros(dgain_ref.shape, F32)

    gates = gates_ref[...]
    width = m_ref.shape[1]
    pull = in_one(sa_ref[:, width:], gain_col - 1) + in_one(sb_ref[:, width:], gain_col - 1)
    weighted = gates * pull
    grad_logits = (weighted - gates * jnp.sum(weighted, axis=1, keepdims=True)).astype(BF)
    logit_ref[...] = grad_logits
    grad = sa_ref[:, :width].astype(F32) + sb_ref[:, :width].astype(F32)
    grad = grad + nt(grad_logits, small_ref[...])
    middle = m_ref[...]
    scale = lax.rsqrt(jnp.mean(middle * middle, axis=1, keepdims=True) + EPSILON)
    unit = middle * scale
    dgain_ref[...] += jnp.sum(grad * unit, axis=0, keepdims=True)
    scaled = grad * column_as_row(small_ref, gain_col)
    inner = jnp.sum(scaled * unit, axis=1, keepdims=True) * (1.0 / width)
    grad_middle = y_ref[...].astype(F32) + scale * (scaled - unit * inner)
    half = width // 2
    gm_ref[...] = jnp.where(tp_ref[0] == 0, grad_middle[:, :half], grad_middle[:, half:])
    branch = (RESIDUAL_SCALE * grad_middle).astype(BF)
    branch_ref[...] = branch
    att_ref[...] = nn(branch, wo_ref[...]).astype(BF)


def project_back_kernel(pairs, gain_col, seqs, tp_ref, *refs):
    dq_ref, kva_ref, kvb_ref, kvc_ref, cos_ref, sin_ref, w_ref, x_ref, small_ref = refs[:9]
    d_ref, own_ref, other_ref, dot_ref, dgain_ref = refs[9:]
    gain = column_as_row(small_ref, gain_col)
    is_first = tp_ref[0] == 0
    rows, q_width = dq_ref.shape
    span = rows // seqs
    for s in range(seqs):
        at = slice(s * span, (s + 1) * span)
        cosine, sine = cos_ref[at], sin_ref[at]
        kv = kva_ref[0, at].astype(F32) + kvb_ref[0, at].astype(F32) + kvc_ref[at].astype(F32)
        for pair in range(pairs):
            lo = pair * 2 * LANES
            part = kv[:, lo : lo + LANES]
            d_ref[at, lo : lo + LANES] = (part * cosine - swap_halves(part) * sine).astype(BF)
            d_ref[at, lo + LANES : lo + 2 * LANES] = kv[:, lo + LANES : lo + 2 * LANES].astype(BF)
        grad = nt(dq_ref[at], w_ref[:, :q_width]) + nt(d_ref[at], w_ref[:, q_width:])
        x = x_ref[at].astype(F32)
        width = x.shape[1]
        scale = lax.rsqrt(jnp.mean(x * x, axis=1, keepdims=True) + EPSILON)
        unit = x * scale
        term = jnp.sum(grad * unit, axis=0, keepdims=True)
        if s == 0:
            dgain_ref[...] = term
        else:
            dgain_ref[...] += term
        scaled = grad * gain
        inner = jnp.sum(scaled * unit, axis=1, keepdims=True) * (1.0 / width) * scale * scale
        lane = lax.broadcasted_iota(jnp.int32, (span, LANES), 1)
        dot = jnp.where(lane == 0, inner, 0.0)
        dot_ref[at] = dot
        scaled = scaled * scale
        half = width // 2
        own_ref[at] = jnp.where(is_first, scaled[:, :half], scaled[:, half:])
        other_ref[at, :half] = jnp.where(is_first, scaled[:, half:], scaled[:, :half]).astype(BF)
        other_ref[at, half:] = in_two(dot, 1)


class Ring:
    def __init__(self, wide, ctx):
        self.wide, self.ctx, self.deep = wide, ctx, ctx // 2
        self.size = wide * self.deep
        deep = self.deep
        order = [
            (f, y)
            for y in range(deep)
            for f in (range(wide) if y % 2 == 0 else range(wide - 1, -1, -1))
        ]
        flat = [[f * ctx + y * 2 + c for f, y in order] for c in range(2)]
        n = self.size
        self.forward = [(row[i], row[(i + 1) % n]) for row in flat for i in range(n)]
        self.backward = [(b, a) for a, b in self.forward]
        f, c = lax.axis_index("fsdp"), lax.axis_index("ctx")
        y = c // 2
        self.place = y * wide + jnp.where(y % 2 == 0, f, wide - 1 - f)

    def chip(self, offset):
        place = (self.place + offset) % self.size
        y, q = place // self.wide, place % self.wide
        f = jnp.where(y % 2 == 0, q, self.wide - 1 - q)
        return f * self.deep + y

    def send(self, array, forward=True):
        return lax.ppermute(array, RING, self.forward if forward else self.backward)

    def places(self, rows):
        far, half = self.size // 2, rows // 2
        found = [(0, 0, rows)]
        for step in range(1, far):
            found += [(-step, 0, rows), (step, 0, rows)]
        if half % 16:
            return found + [(-far, 0, rows)]
        return found + [(-far, 0, half), (far, half, half)]


class Gather:
    def __init__(self, ring, block, name):
        self.ring, self.step, self.rows, self.name = ring, 0, block.shape[1], name
        self.moving = (block, block)
        self.parts = [block]

    def prepare(self):
        if self.step == self.ring.size // 2 - 1:
            half = self.rows // 2
            ahead, back = self.moving
            self.moving = (ahead[:, :half], back[:, half:]) if half % 16 == 0 else (ahead,)

    def send(self):
        self.step += 1
        with jax.named_scope(f"{self.name}_step_{self.step}"):
            self.moving = tuple(
                self.ring.send(array, i == 0) for i, array in enumerate(self.moving)
            )
        self.parts += self.moving

    def done(self):
        return self.step == self.ring.size // 2


class Scatter:
    def __init__(self, ring, parts, name):
        self.ring, self.parts, self.step, self.name = ring, parts, 0, name
        self.far = ring.size // 2
        self.halved = len(parts) == ring.size + 1
        self.moving = (parts[-2], parts[-1]) if self.halved else (parts[-1],)

    def prepare(self):
        if self.step:
            s = self.far - self.step
            self.moving = add_pair(self.parts[2 * s], self.parts[2 * s - 1], *self.moving)

    def send(self):
        self.step += 1
        with jax.named_scope(f"{self.name}_step_{self.step}"):
            self.moving = tuple(
                self.ring.send(array, i == 0) for i, array in enumerate(self.moving)
            )

    def done(self):
        return self.step == self.far


def add_pair_kernel(near_ref, behind_ref, *refs):
    moved, outs = refs[:-2], refs[-2:]
    rows = near_ref.shape[1]
    for i, (mine, out) in enumerate(zip((near_ref, behind_ref), outs)):
        if i >= len(moved):
            out[...] = mine[...]
            continue
        came = moved[i]
        size = came.shape[1]
        at = slice(0, size) if i == 0 else slice(rows - size, rows)
        total = (mine[:, at].astype(F32) + came[...].astype(F32)).astype(BF)
        if size == rows:
            out[...] = total
        else:
            rest = slice(size, rows) if i == 0 else slice(0, rows - size)
            out[:, at] = total
            out[:, rest] = mine[:, rest]


def add_pair(near, behind, *moved):
    def spec(array):
        return pl.BlockSpec((1,) + array.shape[1:], lambda i: (i, 0, 0))

    arrays = (near, behind, *moved)
    out = jax.ShapeDtypeStruct(near.shape, BF)
    return pl.pallas_call(
        add_pair_kernel,
        grid=(near.shape[0],),
        in_specs=[spec(array) for array in arrays],
        out_specs=[spec(near)] * 2,
        out_shape=[out] * 2,
        compiler_params=params("arbitrary"),
        name="add_pair",
    )(*arrays)


def pinned(call):
    def run(*args):
        return call(
            *[
                pltpu.with_memory_space_constraint(a, pltpu.HBM)
                if a.ndim > 1 and a.dtype != jnp.int32
                else a
                for a in args
            ]
        )

    return run


def lock(*values):
    return lax.optimization_barrier(values)


def per_device(
    tokens,
    prefix,
    routes,
    w_query,
    w_key,
    w_value,
    w_out,
    w_router,
    gain_attn,
    gain_ffn,
    w_gate,
    w_up,
    w_down,
    cotangent,
):
    wide, ctx = lax.axis_size("fsdp"), lax.axis_size("ctx")
    seqs, span, feature = tokens.shape
    rows = seqs * span
    width = 2 * feature
    shard = w_query.shape[0]
    experts = w_router.shape[1]
    per_core = experts // 2
    hid = w_gate.shape[2]
    q_width, kv_width = w_query.shape[1], w_key.shape[1]
    pairs = kv_width // LANES
    deep = ctx // 2
    quarter = per_core // 4
    plan = ((quarter, quarter), (quarter,), (per_core - 3 * quarter,))
    tp, c = lax.axis_index("tp"), lax.axis_index("ctx")
    core, y = c % 2, c // 2
    ring = Ring(wide, ctx)
    n = ring.size
    core_perm = [(i, i ^ 1) for i in range(ctx)]

    def swap_core(array, name="rows"):
        with jax.named_scope(f"{name}_over_core"):
            return lax.ppermute(array, "ctx", core_perm)

    def swap_tp(array, name="rows"):
        with jax.named_scope(f"{name}_over_tp"):
            return lax.ppermute(array, "tp", [(0, 1), (1, 0)])

    up_y = [(i, (i + 2) % ctx) for i in range(ctx)]
    down_y = [(i, (i - 2) % ctx) for i in range(ctx)]

    def shift_y(array, perm, name):
        with jax.named_scope(f"{name}_over_y"):
            return lax.ppermute(array, "ctx", perm)

    tp_scalar = tp.astype(jnp.int32).reshape(1)

    def by_core(mine, other, axis):
        return jnp.where(
            core == 0,
            jnp.concatenate([mine, other], axis),
            jnp.concatenate([other, mine], axis),
        )

    vmem = pl.BlockSpec(memory_space=pltpu.VMEM)
    smem = pl.BlockSpec(memory_space=pltpu.SMEM)
    any_spec = pl.BlockSpec(memory_space=pl.ANY)
    qkv_width = q_width + 2 * kv_width
    in_hbm = lambda array: pltpu.with_memory_space_constraint(array, pltpu.HBM)
    small_rows = max(shard, LANES)
    bundle = pl.pallas_call(
        pack_kernel,
        in_specs=[any_spec] * 4 + [vmem] * 3,
        out_specs=vmem,
        out_shape=jax.ShapeDtypeStruct((1, shard, qkv_width + q_width + LANES), BF),
        scratch_shapes=[pltpu.VMEM((LANES, small_rows), F32), pltpu.SemaphoreType.DMA(())],
        compiler_params=params(),
        name="pack",
    )(
        *[in_hbm(w) for w in (w_query, w_key, w_value, w_out.T)],
        w_router.T,
        gain_attn[None],
        gain_ffn[None],
    )
    own_tokens = tokens.reshape(rows, feature)
    own_cot = cotangent.reshape(rows, feature)
    core_scalar = core.astype(jnp.int32).reshape(1)
    def segment(ticks, *values):
        chains = [chain for chain in ticks if not chain.done()]

        values = together(chains, *values)
        if any(chain.step for chain in chains):
            for chain in chains:
                chain.prepare()
            values = together(chains, *values)
        for chain in chains:
            chain.send()
        return values

    def together(chains, *values):
        held = [array for chain in chains for array in chain.moving]
        out = lock(*held, *values)
        at = 0
        for chain in chains:
            size = len(chain.moving)
            chain.moving = tuple(out[at : at + size])
            at += size
        return out[at:]

    def arrive(chain, *values):
        return together([chain], *values)

    first = Gather(ring, bundle, "bundle")
    half_shape = jax.ShapeDtypeStruct((per_core, shard, 3 * hid), BF)
    *raw_w, own_tokens, bundle = segment(
        [first], w_gate, w_up, w_down.transpose(0, 2, 1), own_tokens, bundle
    )
    mine_w, other_w = pl.pallas_call(
        pack_experts_kernel,
        in_specs=[smem] + [any_spec] * 3,
        out_specs=[vmem] * 2,
        out_shape=[half_shape] * 2,
        scratch_shapes=[pltpu.SemaphoreType.DMA(())],
        compiler_params=params(),
        name="pack_experts",
    )(core_scalar, *[in_hbm(w) for w in raw_w])
    from_core = [swap_core(bundle, "bundle")]
    other_w = swap_core(other_w, "experts")
    from_core[0], other_w, mine_w = segment([first], from_core[0], other_w, mine_w)
    blocks_w = list(
        pl.pallas_call(
            join_kernel,
            in_specs=[smem] + [vmem] * 2,
            out_specs=[vmem] * len(plan),
            out_shape=[
                jax.ShapeDtypeStruct((sum(sizes), 2 * shard, 3 * hid), BF) for sizes in plan
            ],
            compiler_params=params(),
            name="join",
        )(core_scalar, mine_w, other_w)
    )
    half_width = HD // 2
    freqs = 10000.0 ** (-jnp.arange(half_width, dtype=F32) / half_width)
    local_pos = c * span + jnp.arange(span, dtype=jnp.int32)
    angles = local_pos.astype(F32)[:, None] * freqs[None, :]
    cosine, sine = jnp.cos(angles), jnp.sin(angles)
    cosine = jnp.tile(jnp.concatenate([cosine] * 4, axis=1), (seqs, 1))
    sine = jnp.tile(jnp.concatenate([-sine, sine, -sine, sine], axis=1), (seqs, 1))
    chips = [ring.chip(d) for d, _, _ in ring.places(shard)]
    chip_list = jnp.stack(chips).astype(jnp.int32)
    bundle_places = ring.places(shard)
    bundle_rows = [
        (chips[j] * 2 + side) * shard + row
        for side in (core, 1 - core)
        for j, (_, row, _) in enumerate(bundle_places)
    ]
    bundle_where = jnp.stack(bundle_rows).astype(jnp.int32)
    places = ring.places(2 * shard)
    part_rows = [ring.chip(d) * 2 * shard + row for d, row, _ in places]
    part_where = jnp.stack([core * per_core] + part_rows).astype(jnp.int32)
    base = jnp.stack(
        [(((y - k) % deep) * 2 + core) * span for k in range(deep)]
        + [(((y - k) % deep) * 2 + 1 - core) * span for k in range(deep)]
    ).astype(jnp.int32)
    other_tokens = swap_tp(own_tokens, "tokens")
    shared = 1
    while not first.done():
        fresh = [swap_core(part, "part") for part in first.parts[shared : first.step * 2 - 1]]
        shared += len(fresh)
        last_step = first.step == ring.size // 2 - 1
        *fresh, blocks_w[0], cosine, sine, chip_list, bundle_where, part_where, base, tokens_here = segment(
            [first],
            *fresh,
            blocks_w[0],
            cosine,
            sine,
            chip_list,
            bundle_where,
            part_where,
            base,
            other_tokens if last_step else own_tokens,
        )
        if last_step:
            other_tokens = tokens_here
        from_core += fresh
    weights = [Gather(ring, block, f"weights_{i}") for i, block in enumerate(blocks_w)]
    rest = [swap_core(part, "part") for part in first.parts[shared:-2]]
    other_cot = swap_tp(own_cot, "cotangent")
    *rest, other_cot, weights[0].moving = arrive(
        first, *rest, other_cot, weights[0].moving[0]
    )
    weights[0].moving = (weights[0].moving,) * 2
    weights[0].send()
    from_core += rest
    rest = [swap_core(part, "part") for part in first.parts[shared + len(rest) :]]
    from_core += rest
    w_qkv, wo_mine, w_small = pl.pallas_call(
        functools.partial(assemble_kernel, bundle_places * 2),
        in_specs=[smem] + [any_spec] * len(bundle_rows),
        out_specs=[vmem] * 3,
        out_shape=[
            jax.ShapeDtypeStruct((width, w), BF) for w in (qkv_width, q_width, LANES)
        ],
        scratch_shapes=[pltpu.SemaphoreType.DMA(())],
        compiler_params=params(),
        name="assemble",
    )(
        bundle_where,
        *[in_hbm(part) for part in first.parts + from_core],
    )
    step_rows = min(rows, 256)
    steps = rows // step_rows
    row_spec = lambda cols: pl.BlockSpec((step_rows, cols), lambda i, *_: (i, 0))
    full_tokens, normed, queries, kv = (pl.pallas_call(
        functools.partial(project_kernel, pairs, q_width, experts),
        grid=(steps,),
        in_specs=[
            smem,
            row_spec(feature),
            row_spec(feature),
            whole((width, LANES)),
            whole((width, qkv_width)),
            row_spec(LANES),
            row_spec(LANES),
        ],
        out_specs=[row_spec(width), row_spec(width), row_spec(q_width), row_spec(2 * kv_width)],
        out_shape=[
            pltpu.HBM((rows, width), BF),
            pltpu.HBM((rows, width), BF),
            jax.ShapeDtypeStruct((rows, q_width), BF),
            jax.ShapeDtypeStruct((rows, 2 * kv_width), BF),
        ],
        compiler_params=params("arbitrary"),
        name="project",
    ))(tp_scalar, own_tokens, other_tokens, w_small, w_qkv, cosine, sine)

    own_side = [kv]
    for _ in range(deep - 1):
        own_side.append(shift_y(own_side[-1], up_y, "kv"))
    other_side = [swap_core(kv, "kv")]
    wo_other = swap_tp(wo_mine, "w_out")
    length = ctx * span

    queries, *own_side = segment(weights[:1], queries, *own_side)
    other_side += [swap_core(block, "kv") for block in own_side[1:]]
    kv_blocks = own_side + other_side
    head_spec = lambda: pl.BlockSpec((span, 2 * LANES), lambda s, p, *_: (s, p))
    prob_spec = pl.BlockSpec((1, 2, 2 * span, length), lambda s, p, *_: (s, p, 0, 0))
    attended, probs = (pl.pallas_call(
        functools.partial(attend_kernel, ctx, span),
        grid_spec=pltpu.PrefetchScalarGridSpec(
            num_scalar_prefetch=2,
            grid=(seqs, pairs),
            in_specs=[head_spec()] * (1 + ctx),
            out_specs=[head_spec(), prob_spec],
        ),
        out_shape=[
            jax.ShapeDtypeStruct((rows, q_width), BF),
            pltpu.HBM((seqs, 2 * pairs, 2 * span, length), BF),
        ],
        compiler_params=params("arbitrary", "arbitrary"),
        name="attend",
    ))(prefix, base, queries, *kv_blocks)

    attended, wo_other = segment(weights[:1], attended, wo_other)
    for _ in range(ring.size // 2 - 4):
        (attended,) = segment(weights[:1], attended)

    attended_other = swap_tp(attended, "attended")
    full_cot = (pl.pallas_call(
            features_kernel,
            in_specs=[smem] + [vmem] * 2,
            out_specs=vmem,
            out_shape=pltpu.HBM((rows, width), BF),
            compiler_params=params(),
            name="features",
        )
    )(tp_scalar, own_cot, other_cot)
    peer_cot = swap_core(full_cot, "full_cot")
    (attended_other,) = segment(weights[:1], attended_other)
    route_rows = routes.reshape(rows, TOP)
    middle, normed_two, gates = (pinned(pl.pallas_call(
        functools.partial(middle_kernel, experts + 1),
        grid=(steps,),
        in_specs=[
            row_spec(q_width),
            row_spec(q_width),
            whole((width, q_width)),
            whole((width, q_width)),
            row_spec(width),
            whole((width, LANES)),
            row_spec(TOP),
        ],
        out_specs=[
            row_spec(width),
            row_spec(width + LANES),
            row_spec(LANES),
        ],
        out_shape=[
            pltpu.HBM((rows, width), F32),
            pltpu.HBM((rows, width + LANES), BF),
            pltpu.HBM((rows, LANES), F32),
        ],
        compiler_params=params("arbitrary"),
        name="middle",
    )))(attended, attended_other, wo_mine, wo_other, full_tokens, w_small, route_rows)
    normed_two, peer_cot = arrive(weights[0], normed_two, peer_cot)
    (normed_two,) = segment(weights[1:], normed_two)
    peer_two = swap_core(normed_two, "normed_two")

    near = [(normed_two, BF), (full_cot, BF), (peer_two, BF), (peer_cot, BF)]
    sources = [in_hbm(array) for array, _ in near]
    wide_acc, acc_shape = (rows, width), (rows, width + LANES)
    count = len(places)

    def run_experts(g, call, accs, dw_parts):
        lead = 1 + count + 4 + len(accs)
        first_call, last_call = not accs, g + 1 == len(plan)
        call_size, start = plan[g][call], sum(plan[g][:call])
        column = sum(sum(sizes) for sizes in plan[:g]) + start
        kept = sum(sum(sizes) for sizes in (plan[1:] if g else plan[:1]))
        sums_start = column - sum(plan[0]) if g else start
        outs = pl.pallas_call(
            functools.partial(
                moe_kernel,
                first_call,
                last_call,
                bool(dw_parts),
                experts,
                column,
                start,
                sums_start,
                call_size,
                places,
            ),
            in_specs=[smem] + [any_spec] * (lead - 1 + len(dw_parts)),
            out_specs=[any_spec] * (3 + count),
            out_shape=[
                pltpu.HBM(acc_shape, F32),
                pltpu.HBM(acc_shape, BF if last_call else F32),
                pltpu.HBM((call_size, 2 * rows, hid), BF),
            ]
            + [pltpu.HBM((kept, r, 3 * hid), BF) for _, _, r in places],
            input_output_aliases={lead + j: 3 + j for j in range(len(dw_parts))},
            scratch_shapes=[pltpu.VMEM(array.shape, kind) for array, kind in near]
            + [pltpu.VMEM(acc_shape, F32)] * 2
            + [
                pltpu.VMEM((call_size, 2 * rows, hid), BF),
                pltpu.VMEM(acc_shape, BF),
                pltpu.VMEM((call_size, width, 3 * hid), BF),
                pltpu.VMEM((2, width, 3 * hid), BF),
                pltpu.SemaphoreType.DMA((call_size,)),
                pltpu.SemaphoreType.DMA((2,)),
                pltpu.SemaphoreType.DMA((4,)),
                pltpu.SemaphoreType.DMA((2,)),
                pltpu.SemaphoreType.DMA((2,)),
                pltpu.SemaphoreType.DMA(()),
            ],
            compiler_params=pltpu.CompilerParams(vmem_limit_bytes=MOE_VMEM),
            name="experts",
        )(
            part_where,
            *[in_hbm(block) for block in weights[g].parts],
            *sources,
            *accs,
            *dw_parts,
        )
        return outs[:2], outs[2], outs[3:]

    accs, mixed_parts, sums = (), [], []

    later = weights[1:]
    for call in range(len(plan[0])):
        if call:
            accs = segment(later, *accs)
            lead_parts = dw_parts
        accs, mixed, dw_parts = run_experts(0, call, accs, lead_parts if call else ())
        mixed_parts.append(mixed)
    sums.append(Scatter(ring, dw_parts, "sums_0"))
    dw_parts = ()
    for g in range(1, len(plan)):
        while weights[g].step < ring.size // 2 - 1:
            accs = segment(later, *accs)
        if not weights[g].done():
            accs = segment([weights[g]], *accs)
        accs = arrive(weights[g], *accs)
        accs = segment([*weights[g + 1 :], sums[0]], *accs)
        accs, mixed, dw_parts = run_experts(g, 0, accs, dw_parts)
        mixed_parts.append(mixed)
    sums.append(Scatter(ring, dw_parts, "sums_1"))

    grad_two, grad_two_peer = arrive(sums[0], *accs)
    part = pl.pallas_call(
        functools.partial(add_terms_kernel, experts),
        in_specs=[vmem] * 2,
        out_specs=vmem,
        out_shape=jax.ShapeDtypeStruct(acc_shape, BF),
        compiler_params=params(),
        name="add_terms",
    )(grad_two, swap_core(grad_two_peer, "grad_two"))
    (part,) = together(sums, part)
    part_other = swap_tp(part, "part")
    sums[0].prepare()
    for chain in sums:
        chain.send()

    moe, moe_peer = pl.pallas_call(
        functools.partial(moe_sum_kernel, places, plan),
        in_specs=[smem] + [any_spec] * (count * len(plan) + len(mixed_parts)),
        out_specs=[vmem] * 2,
        out_shape=[pltpu.HBM(wide_acc, F32), pltpu.HBM(wide_acc, BF)],
        scratch_shapes=[pltpu.VMEM((width, sum(sizes) * hid), BF) for sizes in plan]
        + [pltpu.VMEM((2 * rows, sum(sizes) * hid), BF) for sizes in plan]
        + [pltpu.SemaphoreType.DMA((len(plan),))] * 2,
        compiler_params=pltpu.CompilerParams(vmem_limit_bytes=MOE_VMEM),
        name="experts_output",
    )(
        part_where,
        *[in_hbm(block) for chain in weights for block in chain.parts],
        *lock(*[in_hbm(mixed) for mixed in mixed_parts], part)[: len(mixed_parts)],
    )

    moe, moe_peer = segment(sums[:1], moe, moe_peer)
    (part_other,) = arrive(sums[1], part_other)
    sums[1].prepare()
    part_other, moe_peer = together(sums[1:], part_other, moe_peer)
    from_core_moe = swap_core(moe_peer, "moe")

    grad_middle, grad_branch, grad_attended, grad_logits, gain_two_term = pl.pallas_call(
        functools.partial(middle_back_kernel, experts + 1),
        grid=(steps,),
        in_specs=[
            smem,
            row_spec(width + LANES),
            row_spec(width + LANES),
            row_spec(LANES),
            row_spec(width),
            row_spec(width),
            whole((width, LANES)),
            whole((width, q_width)),
        ],
        out_specs=[
            row_spec(feature),
            row_spec(width),
            row_spec(q_width),
            row_spec(LANES),
            whole((1, width)),
        ],
        out_shape=[
            pltpu.HBM((rows, feature), F32),
            jax.ShapeDtypeStruct((rows, width), BF),
            jax.ShapeDtypeStruct((rows, q_width), BF),
            jax.ShapeDtypeStruct((rows, LANES), BF),
            jax.ShapeDtypeStruct((1, width), F32),
        ],
        compiler_params=params("arbitrary"),
        name="middle_back",
    )(tp_scalar, part, part_other, gates, middle, full_cot, w_small, wo_mine)
    back_spec = pl.BlockSpec((deep, span, 2 * LANES), lambda s, p: (0, s, p))
    turn_spec = pl.BlockSpec((span, LANES), lambda s, p: (s, 0))
    grad_q, grad_kv_own, grad_kv_peer = pl.pallas_call(
        functools.partial(attend_back_kernel, ctx, span),
        grid=(seqs, pairs),
        in_specs=[prob_spec] + [head_spec()] * 2 + [turn_spec] * 2 + [head_spec()] * ctx,
        out_specs=[head_spec(), back_spec, back_spec],
        out_shape=[
            pltpu.HBM((rows, q_width), BF),
            pltpu.HBM((deep, rows, 2 * kv_width), BF),
            pltpu.HBM((deep, rows, 2 * kv_width), BF),
        ],
        compiler_params=params("arbitrary", "arbitrary"),
        name="attend_back",
    )(in_hbm(probs), queries, grad_attended, cosine, sine, *kv_blocks)
    grad_q, grad_kv_own, grad_kv_peer, from_core_moe = arrive(
        sums[0], grad_q, grad_kv_own, grad_kv_peer, from_core_moe
    )

    def to_owner(grad_kv_own, from_peer):
        travel = jnp.zeros(from_peer.shape[1:], BF)
        for k in range(deep - 1, 0, -1):
            piece = grad_kv_own[k] + from_peer[k]
            if k < deep - 1:
                piece = piece + travel
            travel = shift_y(piece, down_y, "grad_kv")
        return travel

    def weight_grads(name, sides, gain_terms, gain_at, cols):
        flat = [array for side in sides for array in side]
        return (pl.pallas_call(
                functools.partial(weight_grad_kernel, [len(side) for side in sides], gain_at),
                in_specs=[smem] + [vmem] * (len(flat) + len(gain_terms)),
                out_specs=[vmem] * 2,
                out_shape=[jax.ShapeDtypeStruct((n, shard, cols), BF)] * 2,
                compiler_params=params(),
                name=f"{name}_weight_grads",
            )
        )(core_scalar, *flat, *gain_terms)

    def close_experts(chain):
        own = chain.parts[0]
        shape = (own.shape[0], shard, 3 * hid)
        kept, sent = pl.pallas_call(
            close_experts_kernel,
            in_specs=[smem] + [vmem] * 3,
            out_specs=[vmem] * 2,
            out_shape=[jax.ShapeDtypeStruct(shape, F32), jax.ShapeDtypeStruct(shape, BF)],
            compiler_params=params(),
            name="close_experts",
        )(core_scalar, own, *chain.moving)
        return kept, sent

    (grad_kv_peer,) = together(sums[1:], grad_kv_peer)
    sums[1].send()
    from_peer = swap_core(grad_kv_peer, "grad_kv")
    early = weight_grads(
        "early",
        [[grad_branch], [attended], [normed], [grad_q], [normed_two], [grad_logits]],
        [gain_two_term],
        experts,
        2 * q_width + LANES,
    )
    travel = to_owner(grad_kv_own, from_peer)
    early = arrive(sums[1], *early)
    sums[1].prepare()
    sums[1].send()
    half_at = lambda array, side: lax.dynamic_slice_in_dim(array, side * feature, feature, 1)
    early_other = swap_core(early[1], "early")
    closed = [close_experts(sums[0])]
    moe_sum = moe + from_core_moe.astype(F32)
    moe_send = half_at(moe_sum, 1 - tp).astype(BF)
    moe_other = swap_tp(moe_send, "moe_send")
    travel, moe_other, *closed[0] = lock(travel, moe_other, *closed[0])
    shapes = [
        ((rows, 2 * kv_width), BF),
        ((rows, feature), F32),
        ((rows, feature + LANES), BF),
        ((rows, LANES), F32),
        ((1, width), F32),
    ]
    grad_kv, grad_own, grad_send, inner, gain_one_term = pl.pallas_call(
        functools.partial(project_back_kernel, pairs, experts, seqs),
        in_specs=[smem] + [vmem] * 9,
        out_specs=[vmem] * 5,
        out_shape=[jax.ShapeDtypeStruct(shape, kind) for shape, kind in shapes],
        compiler_params=params(),
        name="project_back",
    )(
        tp_scalar,
        grad_q,
        grad_kv_own,
        from_peer,
        travel,
        cosine,
        sine,
        w_qkv,
        full_tokens,
        w_small,
    )
    late = weight_grads(
        "late", [[normed], [grad_kv]], [gain_one_term], 0, 2 * kv_width + LANES
    )
    late_other = swap_core(late[1], "late")
    late_other, early_other = lock(late_other, early_other)
    cols = early_other.shape[2] + late_other.shape[2]
    last = Scatter(
        ring,
        pinned(pl.pallas_call(
            functools.partial(order_kernel, bundle_places),
            in_specs=[smem] + [vmem] * 4,
            out_specs=[vmem] * len(bundle_places),
            out_shape=[jax.ShapeDtypeStruct((1, r, cols), BF) for _, _, r in bundle_places],
            compiler_params=params(),
            name="order",
        ))(chip_list, early[0], early_other, late[0], late_other),
        "last",
    )
    (grad_send,) = together([last, sums[1]], grad_send)
    last.send()
    sums[1].prepare()
    together([last, sums[1]])
    sums[1].send()
    grad_other = swap_tp(grad_send, "grad_normed")
    segment([last])
    grad_tokens = pinned(
        pl.pallas_call(
            token_grads_kernel,
            in_specs=[vmem] * 5,
            out_specs=vmem,
            out_shape=pltpu.HBM((rows, feature), F32),
            compiler_params=params(),
            name="token_grads",
        )
    )(own_tokens, grad_own, inner, grad_other, grad_middle)
    output = (half_at(middle, tp) + half_at(moe_sum, tp) + moe_other.astype(F32)).astype(BF)
    grad_tokens, output = segment([last], grad_tokens, output)
    while not sums[1].done():
        segment(sums[1:])
    together([last, sums[1]])
    closed.append(close_experts(sums[1]))
    closed = [[kept, swap_core(sent, "expert_grads")] for kept, sent in closed]
    while not last.done():
        segment([last])
    arrive(last)
    widths = (("one", q_width), ("one", q_width), ("one", LANES), ("pairs", 2 * kv_width), ("one", LANES))
    out_term, grad_query, small_term, grad_key, grad_value, gain_term = (pinned(pl.pallas_call(
            functools.partial(close_weights_kernel, widths),
            in_specs=[vmem] * 3,
            out_specs=[vmem] * 6,
            out_shape=[
                jax.ShapeDtypeStruct((shard, w), F32)
                for w in (q_width, q_width, LANES, kv_width, kv_width, LANES)
            ],
            compiler_params=params(),
            name="close_weights",
        ))
    )(last.parts[0], *last.moving)
    grad_out = out_term.T
    grad_router = small_term[:, :experts]
    grad_gain_ffn = small_term[:, experts]
    gain_half = gain_term[:, 0]
    gain_other = swap_tp(gain_half, "gain")

    grad_gate, grad_up, down_term = (pl.pallas_call(
            functools.partial(expert_grads_kernel, len(sums)),
            in_specs=[smem] + [vmem] * (2 * len(sums)),
            out_specs=[vmem] * 3,
            out_shape=[pltpu.HBM((experts, shard, hid), F32)] * 3,
            compiler_params=params(),
            name="expert_grads",
        )
    )(
        core_scalar,
        *[closed[k][0] for k in range(len(sums))],
        *[closed[k][1] for k in range(len(sums))],
    )
    gain_other, grad_gate, grad_up, down_term = lock(gain_other, grad_gate, grad_up, down_term)
    grad_gain_attn = gain_half + gain_other
    grad_down = down_term.transpose(0, 2, 1)

    return (
        output.reshape(seqs, span, feature),
        grad_tokens.reshape(seqs, span, feature),
        grad_query,
        grad_key,
        grad_value,
        grad_out,
        grad_router,
        grad_gain_attn,
        grad_gain_ffn,
        grad_gate,
        grad_up,
        grad_down,
    )


def solution(mesh):
    in_specs = (
        P("fsdp", "ctx", "tp"),
        P("fsdp"),
        P("ctx", "fsdp", None, None),
        P(("fsdp", "ctx"), "tp"),
        P(("fsdp", "ctx"), "tp"),
        P(("fsdp", "ctx"), "tp"),
        P("tp", ("fsdp", "ctx")),
        P(("fsdp", "ctx"), None),
        P(("fsdp", "ctx")),
        P(("fsdp", "ctx")),
        P(None, ("fsdp", "ctx"), "tp"),
        P(None, ("fsdp", "ctx"), "tp"),
        P(None, "tp", ("fsdp", "ctx")),
        P("fsdp", "ctx", "tp"),
    )
    out_specs = (
        P("fsdp", "ctx", "tp"),
        P("fsdp", "ctx", "tp"),
        P(("fsdp", "ctx"), "tp"),
        P(("fsdp", "ctx"), "tp"),
        P(("fsdp", "ctx"), "tp"),
        P("tp", ("fsdp", "ctx")),
        P(("fsdp", "ctx"), None),
        P(("fsdp", "ctx")),
        P(("fsdp", "ctx")),
        P(None, ("fsdp", "ctx"), "tp"),
        P(None, ("fsdp", "ctx"), "tp"),
        P(None, "tp", ("fsdp", "ctx")),
    )
    return jax.shard_map(
        per_device, mesh=mesh, in_specs=in_specs, out_specs=out_specs, check_vma=False
    )
```

```python
import functools

import jax
import jax.numpy as jnp
from jax import lax
from jax.experimental import pallas as pl
from jax.experimental.pallas import tpu as pltpu
from jax.sharding import PartitionSpec as P

HD = 64
TOP = 8
LANES = 128

EPSILON = 1e-06
ATTN_SCALE = 0.015625
RESIDUAL_SCALE = 0.22
MASKED_SCORE = -1e30
RING = ("fsdp", "ctx")
BF = jnp.bfloat16
F32 = jnp.float32
VMEM_LIMIT = 24 * 1024 * 1024
MOE_VMEM = 56 * 1024 * 1024


def nt(a, b):
    return lax.dot_general(a, b, (((1,), (1,)), ((), ())), preferred_element_type=F32)


def nn(a, b):
    return lax.dot_general(a, b, (((1,), (0,)), ((), ())), preferred_element_type=F32)


def tn(a, b):
    return lax.dot_general(a, b, (((0,), (0,)), ((), ())), preferred_element_type=F32)


def params(*semantics):
    return pltpu.CompilerParams(
        dimension_semantics=semantics, vmem_limit_bytes=VMEM_LIMIT
    )


def whole(shape):
    zeros = (0,) * len(shape)
    return pl.BlockSpec(shape, lambda *_: zeros, pipeline_mode=pl.Buffered(1))


def swap_halves(slab):
    lane = lax.broadcasted_iota(jnp.int32, slab.shape, 1) % HD
    return jnp.where(
        lane < HD // 2, pltpu.roll(slab, LANES - HD // 2, 1), pltpu.roll(slab, HD // 2, 1)
    )


def column_as_row(ref, column):
    lane = lax.broadcasted_iota(jnp.int32, (16, ref.shape[1]), 1)
    return nt(jnp.where(lane == column, 1.0, 0.0).astype(BF), ref[...])[:1]


def pack_kernel(q_ref, k_ref, v_ref, out_ref, router_ref, one_ref, two_ref, packed_ref, *scratch):
    stage, sem = scratch
    rows, q_width = q_ref.shape
    copies, at = [], 0

    def copy(source, width):
        nonlocal at
        copies.append(pltpu.make_async_copy(source, packed_ref.at[0, :, pl.ds(at, width)], sem))
        copies[-1].start()
        at += width

    copy(q_ref, q_width)
    for pair in range(k_ref.shape[1] // LANES):
        cols = pl.ds(pair * LANES, LANES)
        copy(k_ref.at[:, cols], LANES)
        copy(v_ref.at[:, cols], LANES)
    copy(out_ref, q_width)
    experts = router_ref.shape[0]
    stage[...] = jnp.zeros(stage.shape, F32)
    stage[:experts, :rows] = router_ref[...].astype(F32)
    stage[experts : experts + 1, :rows] = one_ref[...].astype(F32)
    stage[experts + 1 : experts + 2, :rows] = two_ref[...].astype(F32)
    packed_ref[0, :, at:] = stage[...].T[:rows].astype(BF)
    for each in copies:
        each.wait()


def pack_experts_kernel(core_ref, gate_ref, up_ref, down_ref, mine_ref, other_ref, sem):
    count, _, cols = mine_ref.shape
    hid = cols // 3
    copies = []
    for out_ref, core in ((mine_ref, core_ref[0]), (other_ref, 1 - core_ref[0])):
        for i, source in enumerate((gate_ref, up_ref, down_ref)):
            copies.append(
                pltpu.make_async_copy(
                    source.at[pl.ds(core * count, count)],
                    out_ref.at[:, :, pl.ds(i * hid, hid)],
                    sem,
                )
            )
            copies[-1].start()
    for copy in copies:
        copy.wait()


def join_kernel(core_ref, mine_ref, other_ref, *groups):
    rows = mine_ref.shape[1]
    for mine_first in (True, False):

        @pl.when((core_ref[0] == 0) == mine_first)
        def _():
            at = 0
            for out_ref in groups:
                size = out_ref.shape[0]
                first, second = (mine_ref, other_ref) if mine_first else (other_ref, mine_ref)
                out_ref[:, :rows] = first[at : at + size]
                out_ref[:, rows:] = second[at : at + size]
                at += size


def assemble_kernel(places, where_ref, *refs):
    count = len(places)
    parts, outs, sem = refs[:count], refs[count:-1], refs[-1]

    def copies():
        for j, (_, _, rows) in enumerate(places):
            first = 0
            for out in outs:
                cols = out.shape[1]
                yield pltpu.make_async_copy(
                    parts[j].at[0, :, pl.ds(first, cols)],
                    out.at[pl.ds(pl.multiple_of(where_ref[j], 16), rows)],
                    sem,
                )
                first += cols

    for copy in copies():
        copy.start()
    for copy in copies():
        copy.wait()


def side_by_side(tp_ref, mine, other):
    first = tp_ref[0] == 0
    return jnp.concatenate([jnp.where(first, mine, other), jnp.where(first, other, mine)], axis=1)


def features_kernel(tp_ref, mine_ref, other_ref, full_ref):
    full_ref[...] = side_by_side(tp_ref, mine_ref[...], other_ref[...])


def project_kernel(
    pairs,
    q_width,
    gain_col,
    tp_ref,
    mine_ref,
    other_ref,
    small_ref,
    w_ref,
    cos_ref,
    sin_ref,
    x_ref,
    n_ref,
    q_ref,
    kv_ref,
):
    x_ref[...] = side_by_side(tp_ref, mine_ref[...], other_ref[...])
    x = x_ref[...].astype(F32)
    gain = column_as_row(small_ref, gain_col)
    scale = lax.rsqrt(jnp.mean(x * x, axis=1, keepdims=True) + EPSILON)
    normed = (x * scale * gain).astype(BF)
    n_ref[...] = normed
    cosine, sine = cos_ref[...], sin_ref[...]
    raw = nn(normed, w_ref[...])
    for slab in range(q_width // LANES):
        cols = slice(slab * LANES, (slab + 1) * LANES)
        part = raw[:, cols]
        turned = (part * cosine + swap_halves(part) * sine).astype(BF)
        q_ref[:, cols] = (turned.astype(F32) * ATTN_SCALE).astype(BF)
    for pair in range(pairs):
        lo = pair * 2 * LANES
        part = raw[:, q_width + lo : q_width + lo + LANES]
        kv_ref[:, lo : lo + LANES] = (part * cosine + swap_halves(part) * sine).astype(BF)
        kv_ref[:, lo + LANES : lo + 2 * LANES] = raw[
            :, q_width + lo + LANES : q_width + lo + 2 * LANES
        ].astype(BF)


def attend_kernel(blocks, span, prefix_ref, base_ref, q_ref, *refs):
    kv_refs = refs[:blocks]
    out_ref, p_ref = refs[blocks:]
    limit_len = prefix_ref[pl.program_id(0)]
    local = base_ref[0] + lax.broadcasted_iota(jnp.int32, (span, 1), 0)
    limit = jnp.maximum(local + 1, limit_len)
    key_pos = jnp.concatenate(
        [
            base_ref[j] + lax.broadcasted_iota(jnp.int32, (1, span), 1)
            for j in range(blocks)
        ],
        axis=1,
    )
    visible = key_pos < limit
    visible = jnp.concatenate([visible, visible], axis=0)
    for g in range(2):
        keys = jnp.concatenate([r[:, g * HD : (g + 1) * HD] for r in kv_refs], axis=0)
        vals = jnp.concatenate(
            [r[:, LANES + g * HD : LANES + (g + 1) * HD] for r in kv_refs], axis=0
        )
        first, second = 2 * g * HD, (2 * g + 1) * HD
        queries = jnp.concatenate(
            [q_ref[:, first : first + HD], q_ref[:, second : second + HD]], axis=0
        )
        scores = jnp.where(visible, nt(queries, keys), MASKED_SCORE)
        expo = jnp.exp(scores - jnp.max(scores, axis=1, keepdims=True))
        probs = (expo * (1.0 / jnp.sum(expo, axis=1, keepdims=True))).astype(BF)
        p_ref[0, g] = probs
        att = nn(probs, vals).astype(BF)
        out_ref[:, first : first + HD] = att[:span]
        out_ref[:, second : second + HD] = att[span:]


def attend_back_kernel(blocks, span, p_ref, q_ref, g_ref, cos_ref, sin_ref, *refs):
    kv_refs = refs[:blocks]
    dq_ref, own_ref, other_ref = refs[-3:]
    cosine, sine = cos_ref[...], sin_ref[...]
    parts = []
    for g in range(2):
        keys = jnp.concatenate([r[:, g * HD : (g + 1) * HD] for r in kv_refs], axis=0)
        vals = jnp.concatenate(
            [r[:, LANES + g * HD : LANES + (g + 1) * HD] for r in kv_refs], axis=0
        )
        first, second = 2 * g * HD, (2 * g + 1) * HD
        queries = jnp.concatenate(
            [q_ref[:, first : first + HD], q_ref[:, second : second + HD]], axis=0
        )
        grads = jnp.concatenate(
            [g_ref[:, first : first + HD], g_ref[:, second : second + HD]], axis=0
        )
        probs = p_ref[0, g]
        wide = probs.astype(F32)
        grad_probs = nt(grads, vals)
        inner = jnp.sum(wide * grad_probs, axis=1, keepdims=True)
        grad_scores = (wide * (grad_probs - inner)).astype(BF)
        dq = nn(grad_scores, keys) * ATTN_SCALE
        slab = jnp.concatenate([dq[:span], dq[span:]], axis=1)
        turned = slab * cosine - swap_halves(slab) * sine
        dq_ref[:, first : first + LANES] = turned.astype(BF)
        parts.append((nn(queries.T, grad_scores), nn(grads.T, probs)))
    stacked = jnp.concatenate([parts[0][0], parts[1][0], parts[0][1], parts[1][1]], axis=0)
    turned = stacked.T.astype(BF)
    half = blocks // 2
    for j in range(half):
        own_ref[j] = turned[j * span : (j + 1) * span]
        other_ref[j] = turned[(half + j) * span : (half + j + 1) * span]


def middle_kernel(
    gain_col, a_ref, b_ref, wa_ref, wb_ref, x_ref, small_ref, routes_ref, m_ref, n_ref, g_ref
):
    branch = nt(a_ref[...], wa_ref[...]) + nt(b_ref[...], wb_ref[...])
    middle = x_ref[...].astype(F32) + RESIDUAL_SCALE * branch
    m_ref[...] = middle
    scale = lax.rsqrt(jnp.mean(middle * middle, axis=1, keepdims=True) + EPSILON)
    wide = middle * scale * column_as_row(small_ref, gain_col)
    normed = wide.astype(BF)
    width = normed.shape[1]
    n_ref[:, :width] = normed
    logits = nn(normed, small_ref[...])
    lane = lax.broadcasted_iota(jnp.int32, logits.shape, 1)
    routes = routes_ref[...]
    routed = lane == routes[:, 0:1]
    for k in range(1, TOP):
        routed = routed | (lane == routes[:, k : k + 1])
    logits = jnp.where(routed, logits, MASKED_SCORE)
    expo = jnp.where(routed, jnp.exp(logits - jnp.max(logits, axis=1, keepdims=True)), 0.0)
    gates = expo / jnp.sum(expo, axis=1, keepdims=True)
    g_ref[...] = gates
    n_ref[:, width:] = in_two(gates, gain_col - 1)


def in_two(pull, experts):
    high = pull.astype(BF).astype(F32)
    return (high + pltpu.roll(pull - high, experts, 1)).astype(BF)


def in_one(terms, experts):
    wide = terms.astype(F32)
    lane = lax.broadcasted_iota(jnp.int32, wide.shape, 1)
    both = wide + pltpu.roll(wide, LANES - experts, 1)
    return jnp.where(lane < experts, both, 0.0)


def moe_kernel(
    first_call, last_call, joins, experts, column, start, sums_start, group, places, where_ref, *refs
):
    count = len(places)
    w_parts, refs = refs[:count], refs[count:]
    sources, refs = refs[:4], refs[4:]
    inits, refs = ((), refs) if first_call else (refs[:2], refs[2:])
    refs = refs[count:] if joins else refs
    outs, mixed_out, dw_parts, refs = refs[:2], refs[2], refs[3 : 3 + count], refs[3 + count :]
    here, accs, refs = refs[:4], refs[4:6], refs[6:]
    mixed_all, narrow, w_all, dw_all, w_sem, dw_sem, near_sem, acc_sem, out_sem, mixed_sem = refs
    xa_ref, ya_ref, xb_ref, yb_ref = here
    rows, width = ya_ref.shape
    hid = w_all.shape[2] // 3

    def window(j):
        return pl.ds(pl.multiple_of(where_ref[1 + j], 16), places[j][2])

    def load(e, j):
        return pltpu.make_async_copy(
            w_parts[j].at[start + e], w_all.at[e, window(j)], w_sem.at[e]
        )

    def store(e, j):
        return pltpu.make_async_copy(
            dw_all.at[e % 2, window(j)], dw_parts[j].at[sums_start + e], dw_sem.at[e % 2]
        )

    nears = [
        pltpu.make_async_copy(a, b, near_sem.at[i]) for i, (a, b) in enumerate(zip(sources, here))
    ]
    fetches = [
        pltpu.make_async_copy(a, b, acc_sem.at[i]) for i, (a, b) in enumerate(zip(inits, accs))
    ]
    mixed_store = pltpu.make_async_copy(mixed_all, mixed_out, mixed_sem)
    for j in range(count):
        load(0, j).start()
    for copy in nears[:2]:
        copy.start()
    results = []
    for e in range(group):
        for j in range(count):
            load(e, j).wait()
        if e == 0:
            for copy in nears[:2]:
                copy.wait()
            for copy in [*fetches[:1], *nears[2:], *fetches[1:]]:
                copy.start()
        expert = where_ref[0] + column + e
        w_gu, w_d = w_all[e, :, : 2 * hid], w_all[e, :, 2 * hid :]
        kept = []
        for side, (x_ref, y_ref) in enumerate(((xa_ref, ya_ref), (xb_ref, yb_ref))):
            acc = accs[side]
            if e == 0 and side == 1:
                for copy in nears[2:]:
                    copy.wait()
                for other in range(1, group):
                    for j in range(count):
                        load(other, j).start()
            pre = nn(x_ref[:, :width], w_gu)
            back = nn(y_ref[...], w_d)
            gates = in_one(x_ref[:, width:], experts)
            lane = lax.broadcasted_iota(jnp.int32, gates.shape, 1)
            mask = lane == expert
            weight = RESIDUAL_SCALE * jnp.sum(
                jnp.where(mask, gates, 0.0), axis=1, keepdims=True
            )
            gate_pre, up_pre = pre[:, :hid], pre[:, hid:]
            sig = jax.nn.sigmoid(gate_pre)
            act = gate_pre * sig
            hidden = act * up_pre
            pull = RESIDUAL_SCALE * jnp.sum(back * hidden, axis=1, keepdims=True)
            scaled = weight * back
            d_up = scaled * act
            d_gate = scaled * up_pre * (sig + act * (1.0 - sig))
            d_gu = jnp.concatenate([d_gate.astype(BF), d_up.astype(BF)], axis=1)
            mixed = (weight * hidden).astype(BF)
            mixed_all[e, side * rows : (side + 1) * rows] = mixed
            if first_call and e == 0:
                acc[:, :width] = nt(d_gu, w_gu)
                acc[:, width:] = jnp.where(mask, pull, 0.0)
            else:
                if e == 0:
                    fetches[side].wait()
                acc[:, :width] += nt(d_gu, w_gu)
                acc[:, width:] += jnp.where(mask, pull, 0.0)
            kept.append((d_gu, mixed))
            if e == group - 1:
                if last_call and side:
                    narrow[:, :width] = acc[:, :width].astype(BF)
                    narrow[:, width:] = in_two(acc[:, width:], experts)
                    acc = narrow
                results.append(pltpu.make_async_copy(acc, outs[side], out_sem.at[side]))
                results[-1].start()
        if e == group - 1:
            mixed_store.start()
        dw_gu = tn(xa_ref[:, :width], kept[0][0]) + tn(xb_ref[:, :width], kept[1][0])
        dw_d = tn(ya_ref[...], kept[0][1]) + tn(yb_ref[...], kept[1][1])
        if e >= 2:
            for j in range(count):
                store(e - 2, j).wait()
        dw_all[e % 2, :, : 2 * hid] = dw_gu.astype(BF)
        dw_all[e % 2, :, 2 * hid :] = dw_d.astype(BF)
        for j in range(count):
            store(e, j).start()
    for e in range(max(0, group - 2), group):
        for j in range(count):
            store(e, j).wait()
    for copy in results:
        copy.wait()
    mixed_store.wait()


def moe_sum_kernel(places, plan, where_ref, *refs):
    count, sets = len(places), len(plan)
    w_sets = [refs[k * count : (k + 1) * count] for k in range(sets)]
    refs = refs[sets * count :]
    calls = sum(len(sizes) for sizes in plan)
    mixed_parts, refs = refs[:calls], refs[calls:]
    own_ref, peer_ref, refs = refs[0], refs[1], refs[2:]
    w_all, mixed_all, (w_sem, mixed_sem) = refs[:sets], refs[sets : 2 * sets], refs[2 * sets :]
    rows = own_ref.shape[0]

    def loads(k):
        hid = w_all[k].shape[1] // sum(plan[k])
        at = 0
        for call, size in enumerate(plan[k]):
            source = mixed_parts[sum(len(sizes) for sizes in plan[:k]) + call]
            for i in range(size):
                cols = pl.ds(at * hid, hid)
                for j in range(count):
                    window = pl.ds(pl.multiple_of(where_ref[1 + j], 16), places[j][2])
                    yield pltpu.make_async_copy(
                        w_sets[k][j].at[at, :, pl.ds(2 * hid, hid)],
                        w_all[k].at[window, cols],
                        w_sem.at[k],
                    )
                yield pltpu.make_async_copy(
                    source.at[i], mixed_all[k].at[:, cols], mixed_sem.at[k]
                )
                at += 1

    for k in range(sets):
        for copy in loads(k):
            copy.start()
    total = None
    for k in range(sets):
        for copy in loads(k):
            copy.wait()
        term = nt(mixed_all[k][...], w_all[k][...])
        total = term if total is None else total + term
    own_ref[...] = total[:rows]
    peer_ref[...] = total[rows:].astype(BF)


def weight_grad_kernel(counts, gain_at, core_ref, *refs):
    sides = []
    for size in counts:
        sides.append(jnp.concatenate([ref[...] for ref in refs[:size]], axis=0))
        refs = refs[size:]
    gain_refs, (kept_ref, sent_ref) = refs[:-2], refs[-2:]
    n, shard, _ = kept_ref.shape
    width = 2 * n * shard
    terms = [tn(left[:, :width], right) for left, right in zip(sides[::2], sides[1::2])]
    if gain_refs:
        if terms[-1].shape[1] != LANES:
            terms.append(jnp.zeros((width, LANES), F32))
        row = lax.broadcasted_iota(jnp.int32, (8, LANES), 0)
        lane = lax.broadcasted_iota(jnp.int32, (8, LANES), 1)
        place = jnp.where((row == 0) & (lane == gain_at), 1.0, 0.0)
        gain = sum(ref[...] for ref in gain_refs)
        terms[-1] = terms[-1] + tn(jnp.broadcast_to(gain, (8, width)), place)
    first = 0
    for term in terms:
        cols = term.shape[1]
        parts = term.astype(BF).reshape(n, 2, shard, cols)
        for mine in range(2):

            @pl.when(core_ref[0] == mine)
            def _():
                kept_ref[:, :, first : first + cols] = parts[:, mine]
                sent_ref[:, :, first : first + cols] = parts[:, 1 - mine]

        first += cols


def order_kernel(places, chips_ref, *refs):
    count = len(places)
    pairs, parts = refs[:-count], refs[-count:]
    for j, (_, row, rows) in enumerate(places):
        chip = chips_ref[j]
        window = pl.ds(row, rows)
        first = 0
        for kept_ref, other_ref in zip(pairs[::2], pairs[1::2]):
            cols = kept_ref.shape[2]
            parts[j][0, :, first : first + cols] = kept_ref[chip, window] + other_ref[chip, window]
            first += cols


def add_terms_kernel(experts, own_ref, peer_ref, *sum_refs):
    width = own_ref.shape[1] - LANES
    rows = own_ref.shape[0] // len(sum_refs)
    for s, sum_ref in enumerate(sum_refs):
        span = slice(s * rows, (s + 1) * rows)
        total = own_ref[span, :width] + peer_ref[span, :width].astype(F32)
        sum_ref[:, :width] = total.astype(BF)
        pull = own_ref[span, width:] + in_one(peer_ref[span, width:], experts)
        sum_ref[:, width:] = in_two(pull, experts)


def close_experts_kernel(core_ref, own_ref, ahead_ref, back_ref, kept_ref, sent_ref):
    rows = kept_ref.shape[1]
    total = own_ref[...].astype(F32) + ahead_ref[...].astype(F32) + back_ref[...].astype(F32)
    is_first = core_ref[0] == 0
    kept_ref[...] = jnp.where(is_first, total[:, :rows], total[:, rows:])
    sent_ref[...] = jnp.where(is_first, total[:, rows:], total[:, :rows]).astype(BF)


def expert_grads_kernel(chains, core_ref, *refs):
    kept_refs, sent_refs, outs = refs[:chains], refs[chains : 2 * chains], refs[2 * chains :]
    count, _, cols = kept_refs[0].shape
    hid = cols // 3
    for k in range(chains):
        for ref, core in ((kept_refs[k], core_ref[0]), (sent_refs[k], 1 - core_ref[0])):
            for i in range(count):
                at = core * chains * count + k * count + i
                for part, out in enumerate(outs):
                    out[at] = ref[i, :, part * hid : (part + 1) * hid].astype(F32)


def close_weights_kernel(widths, own_ref, ahead_ref, back_ref, *outs):
    def total(cols):
        return (
            own_ref[0, :, cols].astype(F32)
            + ahead_ref[0, :, cols].astype(F32)
            + back_ref[0, :, cols].astype(F32)
        )

    first = 0
    for kind, width in widths:
        if kind == "pairs":
            for pair in range(width // (2 * LANES)):
                for side in range(2):
                    lo = first + (2 * pair + side) * LANES
                    outs[side][:, pair * LANES : (pair + 1) * LANES] = total(slice(lo, lo + LANES))
            outs = outs[2:]
        else:
            outs[0][...] = total(slice(first, first + width))
            outs = outs[1:]
        first += width


def token_grads_kernel(x_ref, own_ref, dot_ref, other_ref, *refs):
    middles, out_ref = refs[:-1], refs[-1]
    feature = x_ref.shape[1]
    span = middles[0].shape[0]
    for s, middle_ref in enumerate(middles):
        at = slice(s * span, (s + 1) * span)
        other = other_ref[at]
        dot = dot_ref[at, :1] + in_one(other[:, feature:], 1)[:, :1]
        total = middle_ref[...] + own_ref[at] + other[:, :feature].astype(F32)
        out_ref[at] = total - x_ref[at].astype(F32) * dot


def middle_back_kernel(
    gain_col,
    tp_ref,
    sa_ref,
    sb_ref,
    gates_ref,
    m_ref,
    y_ref,
    small_ref,
    wo_ref,
    gm_ref,
    branch_ref,
    att_ref,
    logit_ref,
    dgain_ref,
):
    @pl.when(pl.program_id(0) == 0)
    def _():
        dgain_ref[...] = jnp.zeros(dgain_ref.shape, F32)

    gates = gates_ref[...]
    width = m_ref.shape[1]
    pull = in_one(sa_ref[:, width:], gain_col - 1) + in_one(sb_ref[:, width:], gain_col - 1)
    weighted = gates * pull
    grad_logits = (weighted - gates * jnp.sum(weighted, axis=1, keepdims=True)).astype(BF)
    logit_ref[...] = grad_logits
    grad = sa_ref[:, :width].astype(F32) + sb_ref[:, :width].astype(F32)
    grad = grad + nt(grad_logits, small_ref[...])
    middle = m_ref[...]
    scale = lax.rsqrt(jnp.mean(middle * middle, axis=1, keepdims=True) + EPSILON)
    unit = middle * scale
    dgain_ref[...] += jnp.sum(grad * unit, axis=0, keepdims=True)
    scaled = grad * column_as_row(small_ref, gain_col)
    inner = jnp.sum(scaled * unit, axis=1, keepdims=True) * (1.0 / width)
    grad_middle = y_ref[...].astype(F32) + scale * (scaled - unit * inner)
    half = width // 2
    gm_ref[...] = jnp.where(tp_ref[0] == 0, grad_middle[:, :half], grad_middle[:, half:])
    branch = (RESIDUAL_SCALE * grad_middle).astype(BF)
    branch_ref[...] = branch
    att_ref[...] = nn(branch, wo_ref[...]).astype(BF)


def project_back_kernel(pairs, gain_col, seqs, tp_ref, *refs):
    dq_ref, kva_ref, kvb_ref, kvc_ref, cos_ref, sin_ref, w_ref, x_ref, small_ref = refs[:9]
    d_ref, own_ref, other_ref, dot_ref, dgain_ref = refs[9:]
    gain = column_as_row(small_ref, gain_col)
    is_first = tp_ref[0] == 0
    rows, q_width = dq_ref.shape
    span = rows // seqs
    for s in range(seqs):
        at = slice(s * span, (s + 1) * span)
        cosine, sine = cos_ref[at], sin_ref[at]
        kv = kva_ref[0, at].astype(F32) + kvb_ref[0, at].astype(F32) + kvc_ref[at].astype(F32)
        for pair in range(pairs):
            lo = pair * 2 * LANES
            part = kv[:, lo : lo + LANES]
            d_ref[at, lo : lo + LANES] = (part * cosine - swap_halves(part) * sine).astype(BF)
            d_ref[at, lo + LANES : lo + 2 * LANES] = kv[:, lo + LANES : lo + 2 * LANES].astype(BF)
        grad = nt(dq_ref[at], w_ref[:, :q_width]) + nt(d_ref[at], w_ref[:, q_width:])
        x = x_ref[at].astype(F32)
        width = x.shape[1]
        scale = lax.rsqrt(jnp.mean(x * x, axis=1, keepdims=True) + EPSILON)
        unit = x * scale
        term = jnp.sum(grad * unit, axis=0, keepdims=True)
        if s == 0:
            dgain_ref[...] = term
        else:
            dgain_ref[...] += term
        scaled = grad * gain
        inner = jnp.sum(scaled * unit, axis=1, keepdims=True) * (1.0 / width) * scale * scale
        lane = lax.broadcasted_iota(jnp.int32, (span, LANES), 1)
        dot = jnp.where(lane == 0, inner, 0.0)
        dot_ref[at] = dot
        scaled = scaled * scale
        half = width // 2
        own_ref[at] = jnp.where(is_first, scaled[:, :half], scaled[:, half:])
        other_ref[at, :half] = jnp.where(is_first, scaled[:, half:], scaled[:, :half]).astype(BF)
        other_ref[at, half:] = in_two(dot, 1)


class Ring:
    def __init__(self, wide, ctx):
        self.wide, self.ctx, self.deep = wide, ctx, ctx // 2
        self.size = wide * self.deep
        deep = self.deep
        order = [
            (f, y)
            for y in range(deep)
            for f in (range(wide) if y % 2 == 0 else range(wide - 1, -1, -1))
        ]
        flat = [[f * ctx + y * 2 + c for f, y in order] for c in range(2)]
        n = self.size
        self.forward = [(row[i], row[(i + 1) % n]) for row in flat for i in range(n)]
        self.backward = [(b, a) for a, b in self.forward]
        f, c = lax.axis_index("fsdp"), lax.axis_index("ctx")
        y = c // 2
        self.place = y * wide + jnp.where(y % 2 == 0, f, wide - 1 - f)

    def chip(self, offset):
        place = (self.place + offset) % self.size
        y, q = place // self.wide, place % self.wide
        f = jnp.where(y % 2 == 0, q, self.wide - 1 - q)
        return f * self.deep + y

    def send(self, array, forward=True):
        return lax.ppermute(array, RING, self.forward if forward else self.backward)

    def places(self, rows):
        far, half = self.size // 2, rows // 2
        found = [(0, 0, rows)]
        for step in range(1, far):
            found += [(-step, 0, rows), (step, 0, rows)]
        if half % 16:
            return found + [(-far, 0, rows)]
        return found + [(-far, 0, half), (far, half, half)]


class Gather:
    def __init__(self, ring, block, name):
        self.ring, self.step, self.rows, self.name = ring, 0, block.shape[1], name
        self.moving = (block, block)
        self.parts = [block]

    def prepare(self):
        if self.step == self.ring.size // 2 - 1:
            half = self.rows // 2
            ahead, back = self.moving
            self.moving = (ahead[:, :half], back[:, half:]) if half % 16 == 0 else (ahead,)

    def send(self):
        self.step += 1
        with jax.named_scope(f"{self.name}_step_{self.step}"):
            self.moving = tuple(
                self.ring.send(array, i == 0) for i, array in enumerate(self.moving)
            )
        self.parts += self.moving

    def done(self):
        return self.step == self.ring.size // 2


class Scatter:
    def __init__(self, ring, parts, name):
        self.ring, self.parts, self.step, self.name = ring, parts, 0, name
        self.far = ring.size // 2
        self.halved = len(parts) == ring.size + 1
        self.moving = (parts[-2], parts[-1]) if self.halved else (parts[-1],)

    def prepare(self):
        if self.step:
            s = self.far - self.step
            self.moving = add_pair(self.parts[2 * s], self.parts[2 * s - 1], *self.moving)

    def send(self):
        self.step += 1
        with jax.named_scope(f"{self.name}_step_{self.step}"):
            self.moving = tuple(
                self.ring.send(array, i == 0) for i, array in enumerate(self.moving)
            )

    def done(self):
        return self.step == self.far


def add_pair_kernel(near_ref, behind_ref, *refs):
    moved, outs = refs[:-2], refs[-2:]
    rows = near_ref.shape[1]
    for i, (mine, out) in enumerate(zip((near_ref, behind_ref), outs)):
        if i >= len(moved):
            out[...] = mine[...]
            continue
        came = moved[i]
        size = came.shape[1]
        at = slice(0, size) if i == 0 else slice(rows - size, rows)
        total = (mine[:, at].astype(F32) + came[...].astype(F32)).astype(BF)
        if size == rows:
            out[...] = total
        else:
            rest = slice(size, rows) if i == 0 else slice(0, rows - size)
            out[:, at] = total
            out[:, rest] = mine[:, rest]


def add_pair(near, behind, *moved):
    def spec(array):
        return pl.BlockSpec((1,) + array.shape[1:], lambda i: (i, 0, 0))

    arrays = (near, behind, *moved)
    out = jax.ShapeDtypeStruct(near.shape, BF)
    return pl.pallas_call(
        add_pair_kernel,
        grid=(near.shape[0],),
        in_specs=[spec(array) for array in arrays],
        out_specs=[spec(near)] * 2,
        out_shape=[out] * 2,
        compiler_params=params("arbitrary"),
        name="add_pair",
    )(*arrays)


def pinned(call):
    def run(*args):
        return call(
            *[
                pltpu.with_memory_space_constraint(a, pltpu.HBM)
                if a.ndim > 1 and a.dtype != jnp.int32
                else a
                for a in args
            ]
        )

    return run


def lock(*values):
    return lax.optimization_barrier(values)


def per_device(
    tokens,
    prefix,
    routes,
    w_query,
    w_key,
    w_value,
    w_out,
    w_router,
    gain_attn,
    gain_ffn,
    w_gate,
    w_up,
    w_down,
    cotangent,
):
    wide, ctx = lax.axis_size("fsdp"), lax.axis_size("ctx")
    seqs, span, feature = tokens.shape
    rows = seqs * span
    width = 2 * feature
    shard = w_query.shape[0]
    experts = w_router.shape[1]
    per_core = experts // 2
    hid = w_gate.shape[2]
    q_width, kv_width = w_query.shape[1], w_key.shape[1]
    pairs = kv_width // LANES
    deep = ctx // 2
    quarter = per_core // 4
    plan = ((quarter, quarter), (quarter,), (per_core - 3 * quarter,))
    tp, c = lax.axis_index("tp"), lax.axis_index("ctx")
    core, y = c % 2, c // 2
    ring = Ring(wide, ctx)
    n = ring.size
    core_perm = [(i, i ^ 1) for i in range(ctx)]

    def swap_core(array, name="rows"):
        with jax.named_scope(f"{name}_over_core"):
            return lax.ppermute(array, "ctx", core_perm)

    def swap_tp(array, name="rows"):
        with jax.named_scope(f"{name}_over_tp"):
            return lax.ppermute(array, "tp", [(0, 1), (1, 0)])

    up_y = [(i, (i + 2) % ctx) for i in range(ctx)]
    down_y = [(i, (i - 2) % ctx) for i in range(ctx)]

    def shift_y(array, perm, name):
        with jax.named_scope(f"{name}_over_y"):
            return lax.ppermute(array, "ctx", perm)

    tp_scalar = tp.astype(jnp.int32).reshape(1)

    def by_core(mine, other, axis):
        return jnp.where(
            core == 0,
            jnp.concatenate([mine, other], axis),
            jnp.concatenate([other, mine], axis),
        )

    vmem = pl.BlockSpec(memory_space=pltpu.VMEM)
    smem = pl.BlockSpec(memory_space=pltpu.SMEM)
    any_spec = pl.BlockSpec(memory_space=pl.ANY)
    qkv_width = q_width + 2 * kv_width
    in_hbm = lambda array: pltpu.with_memory_space_constraint(array, pltpu.HBM)
    small_rows = max(shard, LANES)
    bundle = pl.pallas_call(
        pack_kernel,
        in_specs=[any_spec] * 4 + [vmem] * 3,
        out_specs=vmem,
        out_shape=jax.ShapeDtypeStruct((1, shard, qkv_width + q_width + LANES), BF),
        scratch_shapes=[pltpu.VMEM((LANES, small_rows), F32), pltpu.SemaphoreType.DMA(())],
        compiler_params=params(),
        name="pack",
    )(
        *[in_hbm(w) for w in (w_query, w_key, w_value, w_out.T)],
        w_router.T,
        gain_attn[None],
        gain_ffn[None],
    )
    own_tokens = tokens.reshape(rows, feature)
    own_cot = cotangent.reshape(rows, feature)
    core_scalar = core.astype(jnp.int32).reshape(1)
    def segment(ticks, *values):
        chains = [chain for chain in ticks if not chain.done()]

        values = together(chains, *values)
        if any(chain.step for chain in chains):
            for chain in chains:
                chain.prepare()
            values = together(chains, *values)
        for chain in chains:
            chain.send()
        return values

    def together(chains, *values):
        held = [array for chain in chains for array in chain.moving]
        out = lock(*held, *values)
        at = 0
        for chain in chains:
            size = len(chain.moving)
            chain.moving = tuple(out[at : at + size])
            at += size
        return out[at:]

    def arrive(chain, *values):
        return together([chain], *values)

    first = Gather(ring, bundle, "bundle")
    half_shape = jax.ShapeDtypeStruct((per_core, shard, 3 * hid), BF)
    *raw_w, own_tokens, bundle = segment(
        [first], w_gate, w_up, w_down.transpose(0, 2, 1), own_tokens, bundle
    )
    mine_w, other_w = pl.pallas_call(
        pack_experts_kernel,
        in_specs=[smem] + [any_spec] * 3,
        out_specs=[vmem] * 2,
        out_shape=[half_shape] * 2,
        scratch_shapes=[pltpu.SemaphoreType.DMA(())],
        compiler_params=params(),
        name="pack_experts",
    )(core_scalar, *[in_hbm(w) for w in raw_w])
    from_core = [swap_core(bundle, "bundle")]
    other_w = swap_core(other_w, "experts")
    from_core[0], other_w, mine_w = segment([first], from_core[0], other_w, mine_w)
    blocks_w = list(
        pl.pallas_call(
            join_kernel,
            in_specs=[smem] + [vmem] * 2,
            out_specs=[vmem] * len(plan),
            out_shape=[
                jax.ShapeDtypeStruct((sum(sizes), 2 * shard, 3 * hid), BF) for sizes in plan
            ],
            compiler_params=params(),
            name="join",
        )(core_scalar, mine_w, other_w)
    )
    half_width = HD // 2
    freqs = 10000.0 ** (-jnp.arange(half_width, dtype=F32) / half_width)
    local_pos = c * span + jnp.arange(span, dtype=jnp.int32)
    angles = local_pos.astype(F32)[:, None] * freqs[None, :]
    cosine, sine = jnp.cos(angles), jnp.sin(angles)
    cosine = jnp.tile(jnp.concatenate([cosine] * 4, axis=1), (seqs, 1))
    sine = jnp.tile(jnp.concatenate([-sine, sine, -sine, sine], axis=1), (seqs, 1))
    chips = [ring.chip(d) for d, _, _ in ring.places(shard)]
    chip_list = jnp.stack(chips).astype(jnp.int32)
    bundle_places = ring.places(shard)
    bundle_rows = [
        (chips[j] * 2 + side) * shard + row
        for side in (core, 1 - core)
        for j, (_, row, _) in enumerate(bundle_places)
    ]
    bundle_where = jnp.stack(bundle_rows).astype(jnp.int32)
    places = ring.places(2 * shard)
    part_rows = [ring.chip(d) * 2 * shard + row for d, row, _ in places]
    part_where = jnp.stack([core * per_core] + part_rows).astype(jnp.int32)
    base = jnp.stack(
        [(((y - k) % deep) * 2 + core) * span for k in range(deep)]
        + [(((y - k) % deep) * 2 + 1 - core) * span for k in range(deep)]
    ).astype(jnp.int32)
    other_tokens = swap_tp(own_tokens, "tokens")
    shared = 1
    while not first.done():
        fresh = [swap_core(part, "part") for part in first.parts[shared : first.step * 2 - 1]]
        shared += len(fresh)
        last_step = first.step == ring.size // 2 - 1
        *fresh, blocks_w[0], cosine, sine, chip_list, bundle_where, part_where, base, tokens_here = segment(
            [first],
            *fresh,
            blocks_w[0],
            cosine,
            sine,
            chip_list,
            bundle_where,
            part_where,
            base,
            other_tokens if last_step else own_tokens,
        )
        if last_step:
            other_tokens = tokens_here
        from_core += fresh
    weights = [Gather(ring, block, f"weights_{i}") for i, block in enumerate(blocks_w)]
    rest = [swap_core(part, "part") for part in first.parts[shared:-2]]
    other_cot = swap_tp(own_cot, "cotangent")
    *rest, other_cot, weights[0].moving = arrive(
        first, *rest, other_cot, weights[0].moving[0]
    )
    weights[0].moving = (weights[0].moving,) * 2
    weights[0].send()
    from_core += rest
    rest = [swap_core(part, "part") for part in first.parts[shared + len(rest) :]]
    from_core += rest
    w_qkv, wo_mine, w_small = pl.pallas_call(
        functools.partial(assemble_kernel, bundle_places * 2),
        in_specs=[smem] + [any_spec] * len(bundle_rows),
        out_specs=[vmem] * 3,
        out_shape=[
            jax.ShapeDtypeStruct((width, w), BF) for w in (qkv_width, q_width, LANES)
        ],
        scratch_shapes=[pltpu.SemaphoreType.DMA(())],
        compiler_params=params(),
        name="assemble",
    )(
        bundle_where,
        *[in_hbm(part) for part in first.parts + from_core],
    )
    step_rows = min(rows, 256)
    steps = rows // step_rows
    row_spec = lambda cols: pl.BlockSpec((step_rows, cols), lambda i, *_: (i, 0))
    full_tokens, normed, queries, kv = (pl.pallas_call(
        functools.partial(project_kernel, pairs, q_width, experts),
        grid=(steps,),
        in_specs=[
            smem,
            row_spec(feature),
            row_spec(feature),
            whole((width, LANES)),
            whole((width, qkv_width)),
            row_spec(LANES),
            row_spec(LANES),
        ],
        out_specs=[row_spec(width), row_spec(width), row_spec(q_width), row_spec(2 * kv_width)],
        out_shape=[
            pltpu.HBM((rows, width), BF),
            pltpu.HBM((rows, width), BF),
            jax.ShapeDtypeStruct((rows, q_width), BF),
            jax.ShapeDtypeStruct((rows, 2 * kv_width), BF),
        ],
        compiler_params=params("arbitrary"),
        name="project",
    ))(tp_scalar, own_tokens, other_tokens, w_small, w_qkv, cosine, sine)

    own_side = [kv]
    for _ in range(deep - 1):
        own_side.append(shift_y(own_side[-1], up_y, "kv"))
    other_side = [swap_core(kv, "kv")]
    wo_other = swap_tp(wo_mine, "w_out")
    length = ctx * span

    queries, *own_side = segment(weights[:1], queries, *own_side)
    other_side += [swap_core(block, "kv") for block in own_side[1:]]
    kv_blocks = own_side + other_side
    head_spec = lambda: pl.BlockSpec((span, 2 * LANES), lambda s, p, *_: (s, p))
    prob_spec = pl.BlockSpec((1, 2, 2 * span, length), lambda s, p, *_: (s, p, 0, 0))
    attended, probs = (pl.pallas_call(
        functools.partial(attend_kernel, ctx, span),
        grid_spec=pltpu.PrefetchScalarGridSpec(
            num_scalar_prefetch=2,
            grid=(seqs, pairs),
            in_specs=[head_spec()] * (1 + ctx),
            out_specs=[head_spec(), prob_spec],
        ),
        out_shape=[
            jax.ShapeDtypeStruct((rows, q_width), BF),
            pltpu.HBM((seqs, 2 * pairs, 2 * span, length), BF),
        ],
        compiler_params=params("arbitrary", "arbitrary"),
        name="attend",
    ))(prefix, base, queries, *kv_blocks)

    attended, wo_other = segment(weights[:1], attended, wo_other)
    for _ in range(ring.size // 2 - 4):
        (attended,) = segment(weights[:1], attended)

    attended_other = swap_tp(attended, "attended")
    full_cot = (pl.pallas_call(
            features_kernel,
            in_specs=[smem] + [vmem] * 2,
            out_specs=vmem,
            out_shape=pltpu.HBM((rows, width), BF),
            compiler_params=params(),
            name="features",
        )
    )(tp_scalar, own_cot, other_cot)
    peer_cot = swap_core(full_cot, "full_cot")
    (attended_other,) = segment(weights[:1], attended_other)
    route_rows = routes.reshape(rows, TOP)
    middle, normed_two, gates = (pinned(pl.pallas_call(
        functools.partial(middle_kernel, experts + 1),
        grid=(steps,),
        in_specs=[
            row_spec(q_width),
            row_spec(q_width),
            whole((width, q_width)),
            whole((width, q_width)),
            row_spec(width),
            whole((width, LANES)),
            row_spec(TOP),
        ],
        out_specs=[
            row_spec(width),
            row_spec(width + LANES),
            row_spec(LANES),
        ],
        out_shape=[
            pltpu.HBM((rows, width), F32),
            pltpu.HBM((rows, width + LANES), BF),
            pltpu.HBM((rows, LANES), F32),
        ],
        compiler_params=params("arbitrary"),
        name="middle",
    )))(attended, attended_other, wo_mine, wo_other, full_tokens, w_small, route_rows)
    normed_two, peer_cot = arrive(weights[0], normed_two, peer_cot)
    (normed_two,) = segment(weights[1:], normed_two)
    peer_two = swap_core(normed_two, "normed_two")

    near = [(normed_two, BF), (full_cot, BF), (peer_two, BF), (peer_cot, BF)]
    sources = [in_hbm(array) for array, _ in near]
    wide_acc, acc_shape = (rows, width), (rows, width + LANES)
    count = len(places)

    def run_experts(g, call, accs, dw_parts):
        lead = 1 + count + 4 + len(accs)
        first_call, last_call = not accs, g + 1 == len(plan)
        call_size, start = plan[g][call], sum(plan[g][:call])
        column = sum(sum(sizes) for sizes in plan[:g]) + start
        kept = sum(sum(sizes) for sizes in (plan[1:] if g else plan[:1]))
        sums_start = column - sum(plan[0]) if g else start
        outs = pl.pallas_call(
            functools.partial(
                moe_kernel,
                first_call,
                last_call,
                bool(dw_parts),
                experts,
                column,
                start,
                sums_start,
                call_size,
                places,
            ),
            in_specs=[smem] + [any_spec] * (lead - 1 + len(dw_parts)),
            out_specs=[any_spec] * (3 + count),
            out_shape=[
                pltpu.HBM(acc_shape, F32),
                pltpu.HBM(acc_shape, BF if last_call else F32),
                pltpu.HBM((call_size, 2 * rows, hid), BF),
            ]
            + [pltpu.HBM((kept, r, 3 * hid), BF) for _, _, r in places],
            input_output_aliases={lead + j: 3 + j for j in range(len(dw_parts))},
            scratch_shapes=[pltpu.VMEM(array.shape, kind) for array, kind in near]
            + [pltpu.VMEM(acc_shape, F32)] * 2
            + [
                pltpu.VMEM((call_size, 2 * rows, hid), BF),
                pltpu.VMEM(acc_shape, BF),
                pltpu.VMEM((call_size, width, 3 * hid), BF),
                pltpu.VMEM((2, width, 3 * hid), BF),
                pltpu.SemaphoreType.DMA((call_size,)),
                pltpu.SemaphoreType.DMA((2,)),
                pltpu.SemaphoreType.DMA((4,)),
                pltpu.SemaphoreType.DMA((2,)),
                pltpu.SemaphoreType.DMA((2,)),
                pltpu.SemaphoreType.DMA(()),
            ],
            compiler_params=pltpu.CompilerParams(vmem_limit_bytes=MOE_VMEM),
            name="experts",
        )(
            part_where,
            *[in_hbm(block) for block in weights[g].parts],
            *sources,
            *accs,
            *dw_parts,
        )
        return outs[:2], outs[2], outs[3:]

    accs, mixed_parts, sums = (), [], []

    later = weights[1:]
    for call in range(len(plan[0])):
        if call:
            accs = segment(later, *accs)
            lead_parts = dw_parts
        accs, mixed, dw_parts = run_experts(0, call, accs, lead_parts if call else ())
        mixed_parts.append(mixed)
    sums.append(Scatter(ring, dw_parts, "sums_0"))
    dw_parts = ()
    for g in range(1, len(plan)):
        while weights[g].step < ring.size // 2 - 1:
            accs = segment(later, *accs)
        if not weights[g].done():
            accs = segment([weights[g]], *accs)
        accs = arrive(weights[g], *accs)
        accs = segment([*weights[g + 1 :], sums[0]], *accs)
        accs, mixed, dw_parts = run_experts(g, 0, accs, dw_parts)
        mixed_parts.append(mixed)
    sums.append(Scatter(ring, dw_parts, "sums_1"))

    grad_two, grad_two_peer = arrive(sums[0], *accs)
    parts = pl.pallas_call(
        functools.partial(add_terms_kernel, experts),
        in_specs=[vmem] * 2,
        out_specs=[vmem] * seqs,
        out_shape=[jax.ShapeDtypeStruct((span, width + LANES), BF)] * seqs,
        compiler_params=params(),
        name="add_terms",
    )(grad_two, swap_core(grad_two_peer, "grad_two"))
    parts = list(together(sums, *parts))
    parts_other = [swap_tp(parts[0], "part")]
    sums[0].prepare()
    for chain in sums:
        chain.send()

    moe, moe_peer = pl.pallas_call(
        functools.partial(moe_sum_kernel, places, plan),
        in_specs=[smem] + [any_spec] * (count * len(plan) + len(mixed_parts)),
        out_specs=[vmem] * 2,
        out_shape=[pltpu.HBM(wide_acc, F32), pltpu.HBM(wide_acc, BF)],
        scratch_shapes=[pltpu.VMEM((width, sum(sizes) * hid), BF) for sizes in plan]
        + [pltpu.VMEM((2 * rows, sum(sizes) * hid), BF) for sizes in plan]
        + [pltpu.SemaphoreType.DMA((len(plan),))] * 2,
        compiler_params=pltpu.CompilerParams(vmem_limit_bytes=MOE_VMEM),
        name="experts_output",
    )(
        part_where,
        *[in_hbm(block) for chain in weights for block in chain.parts],
        *lock(*[in_hbm(mixed) for mixed in mixed_parts], parts[0])[: len(mixed_parts)],
    )

    def sequence_back(s, part_other, before):
        at = lambda cols: pl.BlockSpec((span, cols), lambda i, *_: (s, 0))
        whole_span = lambda cols: pl.BlockSpec((span, cols), lambda i, *_: (0, 0))
        grad_middle, grad_branch, grad_attended, grad_logits, gain_term = pl.pallas_call(
            functools.partial(middle_back_kernel, experts + 1),
            grid=(1,),
            in_specs=[
                smem,
                whole_span(width + LANES),
                whole_span(width + LANES),
                at(LANES),
                at(width),
                at(width),
                whole((width, LANES)),
                whole((width, q_width)),
            ],
            out_specs=[
                whole_span(feature),
                whole_span(width),
                whole_span(q_width),
                whole_span(LANES),
                whole((1, width)),
            ],
            out_shape=[
                pltpu.HBM((span, feature), F32),
                pltpu.HBM((span, width), BF),
                jax.ShapeDtypeStruct((span, q_width), BF),
                pltpu.HBM((span, LANES), BF),
                pltpu.HBM((1, width), F32),
            ],
            compiler_params=params("arbitrary"),
            name="middle_back",
        )(tp_scalar, parts[s], part_other, gates, middle, full_cot, w_small, wo_mine)
        head = lambda row: pl.BlockSpec((span, 2 * LANES), lambda p: (row, p))
        turn = pl.BlockSpec((span, LANES), lambda p: (s, 0))
        back = pl.BlockSpec((deep, span, 2 * LANES), lambda p: (0, s, p))
        grads = pl.pallas_call(
            functools.partial(attend_back_kernel, ctx, span),
            grid=(pairs,),
            in_specs=[
                pl.BlockSpec((1, 2, 2 * span, length), lambda p: (s, p, 0, 0)),
                head(s),
                head(0),
                turn,
                turn,
            ]
            + [head(s)] * ctx
            + [any_spec] * len(before),
            out_specs=[head(s), back, back],
            out_shape=[
                pltpu.HBM((rows, q_width), BF),
                pltpu.HBM((deep, rows, 2 * kv_width), BF),
                pltpu.HBM((deep, rows, 2 * kv_width), BF),
            ],
            input_output_aliases={5 + ctx + j: j for j in range(len(before))},
            compiler_params=params("arbitrary"),
            name="attend_back",
        )(in_hbm(probs), queries, grad_attended, cosine, sine, *kv_blocks, *before)
        return (grad_middle, grad_branch, grad_logits, gain_term), grads

    parts_other[0], moe, moe_peer = lock(parts_other[0], moe, moe_peer)
    saved, found = [], ()
    for s in range(seqs):
        if s + 1 < seqs:
            parts[s + 1] = lock(parts[s + 1], parts_other[s])[0]
            parts_other.append(swap_tp(parts[s + 1], "part"))
        kept, found = sequence_back(s, parts_other[s], found)
        if s == 0:
            found = segment(sums[:1], *found)
            parts_other[-1], *found = arrive(sums[1], parts_other[-1], *found)
            sums[1].prepare()
            (parts_other[-1],) = together(sums[1:], parts_other[-1])
            from_core_moe = swap_core(lock(moe_peer, parts_other[-1])[0], "moe")
        saved.append(kept)
    half_at = lambda array, side: lax.dynamic_slice_in_dim(array, side * feature, feature, 1)
    moe_sum = moe + from_core_moe.astype(F32)
    moe_send = half_at(moe_sum, 1 - tp).astype(BF)
    grad_q, grad_kv_own, grad_kv_peer, moe_send = arrive(sums[0], *found, moe_send)

    def to_owner(grad_kv_own, from_peer):
        travel = jnp.zeros(from_peer.shape[1:], BF)
        for k in range(deep - 1, 0, -1):
            piece = grad_kv_own[k] + from_peer[k]
            if k < deep - 1:
                piece = piece + travel
            travel = shift_y(piece, down_y, "grad_kv")
        return travel

    def weight_grads(name, sides, gain_terms, gain_at, cols):
        flat = [array for side in sides for array in side]
        return (pl.pallas_call(
                functools.partial(weight_grad_kernel, [len(side) for side in sides], gain_at),
                in_specs=[smem] + [vmem] * (len(flat) + len(gain_terms)),
                out_specs=[vmem] * 2,
                out_shape=[jax.ShapeDtypeStruct((n, shard, cols), BF)] * 2,
                compiler_params=params(),
                name=f"{name}_weight_grads",
            )
        )(core_scalar, *flat, *gain_terms)

    def close_experts(chain):
        own = chain.parts[0]
        shape = (own.shape[0], shard, 3 * hid)
        kept, sent = pl.pallas_call(
            close_experts_kernel,
            in_specs=[smem] + [vmem] * 3,
            out_specs=[vmem] * 2,
            out_shape=[jax.ShapeDtypeStruct(shape, F32), jax.ShapeDtypeStruct(shape, BF)],
            compiler_params=params(),
            name="close_experts",
        )(core_scalar, own, *chain.moving)
        return kept, sent

    (grad_kv_peer,) = together(sums[1:], grad_kv_peer)
    sums[1].send()
    from_peer = swap_core(grad_kv_peer, "grad_kv")
    early = weight_grads(
        "early",
        [
            [kept[1] for kept in saved],
            [attended],
            [normed],
            [grad_q],
            [normed_two],
            [kept[2] for kept in saved],
        ],
        [kept[3] for kept in saved],
        experts,
        2 * q_width + LANES,
    )
    travel = to_owner(grad_kv_own, from_peer)
    segment(sums[1:])
    early_other = swap_core(early[1], "early")
    closed = [close_experts(sums[0])]
    moe_other = swap_tp(moe_send, "moe_send")
    travel, moe_other, *closed[0] = lock(travel, moe_other, *closed[0])
    shapes = [
        ((rows, 2 * kv_width), BF),
        ((rows, feature), F32),
        ((rows, feature + LANES), BF),
        ((rows, LANES), F32),
        ((1, width), F32),
    ]
    grad_kv, grad_own, grad_send, inner, gain_one_term = pl.pallas_call(
        functools.partial(project_back_kernel, pairs, experts, seqs),
        in_specs=[smem] + [vmem] * 9,
        out_specs=[vmem] * 5,
        out_shape=[jax.ShapeDtypeStruct(shape, kind) for shape, kind in shapes],
        compiler_params=params(),
        name="project_back",
    )(
        tp_scalar,
        grad_q,
        grad_kv_own,
        from_peer,
        travel,
        cosine,
        sine,
        w_qkv,
        full_tokens,
        w_small,
    )
    late = weight_grads(
        "late", [[normed], [grad_kv]], [gain_one_term], 0, 2 * kv_width + LANES
    )
    late_other = swap_core(late[1], "late")
    late_other, early_other = lock(late_other, early_other)
    cols = early_other.shape[2] + late_other.shape[2]
    last = Scatter(
        ring,
        pinned(pl.pallas_call(
            functools.partial(order_kernel, bundle_places),
            in_specs=[smem] + [vmem] * 4,
            out_specs=[vmem] * len(bundle_places),
            out_shape=[jax.ShapeDtypeStruct((1, r, cols), BF) for _, _, r in bundle_places],
            compiler_params=params(),
            name="order",
        ))(chip_list, early[0], early_other, late[0], late_other),
        "last",
    )
    (grad_send,) = together([last], grad_send)
    last.send()
    arrive(sums[1])
    sums[1].prepare()
    together([last, sums[1]])
    sums[1].send()
    grad_other = swap_tp(grad_send, "grad_normed")
    segment([last])
    grad_tokens = pinned(
        pl.pallas_call(
            token_grads_kernel,
            in_specs=[vmem] * (4 + seqs),
            out_specs=vmem,
            out_shape=pltpu.HBM((rows, feature), F32),
            compiler_params=params(),
            name="token_grads",
        )
    )(own_tokens, grad_own, inner, grad_other, *[kept[0] for kept in saved])
    output = (half_at(middle, tp) + half_at(moe_sum, tp) + moe_other.astype(F32)).astype(BF)
    grad_tokens, output = segment([last], grad_tokens, output)
    while not sums[1].done():
        segment(sums[1:])
    together([last, sums[1]])
    closed.append(close_experts(sums[1]))
    closed = [[kept, swap_core(sent, "expert_grads")] for kept, sent in closed]
    while not last.done():
        segment([last])
    arrive(last)
    widths = (("one", q_width), ("one", q_width), ("one", LANES), ("pairs", 2 * kv_width), ("one", LANES))
    out_term, grad_query, small_term, grad_key, grad_value, gain_term = (pinned(pl.pallas_call(
            functools.partial(close_weights_kernel, widths),
            in_specs=[vmem] * 3,
            out_specs=[vmem] * 6,
            out_shape=[
                jax.ShapeDtypeStruct((shard, w), F32)
                for w in (q_width, q_width, LANES, kv_width, kv_width, LANES)
            ],
            compiler_params=params(),
            name="close_weights",
        ))
    )(last.parts[0], *last.moving)
    grad_out = out_term.T
    grad_router = small_term[:, :experts]
    grad_gain_ffn = small_term[:, experts]
    gain_half = gain_term[:, 0]
    gain_other = swap_tp(gain_half, "gain")

    grad_gate, grad_up, down_term = (pl.pallas_call(
            functools.partial(expert_grads_kernel, len(sums)),
            in_specs=[smem] + [vmem] * (2 * len(sums)),
            out_specs=[vmem] * 3,
            out_shape=[pltpu.HBM((experts, shard, hid), F32)] * 3,
            compiler_params=params(),
            name="expert_grads",
        )
    )(
        core_scalar,
        *[closed[k][0] for k in range(len(sums))],
        *[closed[k][1] for k in range(len(sums))],
    )
    gain_other, grad_gate, grad_up, down_term = lock(gain_other, grad_gate, grad_up, down_term)
    grad_gain_attn = gain_half + gain_other
    grad_down = down_term.transpose(0, 2, 1)

    return (
        output.reshape(seqs, span, feature),
        grad_tokens.reshape(seqs, span, feature),
        grad_query,
        grad_key,
        grad_value,
        grad_out,
        grad_router,
        grad_gain_attn,
        grad_gain_ffn,
        grad_gate,
        grad_up,
        grad_down,
    )


def solution(mesh):
    in_specs = (
        P("fsdp", "ctx", "tp"),
        P("fsdp"),
        P("ctx", "fsdp", None, None),
        P(("fsdp", "ctx"), "tp"),
        P(("fsdp", "ctx"), "tp"),
        P(("fsdp", "ctx"), "tp"),
        P("tp", ("fsdp", "ctx")),
        P(("fsdp", "ctx"), None),
        P(("fsdp", "ctx")),
        P(("fsdp", "ctx")),
        P(None, ("fsdp", "ctx"), "tp"),
        P(None, ("fsdp", "ctx"), "tp"),
        P(None, "tp", ("fsdp", "ctx")),
        P("fsdp", "ctx", "tp"),
    )
    out_specs = (
        P("fsdp", "ctx", "tp"),
        P("fsdp", "ctx", "tp"),
        P(("fsdp", "ctx"), "tp"),
        P(("fsdp", "ctx"), "tp"),
        P(("fsdp", "ctx"), "tp"),
        P("tp", ("fsdp", "ctx")),
        P(("fsdp", "ctx"), None),
        P(("fsdp", "ctx")),
        P(("fsdp", "ctx")),
        P(None, ("fsdp", "ctx"), "tp"),
        P(None, ("fsdp", "ctx"), "tp"),
        P(None, "tp", ("fsdp", "ctx")),
    )
    return jax.shard_map(
        per_device, mesh=mesh, in_specs=in_specs, out_specs=out_specs, check_vma=False
    )
```

```python
import functools

import jax
import jax.numpy as jnp
from jax import lax
from jax.experimental import pallas as pl
from jax.experimental.pallas import tpu as pltpu
from jax.sharding import PartitionSpec as P

HD = 64
TOP = 8
LANES = 128

EPSILON = 1e-06
ATTN_SCALE = 0.015625
RESIDUAL_SCALE = 0.22
MASKED_SCORE = -1e30
RING = ("fsdp", "ctx")
BF = jnp.bfloat16
F32 = jnp.float32
VMEM_LIMIT = 24 * 1024 * 1024
MOE_VMEM = 56 * 1024 * 1024


def nt(a, b):
    return lax.dot_general(a, b, (((1,), (1,)), ((), ())), preferred_element_type=F32)


def nn(a, b):
    return lax.dot_general(a, b, (((1,), (0,)), ((), ())), preferred_element_type=F32)


def tn(a, b):
    return lax.dot_general(a, b, (((0,), (0,)), ((), ())), preferred_element_type=F32)


def params(*semantics):
    return pltpu.CompilerParams(
        dimension_semantics=semantics, vmem_limit_bytes=VMEM_LIMIT
    )


def whole(shape):
    zeros = (0,) * len(shape)
    return pl.BlockSpec(shape, lambda *_: zeros, pipeline_mode=pl.Buffered(1))


def swap_halves(slab):
    lane = lax.broadcasted_iota(jnp.int32, slab.shape, 1) % HD
    return jnp.where(
        lane < HD // 2, pltpu.roll(slab, LANES - HD // 2, 1), pltpu.roll(slab, HD // 2, 1)
    )


def column_as_row(ref, column):
    lane = lax.broadcasted_iota(jnp.int32, (16, ref.shape[1]), 1)
    return nt(jnp.where(lane == column, 1.0, 0.0).astype(BF), ref[...])[:1]


def pack_kernel(q_ref, k_ref, v_ref, out_ref, router_ref, one_ref, two_ref, packed_ref, *scratch):
    stage, sem = scratch
    rows, q_width = q_ref.shape
    copies, at = [], 0

    def copy(source, width):
        nonlocal at
        copies.append(pltpu.make_async_copy(source, packed_ref.at[0, :, pl.ds(at, width)], sem))
        copies[-1].start()
        at += width

    copy(q_ref, q_width)
    for pair in range(k_ref.shape[1] // LANES):
        cols = pl.ds(pair * LANES, LANES)
        copy(k_ref.at[:, cols], LANES)
        copy(v_ref.at[:, cols], LANES)
    copy(out_ref, q_width)
    experts = router_ref.shape[0]
    stage[...] = jnp.zeros(stage.shape, F32)
    stage[:experts, :rows] = router_ref[...].astype(F32)
    stage[experts : experts + 1, :rows] = one_ref[...].astype(F32)
    stage[experts + 1 : experts + 2, :rows] = two_ref[...].astype(F32)
    packed_ref[0, :, at:] = stage[...].T[:rows].astype(BF)
    for each in copies:
        each.wait()


def pack_experts_kernel(core_ref, gate_ref, up_ref, down_ref, mine_ref, other_ref, sem):
    count, _, cols = mine_ref.shape
    hid = cols // 3
    copies = []
    for out_ref, core in ((mine_ref, core_ref[0]), (other_ref, 1 - core_ref[0])):
        for i, source in enumerate((gate_ref, up_ref, down_ref)):
            copies.append(
                pltpu.make_async_copy(
                    source.at[pl.ds(core * count, count)],
                    out_ref.at[:, :, pl.ds(i * hid, hid)],
                    sem,
                )
            )
            copies[-1].start()
    for copy in copies:
        copy.wait()


def join_kernel(core_ref, mine_ref, other_ref, *groups):
    rows = mine_ref.shape[1]
    for mine_first in (True, False):

        @pl.when((core_ref[0] == 0) == mine_first)
        def _():
            at = 0
            for out_ref in groups:
                size = out_ref.shape[0]
                first, second = (mine_ref, other_ref) if mine_first else (other_ref, mine_ref)
                out_ref[:, :rows] = first[at : at + size]
                out_ref[:, rows:] = second[at : at + size]
                at += size


def assemble_kernel(places, where_ref, *refs):
    count = len(places)
    parts, outs, sem = refs[:count], refs[count:-1], refs[-1]

    def copies():
        for j, (_, _, rows) in enumerate(places):
            first = 0
            for out in outs:
                cols = out.shape[1]
                yield pltpu.make_async_copy(
                    parts[j].at[0, :, pl.ds(first, cols)],
                    out.at[pl.ds(pl.multiple_of(where_ref[j], 16), rows)],
                    sem,
                )
                first += cols

    for copy in copies():
        copy.start()
    for copy in copies():
        copy.wait()


def side_by_side(tp_ref, mine, other):
    first = tp_ref[0] == 0
    return jnp.concatenate([jnp.where(first, mine, other), jnp.where(first, other, mine)], axis=1)


def features_kernel(tp_ref, mine_ref, other_ref, full_ref):
    full_ref[...] = side_by_side(tp_ref, mine_ref[...], other_ref[...])


def project_kernel(
    pairs,
    q_width,
    gain_col,
    tp_ref,
    mine_ref,
    other_ref,
    small_ref,
    w_ref,
    cos_ref,
    sin_ref,
    x_ref,
    n_ref,
    q_ref,
    kv_ref,
):
    x_ref[...] = side_by_side(tp_ref, mine_ref[...], other_ref[...])
    x = x_ref[...].astype(F32)
    gain = column_as_row(small_ref, gain_col)
    scale = lax.rsqrt(jnp.mean(x * x, axis=1, keepdims=True) + EPSILON)
    normed = (x * scale * gain).astype(BF)
    n_ref[...] = normed
    cosine, sine = cos_ref[...], sin_ref[...]
    raw = nn(normed, w_ref[...])
    for slab in range(q_width // LANES):
        cols = slice(slab * LANES, (slab + 1) * LANES)
        part = raw[:, cols]
        turned = (part * cosine + swap_halves(part) * sine).astype(BF)
        q_ref[:, cols] = (turned.astype(F32) * ATTN_SCALE).astype(BF)
    for pair in range(pairs):
        lo = pair * 2 * LANES
        part = raw[:, q_width + lo : q_width + lo + LANES]
        kv_ref[:, lo : lo + LANES] = (part * cosine + swap_halves(part) * sine).astype(BF)
        kv_ref[:, lo + LANES : lo + 2 * LANES] = raw[
            :, q_width + lo + LANES : q_width + lo + 2 * LANES
        ].astype(BF)


def attend_kernel(blocks, span, prefix_ref, base_ref, q_ref, *refs):
    kv_refs = refs[:blocks]
    out_ref, p_ref = refs[blocks:]
    limit_len = prefix_ref[pl.program_id(0)]
    local = base_ref[0] + lax.broadcasted_iota(jnp.int32, (span, 1), 0)
    limit = jnp.maximum(local + 1, limit_len)
    key_pos = jnp.concatenate(
        [
            base_ref[j] + lax.broadcasted_iota(jnp.int32, (1, span), 1)
            for j in range(blocks)
        ],
        axis=1,
    )
    visible = key_pos < limit
    visible = jnp.concatenate([visible, visible], axis=0)
    for g in range(2):
        keys = jnp.concatenate([r[:, g * HD : (g + 1) * HD] for r in kv_refs], axis=0)
        vals = jnp.concatenate(
            [r[:, LANES + g * HD : LANES + (g + 1) * HD] for r in kv_refs], axis=0
        )
        first, second = 2 * g * HD, (2 * g + 1) * HD
        queries = jnp.concatenate(
            [q_ref[:, first : first + HD], q_ref[:, second : second + HD]], axis=0
        )
        scores = jnp.where(visible, nt(queries, keys), MASKED_SCORE)
        expo = jnp.exp(scores - jnp.max(scores, axis=1, keepdims=True))
        probs = (expo * (1.0 / jnp.sum(expo, axis=1, keepdims=True))).astype(BF)
        p_ref[0, g] = probs
        att = nn(probs, vals).astype(BF)
        out_ref[:, first : first + HD] = att[:span]
        out_ref[:, second : second + HD] = att[span:]


def attend_back_kernel(blocks, span, p_ref, q_ref, g_ref, cos_ref, sin_ref, *refs):
    kv_refs = refs[:blocks]
    dq_ref, own_ref, other_ref = refs[-3:]
    cosine, sine = cos_ref[...], sin_ref[...]
    parts = []
    for g in range(2):
        keys = jnp.concatenate([r[:, g * HD : (g + 1) * HD] for r in kv_refs], axis=0)
        vals = jnp.concatenate(
            [r[:, LANES + g * HD : LANES + (g + 1) * HD] for r in kv_refs], axis=0
        )
        first, second = 2 * g * HD, (2 * g + 1) * HD
        queries = jnp.concatenate(
            [q_ref[:, first : first + HD], q_ref[:, second : second + HD]], axis=0
        )
        grads = jnp.concatenate(
            [g_ref[:, first : first + HD], g_ref[:, second : second + HD]], axis=0
        )
        probs = p_ref[0, g]
        wide = probs.astype(F32)
        grad_probs = nt(grads, vals)
        inner = jnp.sum(wide * grad_probs, axis=1, keepdims=True)
        grad_scores = (wide * (grad_probs - inner)).astype(BF)
        dq = nn(grad_scores, keys) * ATTN_SCALE
        slab = jnp.concatenate([dq[:span], dq[span:]], axis=1)
        turned = slab * cosine - swap_halves(slab) * sine
        dq_ref[:, first : first + LANES] = turned.astype(BF)
        parts.append((nn(queries.T, grad_scores), nn(grads.T, probs)))
    stacked = jnp.concatenate([parts[0][0], parts[1][0], parts[0][1], parts[1][1]], axis=0)
    turned = stacked.T.astype(BF)
    half = blocks // 2
    for j in range(half):
        own_ref[j] = turned[j * span : (j + 1) * span]
        other_ref[j] = turned[(half + j) * span : (half + j + 1) * span]


def middle_kernel(
    gain_col, a_ref, b_ref, wa_ref, wb_ref, x_ref, small_ref, routes_ref, m_ref, n_ref, g_ref
):
    branch = nt(a_ref[...], wa_ref[...]) + nt(b_ref[...], wb_ref[...])
    middle = x_ref[...].astype(F32) + RESIDUAL_SCALE * branch
    m_ref[...] = middle
    scale = lax.rsqrt(jnp.mean(middle * middle, axis=1, keepdims=True) + EPSILON)
    wide = middle * scale * column_as_row(small_ref, gain_col)
    normed = wide.astype(BF)
    width = normed.shape[1]
    n_ref[:, :width] = normed
    logits = nn(normed, small_ref[...])
    lane = lax.broadcasted_iota(jnp.int32, logits.shape, 1)
    routes = routes_ref[...]
    routed = lane == routes[:, 0:1]
    for k in range(1, TOP):
        routed = routed | (lane == routes[:, k : k + 1])
    logits = jnp.where(routed, logits, MASKED_SCORE)
    expo = jnp.where(routed, jnp.exp(logits - jnp.max(logits, axis=1, keepdims=True)), 0.0)
    gates = expo / jnp.sum(expo, axis=1, keepdims=True)
    g_ref[...] = gates
    n_ref[:, width:] = in_two(gates, gain_col - 1)


def in_two(pull, experts):
    high = pull.astype(BF).astype(F32)
    return (high + pltpu.roll(pull - high, experts, 1)).astype(BF)


def in_one(terms, experts):
    wide = terms.astype(F32)
    lane = lax.broadcasted_iota(jnp.int32, wide.shape, 1)
    both = wide + pltpu.roll(wide, LANES - experts, 1)
    return jnp.where(lane < experts, both, 0.0)


def moe_kernel(
    first_call, last_call, joins, experts, column, start, sums_start, group, places, where_ref, *refs
):
    count = len(places)
    w_parts, refs = refs[:count], refs[count:]
    sources, refs = refs[:4], refs[4:]
    inits, refs = ((), refs) if first_call else (refs[:2], refs[2:])
    refs = refs[count:] if joins else refs
    outs, mixed_out, dw_parts, refs = refs[:2], refs[2], refs[3 : 3 + count], refs[3 + count :]
    here, accs, refs = refs[:4], refs[4:6], refs[6:]
    mixed_all, narrow, w_all, dw_all, w_sem, dw_sem, near_sem, acc_sem, out_sem, mixed_sem = refs
    xa_ref, ya_ref, xb_ref, yb_ref = here
    rows, width = ya_ref.shape
    hid = w_all.shape[2] // 3

    def window(j):
        return pl.ds(pl.multiple_of(where_ref[1 + j], 16), places[j][2])

    def load(e, j):
        return pltpu.make_async_copy(
            w_parts[j].at[start + e], w_all.at[e, window(j)], w_sem.at[e]
        )

    def store(e, j):
        return pltpu.make_async_copy(
            dw_all.at[e % 2, window(j)], dw_parts[j].at[sums_start + e], dw_sem.at[e % 2]
        )

    nears = [
        pltpu.make_async_copy(a, b, near_sem.at[i]) for i, (a, b) in enumerate(zip(sources, here))
    ]
    fetches = [
        pltpu.make_async_copy(a, b, acc_sem.at[i]) for i, (a, b) in enumerate(zip(inits, accs))
    ]
    mixed_store = pltpu.make_async_copy(mixed_all, mixed_out, mixed_sem)
    for j in range(count):
        load(0, j).start()
    for copy in nears[:2]:
        copy.start()
    results = []
    for e in range(group):
        for j in range(count):
            load(e, j).wait()
        if e == 0:
            for copy in nears[:2]:
                copy.wait()
            for copy in [*fetches[:1], *nears[2:], *fetches[1:]]:
                copy.start()
        expert = where_ref[0] + column + e
        w_gu, w_d = w_all[e, :, : 2 * hid], w_all[e, :, 2 * hid :]
        kept = []
        for side, (x_ref, y_ref) in enumerate(((xa_ref, ya_ref), (xb_ref, yb_ref))):
            acc = accs[side]
            if e == 0 and side == 1:
                for copy in nears[2:]:
                    copy.wait()
                for other in range(1, group):
                    for j in range(count):
                        load(other, j).start()
            pre = nn(x_ref[:, :width], w_gu)
            back = nn(y_ref[...], w_d)
            gates = in_one(x_ref[:, width:], experts)
            lane = lax.broadcasted_iota(jnp.int32, gates.shape, 1)
            mask = lane == expert
            weight = RESIDUAL_SCALE * jnp.sum(
                jnp.where(mask, gates, 0.0), axis=1, keepdims=True
            )
            gate_pre, up_pre = pre[:, :hid], pre[:, hid:]
            sig = jax.nn.sigmoid(gate_pre)
            act = gate_pre * sig
            hidden = act * up_pre
            pull = RESIDUAL_SCALE * jnp.sum(back * hidden, axis=1, keepdims=True)
            scaled = weight * back
            d_up = scaled * act
            d_gate = scaled * up_pre * (sig + act * (1.0 - sig))
            d_gu = jnp.concatenate([d_gate.astype(BF), d_up.astype(BF)], axis=1)
            mixed = (weight * hidden).astype(BF)
            mixed_all[e, side * rows : (side + 1) * rows] = mixed
            if first_call and e == 0:
                acc[:, :width] = nt(d_gu, w_gu)
                acc[:, width:] = jnp.where(mask, pull, 0.0)
            else:
                if e == 0:
                    fetches[side].wait()
                acc[:, :width] += nt(d_gu, w_gu)
                acc[:, width:] += jnp.where(mask, pull, 0.0)
            kept.append((d_gu, mixed))
            if e == group - 1:
                if last_call and side:
                    narrow[:, :width] = acc[:, :width].astype(BF)
                    narrow[:, width:] = in_two(acc[:, width:], experts)
                    acc = narrow
                results.append(pltpu.make_async_copy(acc, outs[side], out_sem.at[side]))
                results[-1].start()
        if e == group - 1:
            mixed_store.start()
        dw_gu = tn(xa_ref[:, :width], kept[0][0]) + tn(xb_ref[:, :width], kept[1][0])
        dw_d = tn(ya_ref[...], kept[0][1]) + tn(yb_ref[...], kept[1][1])
        if e >= 2:
            for j in range(count):
                store(e - 2, j).wait()
        dw_all[e % 2, :, : 2 * hid] = dw_gu.astype(BF)
        dw_all[e % 2, :, 2 * hid :] = dw_d.astype(BF)
        for j in range(count):
            store(e, j).start()
    for e in range(max(0, group - 2), group):
        for j in range(count):
            store(e, j).wait()
    for copy in results:
        copy.wait()
    mixed_store.wait()


def moe_sum_kernel(places, plan, where_ref, *refs):
    count, sets = len(places), len(plan)
    w_sets = [refs[k * count : (k + 1) * count] for k in range(sets)]
    refs = refs[sets * count :]
    calls = sum(len(sizes) for sizes in plan)
    mixed_parts, refs = refs[:calls], refs[calls:]
    own_ref, peer_ref, refs = refs[0], refs[1], refs[2:]
    w_all, mixed_all, (w_sem, mixed_sem) = refs[:sets], refs[sets : 2 * sets], refs[2 * sets :]
    rows = own_ref.shape[0]

    def loads(k):
        hid = w_all[k].shape[1] // sum(plan[k])
        at = 0
        for call, size in enumerate(plan[k]):
            source = mixed_parts[sum(len(sizes) for sizes in plan[:k]) + call]
            for i in range(size):
                cols = pl.ds(at * hid, hid)
                for j in range(count):
                    window = pl.ds(pl.multiple_of(where_ref[1 + j], 16), places[j][2])
                    yield pltpu.make_async_copy(
                        w_sets[k][j].at[at, :, pl.ds(2 * hid, hid)],
                        w_all[k].at[window, cols],
                        w_sem.at[k],
                    )
                yield pltpu.make_async_copy(
                    source.at[i], mixed_all[k].at[:, cols], mixed_sem.at[k]
                )
                at += 1

    for k in range(sets):
        for copy in loads(k):
            copy.start()
    total = None
    for k in range(sets):
        for copy in loads(k):
            copy.wait()
        term = nt(mixed_all[k][...], w_all[k][...])
        total = term if total is None else total + term
    own_ref[...] = total[:rows]
    peer_ref[...] = total[rows:].astype(BF)


def weight_grad_kernel(counts, gain_at, core_ref, *refs):
    sides = []
    for size in counts:
        sides.append(jnp.concatenate([ref[...] for ref in refs[:size]], axis=0))
        refs = refs[size:]
    gain_refs, (kept_ref, sent_ref) = refs[:-2], refs[-2:]
    n, shard, _ = kept_ref.shape
    width = 2 * n * shard
    terms = [tn(left[:, :width], right) for left, right in zip(sides[::2], sides[1::2])]
    if gain_refs:
        if terms[-1].shape[1] != LANES:
            terms.append(jnp.zeros((width, LANES), F32))
        row = lax.broadcasted_iota(jnp.int32, (8, LANES), 0)
        lane = lax.broadcasted_iota(jnp.int32, (8, LANES), 1)
        place = jnp.where((row == 0) & (lane == gain_at), 1.0, 0.0)
        gain = sum(ref[...] for ref in gain_refs)
        terms[-1] = terms[-1] + tn(jnp.broadcast_to(gain, (8, width)), place)
    first = 0
    for term in terms:
        cols = term.shape[1]
        parts = term.astype(BF).reshape(n, 2, shard, cols)
        for mine in range(2):

            @pl.when(core_ref[0] == mine)
            def _():
                kept_ref[:, :, first : first + cols] = parts[:, mine]
                sent_ref[:, :, first : first + cols] = parts[:, 1 - mine]

        first += cols


def order_kernel(places, chips_ref, *refs):
    count = len(places)
    pairs, parts = refs[:-count], refs[-count:]
    for j, (_, row, rows) in enumerate(places):
        chip = chips_ref[j]
        window = pl.ds(row, rows)
        first = 0
        for kept_ref, other_ref in zip(pairs[::2], pairs[1::2]):
            cols = kept_ref.shape[2]
            parts[j][0, :, first : first + cols] = kept_ref[chip, window] + other_ref[chip, window]
            first += cols


def add_terms_kernel(experts, own_ref, peer_ref, *sum_refs):
    width = own_ref.shape[1] - LANES
    rows = own_ref.shape[0] // len(sum_refs)
    for s, sum_ref in enumerate(sum_refs):
        span = slice(s * rows, (s + 1) * rows)
        total = own_ref[span, :width] + peer_ref[span, :width].astype(F32)
        sum_ref[:, :width] = total.astype(BF)
        pull = own_ref[span, width:] + in_one(peer_ref[span, width:], experts)
        sum_ref[:, width:] = in_two(pull, experts)


def close_experts_kernel(core_ref, own_ref, ahead_ref, back_ref, kept_ref, sent_ref):
    rows = kept_ref.shape[1]
    total = own_ref[...].astype(F32) + ahead_ref[...].astype(F32) + back_ref[...].astype(F32)
    is_first = core_ref[0] == 0
    kept_ref[...] = jnp.where(is_first, total[:, :rows], total[:, rows:])
    sent_ref[...] = jnp.where(is_first, total[:, rows:], total[:, :rows]).astype(BF)


def expert_grads_kernel(chains, core_ref, *refs):
    kept_refs, sent_refs, outs = refs[:chains], refs[chains : 2 * chains], refs[2 * chains :]
    count, _, cols = kept_refs[0].shape
    hid = cols // 3
    for k in range(chains):
        for ref, core in ((kept_refs[k], core_ref[0]), (sent_refs[k], 1 - core_ref[0])):
            for i in range(count):
                at = core * chains * count + k * count + i
                for part, out in enumerate(outs):
                    out[at] = ref[i, :, part * hid : (part + 1) * hid].astype(F32)


def close_weights_kernel(widths, own_ref, ahead_ref, back_ref, *refs):
    across, outs = refs[:3], refs[3:]
    gain_ref = outs[-1]
    def total(cols):
        return (
            own_ref[0, :, cols].astype(F32)
            + ahead_ref[0, :, cols].astype(F32)
            + back_ref[0, :, cols].astype(F32)
        )

    first = 0
    for kind, width in widths:
        if kind == "pairs":
            for pair in range(width // (2 * LANES)):
                for side in range(2):
                    lo = first + (2 * pair + side) * LANES
                    outs[side][:, pair * LANES : (pair + 1) * LANES] = total(slice(lo, lo + LANES))
            outs = outs[2:]
        else:
            outs[0][...] = total(slice(first, first + width))
            outs = outs[1:]
        first += width
    for ref in across:
        gain_ref[...] += ref[0].astype(F32)


def token_grads_kernel(x_ref, own_ref, dot_ref, other_ref, *refs):
    middles, out_ref = refs[:-1], refs[-1]
    feature = x_ref.shape[1]
    span = middles[0].shape[0]
    for s, middle_ref in enumerate(middles):
        at = slice(s * span, (s + 1) * span)
        other = other_ref[at]
        dot = dot_ref[at, :1] + in_one(other[:, feature:], 1)[:, :1]
        total = middle_ref[...] + own_ref[at] + other[:, :feature].astype(F32)
        out_ref[at] = total - x_ref[at].astype(F32) * dot


def middle_back_kernel(
    gain_col,
    tp_ref,
    sa_ref,
    sb_ref,
    gates_ref,
    m_ref,
    y_ref,
    small_ref,
    wo_ref,
    gm_ref,
    branch_ref,
    att_ref,
    logit_ref,
    dgain_ref,
):
    @pl.when(pl.program_id(0) == 0)
    def _():
        dgain_ref[...] = jnp.zeros(dgain_ref.shape, F32)

    gates = gates_ref[...]
    width = m_ref.shape[1]
    pull = in_one(sa_ref[:, width:], gain_col - 1) + in_one(sb_ref[:, width:], gain_col - 1)
    weighted = gates * pull
    grad_logits = (weighted - gates * jnp.sum(weighted, axis=1, keepdims=True)).astype(BF)
    logit_ref[...] = grad_logits
    grad = sa_ref[:, :width].astype(F32) + sb_ref[:, :width].astype(F32)
    grad = grad + nt(grad_logits, small_ref[...])
    middle = m_ref[...]
    scale = lax.rsqrt(jnp.mean(middle * middle, axis=1, keepdims=True) + EPSILON)
    unit = middle * scale
    dgain_ref[...] += jnp.sum(grad * unit, axis=0, keepdims=True)
    scaled = grad * column_as_row(small_ref, gain_col)
    inner = jnp.sum(scaled * unit, axis=1, keepdims=True) * (1.0 / width)
    grad_middle = y_ref[...].astype(F32) + scale * (scaled - unit * inner)
    half = width // 2
    gm_ref[...] = jnp.where(tp_ref[0] == 0, grad_middle[:, :half], grad_middle[:, half:])
    branch = (RESIDUAL_SCALE * grad_middle).astype(BF)
    branch_ref[...] = branch
    att_ref[...] = nn(branch, wo_ref[...]).astype(BF)


def project_back_kernel(pairs, gain_col, seqs, tp_ref, *refs):
    dq_ref, kva_ref, kvb_ref, kvc_ref, cos_ref, sin_ref, w_ref, x_ref, small_ref = refs[:9]
    d_ref, own_ref, other_ref, dot_ref, dgain_ref = refs[9:]
    gain = column_as_row(small_ref, gain_col)
    is_first = tp_ref[0] == 0
    rows, q_width = dq_ref.shape
    span = rows // seqs
    for s in range(seqs):
        at = slice(s * span, (s + 1) * span)
        cosine, sine = cos_ref[at], sin_ref[at]
        kv = kva_ref[0, at].astype(F32) + kvb_ref[0, at].astype(F32) + kvc_ref[at].astype(F32)
        for pair in range(pairs):
            lo = pair * 2 * LANES
            part = kv[:, lo : lo + LANES]
            d_ref[at, lo : lo + LANES] = (part * cosine - swap_halves(part) * sine).astype(BF)
            d_ref[at, lo + LANES : lo + 2 * LANES] = kv[:, lo + LANES : lo + 2 * LANES].astype(BF)
        grad = nt(dq_ref[at], w_ref[:, :q_width]) + nt(d_ref[at], w_ref[:, q_width:])
        x = x_ref[at].astype(F32)
        width = x.shape[1]
        scale = lax.rsqrt(jnp.mean(x * x, axis=1, keepdims=True) + EPSILON)
        unit = x * scale
        term = jnp.sum(grad * unit, axis=0, keepdims=True)
        if s == 0:
            dgain_ref[...] = term
        else:
            dgain_ref[...] += term
        scaled = grad * gain
        inner = jnp.sum(scaled * unit, axis=1, keepdims=True) * (1.0 / width) * scale * scale
        lane = lax.broadcasted_iota(jnp.int32, (span, LANES), 1)
        dot = jnp.where(lane == 0, inner, 0.0)
        dot_ref[at] = dot
        scaled = scaled * scale
        half = width // 2
        own_ref[at] = jnp.where(is_first, scaled[:, :half], scaled[:, half:])
        other_ref[at, :half] = jnp.where(is_first, scaled[:, half:], scaled[:, :half]).astype(BF)
        other_ref[at, half:] = in_two(dot, 1)


class Ring:
    def __init__(self, wide, ctx):
        self.wide, self.ctx, self.deep = wide, ctx, ctx // 2
        self.size = wide * self.deep
        deep = self.deep
        order = [
            (f, y)
            for y in range(deep)
            for f in (range(wide) if y % 2 == 0 else range(wide - 1, -1, -1))
        ]
        flat = [[f * ctx + y * 2 + c for f, y in order] for c in range(2)]
        n = self.size
        self.forward = [(row[i], row[(i + 1) % n]) for row in flat for i in range(n)]
        self.backward = [(b, a) for a, b in self.forward]
        f, c = lax.axis_index("fsdp"), lax.axis_index("ctx")
        y = c // 2
        self.place = y * wide + jnp.where(y % 2 == 0, f, wide - 1 - f)

    def chip(self, offset):
        place = (self.place + offset) % self.size
        y, q = place // self.wide, place % self.wide
        f = jnp.where(y % 2 == 0, q, self.wide - 1 - q)
        return f * self.deep + y

    def send(self, array, forward=True):
        return lax.ppermute(array, RING, self.forward if forward else self.backward)

    def places(self, rows):
        far, half = self.size // 2, rows // 2
        found = [(0, 0, rows)]
        for step in range(1, far):
            found += [(-step, 0, rows), (step, 0, rows)]
        if half % 16:
            return found + [(-far, 0, rows)]
        return found + [(-far, 0, half), (far, half, half)]


class Gather:
    def __init__(self, ring, block, name):
        self.ring, self.step, self.rows, self.name = ring, 0, block.shape[1], name
        self.moving = (block, block)
        self.parts = [block]

    def prepare(self):
        if self.step == self.ring.size // 2 - 1:
            half = self.rows // 2
            ahead, back = self.moving
            self.moving = (ahead[:, :half], back[:, half:]) if half % 16 == 0 else (ahead,)

    def send(self):
        self.step += 1
        with jax.named_scope(f"{self.name}_step_{self.step}"):
            self.moving = tuple(
                self.ring.send(array, i == 0) for i, array in enumerate(self.moving)
            )
        self.parts += self.moving

    def done(self):
        return self.step == self.ring.size // 2


class Scatter:
    def __init__(self, ring, parts, name):
        self.ring, self.parts, self.step, self.name = ring, parts, 0, name
        self.far = ring.size // 2
        self.halved = len(parts) == ring.size + 1
        self.moving = (parts[-2], parts[-1]) if self.halved else (parts[-1],)

    def prepare(self):
        if self.step:
            s = self.far - self.step
            self.moving = add_pair(self.parts[2 * s], self.parts[2 * s - 1], *self.moving)

    def send(self):
        self.step += 1
        with jax.named_scope(f"{self.name}_step_{self.step}"):
            self.moving = tuple(
                self.ring.send(array, i == 0) for i, array in enumerate(self.moving)
            )

    def done(self):
        return self.step == self.far


def add_pair_kernel(near_ref, behind_ref, *refs):
    moved, outs = refs[:-2], refs[-2:]
    rows = near_ref.shape[1]
    for i, (mine, out) in enumerate(zip((near_ref, behind_ref), outs)):
        if i >= len(moved):
            out[...] = mine[...]
            continue
        came = moved[i]
        size = came.shape[1]
        at = slice(0, size) if i == 0 else slice(rows - size, rows)
        total = (mine[:, at].astype(F32) + came[...].astype(F32)).astype(BF)
        if size == rows:
            out[...] = total
        else:
            rest = slice(size, rows) if i == 0 else slice(0, rows - size)
            out[:, at] = total
            out[:, rest] = mine[:, rest]


def add_pair(near, behind, *moved):
    def spec(array):
        return pl.BlockSpec((1,) + array.shape[1:], lambda i: (i, 0, 0))

    arrays = (near, behind, *moved)
    out = jax.ShapeDtypeStruct(near.shape, BF)
    return pl.pallas_call(
        add_pair_kernel,
        grid=(near.shape[0],),
        in_specs=[spec(array) for array in arrays],
        out_specs=[spec(near)] * 2,
        out_shape=[out] * 2,
        compiler_params=params("arbitrary"),
        name="add_pair",
    )(*arrays)


def pinned(call):
    def run(*args):
        return call(
            *[
                pltpu.with_memory_space_constraint(a, pltpu.HBM)
                if a.ndim > 1 and a.dtype != jnp.int32
                else a
                for a in args
            ]
        )

    return run


def lock(*values):
    return lax.optimization_barrier(values)


def per_device(
    tokens,
    prefix,
    routes,
    w_query,
    w_key,
    w_value,
    w_out,
    w_router,
    gain_attn,
    gain_ffn,
    w_gate,
    w_up,
    w_down,
    cotangent,
):
    wide, ctx = lax.axis_size("fsdp"), lax.axis_size("ctx")
    seqs, span, feature = tokens.shape
    rows = seqs * span
    width = 2 * feature
    shard = w_query.shape[0]
    experts = w_router.shape[1]
    per_core = experts // 2
    hid = w_gate.shape[2]
    q_width, kv_width = w_query.shape[1], w_key.shape[1]
    pairs = kv_width // LANES
    deep = ctx // 2
    quarter = per_core // 4
    plan = ((quarter, quarter), (quarter,), (per_core - 3 * quarter,))
    tp, c = lax.axis_index("tp"), lax.axis_index("ctx")
    core, y = c % 2, c // 2
    ring = Ring(wide, ctx)
    n = ring.size
    core_perm = [(i, i ^ 1) for i in range(ctx)]

    def swap_core(array, name="rows"):
        with jax.named_scope(f"{name}_over_core"):
            return lax.ppermute(array, "ctx", core_perm)

    def swap_tp(array, name="rows"):
        with jax.named_scope(f"{name}_over_tp"):
            return lax.ppermute(array, "tp", [(0, 1), (1, 0)])

    up_y = [(i, (i + 2) % ctx) for i in range(ctx)]
    down_y = [(i, (i - 2) % ctx) for i in range(ctx)]

    def shift_y(array, perm, name):
        with jax.named_scope(f"{name}_over_y"):
            return lax.ppermute(array, "ctx", perm)

    tp_scalar = tp.astype(jnp.int32).reshape(1)

    def by_core(mine, other, axis):
        return jnp.where(
            core == 0,
            jnp.concatenate([mine, other], axis),
            jnp.concatenate([other, mine], axis),
        )

    vmem = pl.BlockSpec(memory_space=pltpu.VMEM)
    smem = pl.BlockSpec(memory_space=pltpu.SMEM)
    any_spec = pl.BlockSpec(memory_space=pl.ANY)
    qkv_width = q_width + 2 * kv_width
    in_hbm = lambda array: pltpu.with_memory_space_constraint(array, pltpu.HBM)
    small_rows = max(shard, LANES)
    bundle = pl.pallas_call(
        pack_kernel,
        in_specs=[any_spec] * 4 + [vmem] * 3,
        out_specs=vmem,
        out_shape=jax.ShapeDtypeStruct((1, shard, qkv_width + q_width + LANES), BF),
        scratch_shapes=[pltpu.VMEM((LANES, small_rows), F32), pltpu.SemaphoreType.DMA(())],
        compiler_params=params(),
        name="pack",
    )(
        *[in_hbm(w) for w in (w_query, w_key, w_value, w_out.T)],
        w_router.T,
        gain_attn[None],
        gain_ffn[None],
    )
    own_tokens = tokens.reshape(rows, feature)
    own_cot = cotangent.reshape(rows, feature)
    core_scalar = core.astype(jnp.int32).reshape(1)
    def segment(ticks, *values):
        chains = [chain for chain in ticks if not chain.done()]

        values = together(chains, *values)
        if any(chain.step for chain in chains):
            for chain in chains:
                chain.prepare()
            values = together(chains, *values)
        for chain in chains:
            chain.send()
        return values

    def together(chains, *values):
        held = [array for chain in chains for array in chain.moving]
        out = lock(*held, *values)
        at = 0
        for chain in chains:
            size = len(chain.moving)
            chain.moving = tuple(out[at : at + size])
            at += size
        return out[at:]

    def arrive(chain, *values):
        return together([chain], *values)

    first = Gather(ring, bundle, "bundle")
    half_shape = jax.ShapeDtypeStruct((per_core, shard, 3 * hid), BF)
    *raw_w, own_tokens, bundle = segment(
        [first], w_gate, w_up, w_down.transpose(0, 2, 1), own_tokens, bundle
    )
    mine_w, other_w = pl.pallas_call(
        pack_experts_kernel,
        in_specs=[smem] + [any_spec] * 3,
        out_specs=[vmem] * 2,
        out_shape=[half_shape] * 2,
        scratch_shapes=[pltpu.SemaphoreType.DMA(())],
        compiler_params=params(),
        name="pack_experts",
    )(core_scalar, *[in_hbm(w) for w in raw_w])
    from_core = [swap_core(bundle, "bundle")]
    other_w = swap_core(other_w, "experts")
    from_core[0], other_w, mine_w = segment([first], from_core[0], other_w, mine_w)
    blocks_w = list(
        pl.pallas_call(
            join_kernel,
            in_specs=[smem] + [vmem] * 2,
            out_specs=[vmem] * len(plan),
            out_shape=[
                jax.ShapeDtypeStruct((sum(sizes), 2 * shard, 3 * hid), BF) for sizes in plan
            ],
            compiler_params=params(),
            name="join",
        )(core_scalar, mine_w, other_w)
    )
    half_width = HD // 2
    freqs = 10000.0 ** (-jnp.arange(half_width, dtype=F32) / half_width)
    local_pos = c * span + jnp.arange(span, dtype=jnp.int32)
    angles = local_pos.astype(F32)[:, None] * freqs[None, :]
    cosine, sine = jnp.cos(angles), jnp.sin(angles)
    cosine = jnp.tile(jnp.concatenate([cosine] * 4, axis=1), (seqs, 1))
    sine = jnp.tile(jnp.concatenate([-sine, sine, -sine, sine], axis=1), (seqs, 1))
    chips = [ring.chip(d) for d, _, _ in ring.places(shard)]
    chip_list = jnp.stack(chips).astype(jnp.int32)
    bundle_places = ring.places(shard)
    bundle_rows = [
        (chips[j] * 2 + side) * shard + row
        for side in (core, 1 - core)
        for j, (_, row, _) in enumerate(bundle_places)
    ]
    bundle_where = jnp.stack(bundle_rows).astype(jnp.int32)
    places = ring.places(2 * shard)
    part_rows = [ring.chip(d) * 2 * shard + row for d, row, _ in places]
    part_where = jnp.stack([core * per_core] + part_rows).astype(jnp.int32)
    base = jnp.stack(
        [(((y - k) % deep) * 2 + core) * span for k in range(deep)]
        + [(((y - k) % deep) * 2 + 1 - core) * span for k in range(deep)]
    ).astype(jnp.int32)
    other_tokens = swap_tp(own_tokens, "tokens")
    shared = 1
    while not first.done():
        fresh = [swap_core(part, "part") for part in first.parts[shared : first.step * 2 - 1]]
        shared += len(fresh)
        last_step = first.step == ring.size // 2 - 1
        *fresh, blocks_w[0], cosine, sine, chip_list, bundle_where, part_where, base, tokens_here = segment(
            [first],
            *fresh,
            blocks_w[0],
            cosine,
            sine,
            chip_list,
            bundle_where,
            part_where,
            base,
            other_tokens if last_step else own_tokens,
        )
        if last_step:
            other_tokens = tokens_here
        from_core += fresh
    weights = [Gather(ring, block, f"weights_{i}") for i, block in enumerate(blocks_w)]
    rest = [swap_core(part, "part") for part in first.parts[shared:-2]]
    other_cot = swap_tp(own_cot, "cotangent")
    *rest, other_cot, weights[0].moving = arrive(
        first, *rest, other_cot, weights[0].moving[0]
    )
    weights[0].moving = (weights[0].moving,) * 2
    weights[0].send()
    from_core += rest
    rest = [swap_core(part, "part") for part in first.parts[shared + len(rest) :]]
    from_core += rest
    w_qkv, wo_mine, w_small = pl.pallas_call(
        functools.partial(assemble_kernel, bundle_places * 2),
        in_specs=[smem] + [any_spec] * len(bundle_rows),
        out_specs=[vmem] * 3,
        out_shape=[
            jax.ShapeDtypeStruct((width, w), BF) for w in (qkv_width, q_width, LANES)
        ],
        scratch_shapes=[pltpu.SemaphoreType.DMA(())],
        compiler_params=params(),
        name="assemble",
    )(
        bundle_where,
        *[in_hbm(part) for part in first.parts + from_core],
    )
    step_rows = min(rows, 256)
    steps = rows // step_rows
    row_spec = lambda cols: pl.BlockSpec((step_rows, cols), lambda i, *_: (i, 0))
    full_tokens, normed, queries, kv = (pl.pallas_call(
        functools.partial(project_kernel, pairs, q_width, experts),
        grid=(steps,),
        in_specs=[
            smem,
            row_spec(feature),
            row_spec(feature),
            whole((width, LANES)),
            whole((width, qkv_width)),
            row_spec(LANES),
            row_spec(LANES),
        ],
        out_specs=[row_spec(width), row_spec(width), row_spec(q_width), row_spec(2 * kv_width)],
        out_shape=[
            pltpu.HBM((rows, width), BF),
            pltpu.HBM((rows, width), BF),
            jax.ShapeDtypeStruct((rows, q_width), BF),
            jax.ShapeDtypeStruct((rows, 2 * kv_width), BF),
        ],
        compiler_params=params("arbitrary"),
        name="project",
    ))(tp_scalar, own_tokens, other_tokens, w_small, w_qkv, cosine, sine)

    own_side = [kv]
    for _ in range(deep - 1):
        own_side.append(shift_y(own_side[-1], up_y, "kv"))
    other_side = [swap_core(kv, "kv")]
    wo_other = swap_tp(wo_mine, "w_out")
    length = ctx * span

    queries, *own_side = segment(weights[:1], queries, *own_side)
    other_side += [swap_core(block, "kv") for block in own_side[1:]]
    kv_blocks = own_side + other_side
    head_spec = lambda: pl.BlockSpec((span, 2 * LANES), lambda s, p, *_: (s, p))
    prob_spec = pl.BlockSpec((1, 2, 2 * span, length), lambda s, p, *_: (s, p, 0, 0))
    attended, probs = (pl.pallas_call(
        functools.partial(attend_kernel, ctx, span),
        grid_spec=pltpu.PrefetchScalarGridSpec(
            num_scalar_prefetch=2,
            grid=(seqs, pairs),
            in_specs=[head_spec()] * (1 + ctx),
            out_specs=[head_spec(), prob_spec],
        ),
        out_shape=[
            jax.ShapeDtypeStruct((rows, q_width), BF),
            pltpu.HBM((seqs, 2 * pairs, 2 * span, length), BF),
        ],
        compiler_params=params("arbitrary", "arbitrary"),
        name="attend",
    ))(prefix, base, queries, *kv_blocks)

    attended, wo_other = segment(weights[:1], attended, wo_other)
    for _ in range(ring.size // 2 - 4):
        (attended,) = segment(weights[:1], attended)

    attended_other = swap_tp(attended, "attended")
    full_cot = (pl.pallas_call(
            features_kernel,
            in_specs=[smem] + [vmem] * 2,
            out_specs=vmem,
            out_shape=pltpu.HBM((rows, width), BF),
            compiler_params=params(),
            name="features",
        )
    )(tp_scalar, own_cot, other_cot)
    peer_cot = swap_core(full_cot, "full_cot")
    (attended_other,) = segment(weights[:1], attended_other)
    route_rows = routes.reshape(rows, TOP)
    middle, normed_two, gates = (pinned(pl.pallas_call(
        functools.partial(middle_kernel, experts + 1),
        grid=(steps,),
        in_specs=[
            row_spec(q_width),
            row_spec(q_width),
            whole((width, q_width)),
            whole((width, q_width)),
            row_spec(width),
            whole((width, LANES)),
            row_spec(TOP),
        ],
        out_specs=[
            row_spec(width),
            row_spec(width + LANES),
            row_spec(LANES),
        ],
        out_shape=[
            pltpu.HBM((rows, width), F32),
            pltpu.HBM((rows, width + LANES), BF),
            pltpu.HBM((rows, LANES), F32),
        ],
        compiler_params=params("arbitrary"),
        name="middle",
    )))(attended, attended_other, wo_mine, wo_other, full_tokens, w_small, route_rows)
    normed_two, peer_cot = arrive(weights[0], normed_two, peer_cot)
    (normed_two,) = segment(weights[1:], normed_two)
    peer_two = swap_core(normed_two, "normed_two")

    near = [(normed_two, BF), (full_cot, BF), (peer_two, BF), (peer_cot, BF)]
    sources = [in_hbm(array) for array, _ in near]
    wide_acc, acc_shape = (rows, width), (rows, width + LANES)
    count = len(places)

    def run_experts(g, call, accs, dw_parts):
        lead = 1 + count + 4 + len(accs)
        first_call, last_call = not accs, g + 1 == len(plan)
        call_size, start = plan[g][call], sum(plan[g][:call])
        column = sum(sum(sizes) for sizes in plan[:g]) + start
        kept = sum(sum(sizes) for sizes in (plan[1:] if g else plan[:1]))
        sums_start = column - sum(plan[0]) if g else start
        outs = pl.pallas_call(
            functools.partial(
                moe_kernel,
                first_call,
                last_call,
                bool(dw_parts),
                experts,
                column,
                start,
                sums_start,
                call_size,
                places,
            ),
            in_specs=[smem] + [any_spec] * (lead - 1 + len(dw_parts)),
            out_specs=[any_spec] * (3 + count),
            out_shape=[
                pltpu.HBM(acc_shape, F32),
                pltpu.HBM(acc_shape, BF if last_call else F32),
                pltpu.HBM((call_size, 2 * rows, hid), BF),
            ]
            + [pltpu.HBM((kept, r, 3 * hid), BF) for _, _, r in places],
            input_output_aliases={lead + j: 3 + j for j in range(len(dw_parts))},
            scratch_shapes=[pltpu.VMEM(array.shape, kind) for array, kind in near]
            + [pltpu.VMEM(acc_shape, F32)] * 2
            + [
                pltpu.VMEM((call_size, 2 * rows, hid), BF),
                pltpu.VMEM(acc_shape, BF),
                pltpu.VMEM((call_size, width, 3 * hid), BF),
                pltpu.VMEM((2, width, 3 * hid), BF),
                pltpu.SemaphoreType.DMA((call_size,)),
                pltpu.SemaphoreType.DMA((2,)),
                pltpu.SemaphoreType.DMA((4,)),
                pltpu.SemaphoreType.DMA((2,)),
                pltpu.SemaphoreType.DMA((2,)),
                pltpu.SemaphoreType.DMA(()),
            ],
            compiler_params=pltpu.CompilerParams(vmem_limit_bytes=MOE_VMEM),
            name="experts",
        )(
            part_where,
            *[in_hbm(block) for block in weights[g].parts],
            *sources,
            *accs,
            *dw_parts,
        )
        return outs[:2], outs[2], outs[3:]

    accs, mixed_parts, sums = (), [], []

    later = weights[1:]
    for call in range(len(plan[0])):
        if call:
            accs = segment(later, *accs)
            lead_parts = dw_parts
        accs, mixed, dw_parts = run_experts(0, call, accs, lead_parts if call else ())
        mixed_parts.append(mixed)
    sums.append(Scatter(ring, dw_parts, "sums_0"))
    dw_parts = ()
    for g in range(1, len(plan)):
        while weights[g].step < ring.size // 2 - 1:
            accs = segment(later, *accs)
        if not weights[g].done():
            accs = segment([weights[g]], *accs)
        accs = arrive(weights[g], *accs)
        accs = segment([*weights[g + 1 :], sums[0]], *accs)
        accs, mixed, dw_parts = run_experts(g, 0, accs, dw_parts)
        mixed_parts.append(mixed)
    sums.append(Scatter(ring, dw_parts, "sums_1"))

    grad_two, grad_two_peer = arrive(sums[0], *accs)
    parts = pl.pallas_call(
        functools.partial(add_terms_kernel, experts),
        in_specs=[vmem] * 2,
        out_specs=[vmem] * seqs,
        out_shape=[jax.ShapeDtypeStruct((span, width + LANES), BF)] * seqs,
        compiler_params=params(),
        name="add_terms",
    )(grad_two, swap_core(grad_two_peer, "grad_two"))
    parts = list(together(sums, *parts))
    parts_other = [swap_tp(parts[0], "part")]
    sums[0].prepare()
    for chain in sums:
        chain.send()

    moe, moe_peer = pl.pallas_call(
        functools.partial(moe_sum_kernel, places, plan),
        in_specs=[smem] + [any_spec] * (count * len(plan) + len(mixed_parts)),
        out_specs=[vmem] * 2,
        out_shape=[pltpu.HBM(wide_acc, F32), pltpu.HBM(wide_acc, BF)],
        scratch_shapes=[pltpu.VMEM((width, sum(sizes) * hid), BF) for sizes in plan]
        + [pltpu.VMEM((2 * rows, sum(sizes) * hid), BF) for sizes in plan]
        + [pltpu.SemaphoreType.DMA((len(plan),))] * 2,
        compiler_params=pltpu.CompilerParams(vmem_limit_bytes=MOE_VMEM),
        name="experts_output",
    )(
        part_where,
        *[in_hbm(block) for chain in weights for block in chain.parts],
        *lock(*[in_hbm(mixed) for mixed in mixed_parts], parts[0])[: len(mixed_parts)],
    )

    def sequence_back(s, part_other, before):
        at = lambda cols: pl.BlockSpec((span, cols), lambda i, *_: (s, 0))
        whole_span = lambda cols: pl.BlockSpec((span, cols), lambda i, *_: (0, 0))
        grad_middle, grad_branch, grad_attended, grad_logits, gain_term = pl.pallas_call(
            functools.partial(middle_back_kernel, experts + 1),
            grid=(1,),
            in_specs=[
                smem,
                whole_span(width + LANES),
                whole_span(width + LANES),
                at(LANES),
                at(width),
                at(width),
                whole((width, LANES)),
                whole((width, q_width)),
            ],
            out_specs=[
                whole_span(feature),
                whole_span(width),
                whole_span(q_width),
                whole_span(LANES),
                whole((1, width)),
            ],
            out_shape=[
                pltpu.HBM((span, feature), F32),
                pltpu.HBM((span, width), BF),
                jax.ShapeDtypeStruct((span, q_width), BF),
                pltpu.HBM((span, LANES), BF),
                pltpu.HBM((1, width), F32),
            ],
            compiler_params=params("arbitrary"),
            name="middle_back",
        )(tp_scalar, parts[s], part_other, gates, middle, full_cot, w_small, wo_mine)
        head = lambda row: pl.BlockSpec((span, 2 * LANES), lambda p: (row, p))
        turn = pl.BlockSpec((span, LANES), lambda p: (s, 0))
        back = pl.BlockSpec((deep, span, 2 * LANES), lambda p: (0, s, p))
        grads = pl.pallas_call(
            functools.partial(attend_back_kernel, ctx, span),
            grid=(pairs,),
            in_specs=[
                pl.BlockSpec((1, 2, 2 * span, length), lambda p: (s, p, 0, 0)),
                head(s),
                head(0),
                turn,
                turn,
            ]
            + [head(s)] * ctx
            + [any_spec] * len(before),
            out_specs=[head(s), back, back],
            out_shape=[
                pltpu.HBM((rows, q_width), BF),
                pltpu.HBM((deep, rows, 2 * kv_width), BF),
                pltpu.HBM((deep, rows, 2 * kv_width), BF),
            ],
            input_output_aliases={5 + ctx + j: j for j in range(len(before))},
            compiler_params=params("arbitrary"),
            name="attend_back",
        )(in_hbm(probs), queries, grad_attended, cosine, sine, *kv_blocks, *before)
        return (grad_middle, grad_branch, grad_logits, gain_term), grads

    parts_other[0], moe, moe_peer = lock(parts_other[0], moe, moe_peer)
    saved, found = [], ()
    for s in range(seqs):
        if s + 1 < seqs:
            parts[s + 1] = lock(parts[s + 1], parts_other[s])[0]
            parts_other.append(swap_tp(parts[s + 1], "part"))
        kept, found = sequence_back(s, parts_other[s], found)
        if s == 0:
            found = segment(sums[:1], *found)
            parts_other[-1], *found = arrive(sums[1], parts_other[-1], *found)
            sums[1].prepare()
            (parts_other[-1],) = together(sums[1:], parts_other[-1])
            from_core_moe = swap_core(lock(moe_peer, parts_other[-1])[0], "moe")
        saved.append(kept)
    half_at = lambda array, side: lax.dynamic_slice_in_dim(array, side * feature, feature, 1)
    moe_sum = moe + from_core_moe.astype(F32)
    moe_send = half_at(moe_sum, 1 - tp).astype(BF)
    grad_q, grad_kv_own, grad_kv_peer, moe_send = arrive(sums[0], *found, moe_send)

    def to_owner(grad_kv_own, from_peer):
        travel = jnp.zeros(from_peer.shape[1:], BF)
        for k in range(deep - 1, 0, -1):
            piece = grad_kv_own[k] + from_peer[k]
            if k < deep - 1:
                piece = piece + travel
            travel = shift_y(piece, down_y, "grad_kv")
        return travel

    def weight_grads(name, sides, gain_terms, gain_at, cols):
        flat = [array for side in sides for array in side]
        return (pl.pallas_call(
                functools.partial(weight_grad_kernel, [len(side) for side in sides], gain_at),
                in_specs=[smem] + [vmem] * (len(flat) + len(gain_terms)),
                out_specs=[vmem] * 2,
                out_shape=[jax.ShapeDtypeStruct((n, shard, cols), BF)] * 2,
                compiler_params=params(),
                name=f"{name}_weight_grads",
            )
        )(core_scalar, *flat, *gain_terms)

    def close_experts(chain):
        own = chain.parts[0]
        shape = (own.shape[0], shard, 3 * hid)
        kept, sent = pl.pallas_call(
            close_experts_kernel,
            in_specs=[smem] + [vmem] * 3,
            out_specs=[vmem] * 2,
            out_shape=[jax.ShapeDtypeStruct(shape, F32), jax.ShapeDtypeStruct(shape, BF)],
            compiler_params=params(),
            name="close_experts",
        )(core_scalar, own, *chain.moving)
        return kept, sent

    (grad_kv_peer,) = together(sums[1:], grad_kv_peer)
    sums[1].send()
    from_peer = swap_core(grad_kv_peer, "grad_kv")
    early = weight_grads(
        "early",
        [
            [kept[1] for kept in saved],
            [attended],
            [normed],
            [grad_q],
            [normed_two],
            [kept[2] for kept in saved],
        ],
        [kept[3] for kept in saved],
        experts,
        2 * q_width + LANES,
    )
    travel = to_owner(grad_kv_own, from_peer)
    segment(sums[1:])
    early_other = swap_core(early[1], "early")
    closed = [close_experts(sums[0])]
    moe_other = swap_tp(moe_send, "moe_send")
    travel, moe_other, *closed[0] = lock(travel, moe_other, *closed[0])
    shapes = [
        ((rows, 2 * kv_width), BF),
        ((rows, feature), F32),
        ((rows, feature + LANES), BF),
        ((rows, LANES), F32),
        ((1, width), F32),
    ]
    grad_kv, grad_own, grad_send, inner, gain_one_term = pl.pallas_call(
        functools.partial(project_back_kernel, pairs, experts, seqs),
        in_specs=[smem] + [vmem] * 9,
        out_specs=[vmem] * 5,
        out_shape=[jax.ShapeDtypeStruct(shape, kind) for shape, kind in shapes],
        compiler_params=params(),
        name="project_back",
    )(
        tp_scalar,
        grad_q,
        grad_kv_own,
        from_peer,
        travel,
        cosine,
        sine,
        w_qkv,
        full_tokens,
        w_small,
    )
    late = weight_grads(
        "late", [[normed], [grad_kv]], [gain_one_term], 0, 2 * kv_width + LANES
    )
    late_other = swap_core(late[1], "late")
    late_other, early_other = lock(late_other, early_other)
    cols = early_other.shape[2] + late_other.shape[2]
    last = Scatter(
        ring,
        pinned(pl.pallas_call(
            functools.partial(order_kernel, bundle_places),
            in_specs=[smem] + [vmem] * 4,
            out_specs=[vmem] * len(bundle_places),
            out_shape=[jax.ShapeDtypeStruct((1, r, cols), BF) for _, _, r in bundle_places],
            compiler_params=params(),
            name="order",
        ))(chip_list, early[0], early_other, late[0], late_other),
        "last",
    )
    (grad_send,) = together([last], grad_send)
    last.send()
    arrive(sums[1])
    sums[1].prepare()
    together([last, sums[1]])
    sums[1].send()
    grad_other = swap_tp(grad_send, "grad_normed")
    segment([last])
    grad_tokens = pinned(
        pl.pallas_call(
            token_grads_kernel,
            in_specs=[vmem] * (4 + seqs),
            out_specs=vmem,
            out_shape=pltpu.HBM((rows, feature), F32),
            compiler_params=params(),
            name="token_grads",
        )
    )(own_tokens, grad_own, inner, grad_other, *[kept[0] for kept in saved])
    output = (half_at(middle, tp) + half_at(moe_sum, tp) + moe_other.astype(F32)).astype(BF)
    grad_tokens, output = segment([last], grad_tokens, output)
    while not sums[1].done():
        segment(sums[1:])
    together([last, sums[1]])
    closed.append(close_experts(sums[1]))
    closed = [[kept, swap_core(sent, "expert_grads")] for kept, sent in closed]
    own_slab = swap_tp(last.parts[0][:, :, -LANES:], "gain")
    while last.step + 1 < last.far:
        segment([last])
    (own_slab,) = together([last], own_slab)
    last.prepare()
    together([last])
    slabs = [array[:, :, -LANES:] for array in last.moving]
    last.send()
    across = [
        lax.ppermute(
            slab,
            RING + ("tp",),
            [(2 * p + t, 2 * q + 1 - t) for p, q in perm for t in range(2)],
        )
        for slab, perm in zip(slabs, (ring.forward, ring.backward))
    ]
    across.append(own_slab)
    grad_gate, grad_up, down_term = (pl.pallas_call(
            functools.partial(expert_grads_kernel, len(sums)),
            in_specs=[smem] + [vmem] * (2 * len(sums)),
            out_specs=[vmem] * 3,
            out_shape=[pltpu.HBM((experts, shard, hid), F32)] * 3,
            compiler_params=params(),
            name="expert_grads",
        )
    )(
        core_scalar,
        *[closed[k][0] for k in range(len(sums))],
        *[closed[k][1] for k in range(len(sums))],
    )
    grad_gate, grad_up, down_term = arrive(last, grad_gate, grad_up, down_term)
    widths = (("one", q_width), ("one", q_width), ("one", LANES), ("pairs", 2 * kv_width), ("one", LANES))
    out_term, grad_query, small_term, grad_key, grad_value, gain_term = (pinned(pl.pallas_call(
            functools.partial(close_weights_kernel, widths),
            in_specs=[vmem] * 6,
            out_specs=[vmem] * 6,
            out_shape=[
                jax.ShapeDtypeStruct((shard, w), F32)
                for w in (q_width, q_width, LANES, kv_width, kv_width, LANES)
            ],
            compiler_params=params(),
            name="close_weights",
        ))
    )(last.parts[0], *last.moving, *across)
    grad_out = out_term.T
    grad_router = small_term[:, :experts]
    grad_gain_ffn = small_term[:, experts]
    grad_gain_attn = gain_term[:, 0]

    grad_down = down_term.transpose(0, 2, 1)

    return (
        output.reshape(seqs, span, feature),
        grad_tokens.reshape(seqs, span, feature),
        grad_query,
        grad_key,
        grad_value,
        grad_out,
        grad_router,
        grad_gain_attn,
        grad_gain_ffn,
        grad_gate,
        grad_up,
        grad_down,
    )


def solution(mesh):
    in_specs = (
        P("fsdp", "ctx", "tp"),
        P("fsdp"),
        P("ctx", "fsdp", None, None),
        P(("fsdp", "ctx"), "tp"),
        P(("fsdp", "ctx"), "tp"),
        P(("fsdp", "ctx"), "tp"),
        P("tp", ("fsdp", "ctx")),
        P(("fsdp", "ctx"), None),
        P(("fsdp", "ctx")),
        P(("fsdp", "ctx")),
        P(None, ("fsdp", "ctx"), "tp"),
        P(None, ("fsdp", "ctx"), "tp"),
        P(None, "tp", ("fsdp", "ctx")),
        P("fsdp", "ctx", "tp"),
    )
    out_specs = (
        P("fsdp", "ctx", "tp"),
        P("fsdp", "ctx", "tp"),
        P(("fsdp", "ctx"), "tp"),
        P(("fsdp", "ctx"), "tp"),
        P(("fsdp", "ctx"), "tp"),
        P("tp", ("fsdp", "ctx")),
        P(("fsdp", "ctx"), None),
        P(("fsdp", "ctx")),
        P(("fsdp", "ctx")),
        P(None, ("fsdp", "ctx"), "tp"),
        P(None, ("fsdp", "ctx"), "tp"),
        P(None, "tp", ("fsdp", "ctx")),
    )
    return jax.shard_map(
        per_device, mesh=mesh, in_specs=in_specs, out_specs=out_specs, check_vma=False
    )
```
